256 devices in a mesh: inner: 16 (over z, core), outer: 16 (over y, x).
Axes of the slice: x: 4, y: 4, z: 8, core: 2. Of those that a mesh axis runs over, the one named last changes fastest.
Arguments:
- acts: bfloat16 [65536, 14848], P(('inner', 'outer')), may hold values from -6 to 6
- key_grad: bfloat16 [65536, 512], P(('inner', 'outer')), may hold values from -0.0234375 to 0.0234375
- shifts: int32 [256, 8], P(('inner', 'outer')), may hold values from 5 to 12, as said below
Outputs:
- weight_grad: float32 [14848, 512], P(('inner', 'outer'))
The draws below stay inside these ranges and needn't reach their ends.
Inputs may be any that keep to these rules, and one draw needn't show every extreme that they name: `shifts`: column k is the exponent that device uses at hop k; columns from log2(256) on are not used.
All inputs are finite; a program needn't handle non-finite values.
Results may differ from the reference program's by a relative error of at most 0.0053.
Values may be sent and summed in bfloat16 or wider, within the bound.
A program may use at most 128 MiB of HBM per device.

```python
import jax
import jax.numpy as jnp
from jax import lax

D = 14848
KEYS = 512
TOK_DEV = 256
TOKENS = 65536
HOP_SLOTS = 8
DEVICES = 256


def draw_shifts(key, part):
    key = jax.random.fold_in(key, 11)
    levels = DEVICES.bit_length() - 1
    hop_index = jnp.arange(HOP_SLOTS, dtype=jnp.int32)
    base_shift = 7 - (hop_index - levels) // 2
    jitter = jax.random.randint(key, (DEVICES, HOP_SLOTS), -1, 2, dtype=jnp.int32)
    table = jnp.clip(base_shift[None, :] + jitter, 5, 12).astype(jnp.int32)
    table = table.at[0, levels - 1].set(5)
    table = table.at[DEVICES - 1, 0].set(12)
    return table.astype(jnp.int32)


def steps_of(stream_key, dims, pieces, low, high):
    def one(dim, blocks):
        steps = jax.random.uniform(jax.random.fold_in(jax.random.fold_in(stream_key, 6), dim), (blocks,), jnp.float32, low / len(pieces), high / len(pieces))
        return jnp.repeat(jnp.exp(steps), dims[dim] // blocks).reshape((-1,) + (1,) * (len(dims) - dim - 1))

    factor_of = one(*pieces[0])
    for cut in pieces[1:]:
        factor_of = factor_of * one(*cut)
    return factor_of


def gaussian(own_key, extent, spread, most, shards=(), kind=jnp.bfloat16):
    array = spread * jax.random.normal(own_key, extent, jnp.float32)
    if shards:
        array = array * steps_of(own_key, extent, shards, -0.22, 0.18)
    return jnp.clip(array, -most, most).astype(kind)


def setup_inputs(seed: int = 0) -> dict:
    splits = jax.random.split(jax.random.key(seed), 4)
    acts = gaussian(splits[0], (TOKENS, D), 1.0, 6.0, ((0, 256),))
    key_grad = gaussian(splits[1], (TOKENS, KEYS), TOKENS ** -0.5, 0.0234375, ((0, 256),))
    shifts = draw_shifts(jax.random.fold_in(splits[3], 71), 0)
    return dict(acts=acts, key_grad=key_grad, shifts=shifts)


clip_bound = 448.0


def power_of_two(shift):
    return jnp.left_shift(jnp.int32(1), shift.astype(jnp.int32)).astype(jnp.float32)


def reference(acts, key_grad, shifts):
    levels = DEVICES.bit_length() - 1
    block_rows = D // DEVICES
    acts_all = acts.reshape(DEVICES, TOK_DEV, D)
    grads_all = key_grad.reshape(DEVICES, TOK_DEV, KEYS).astype(jnp.float32)
    device_ids = jnp.arange(DEVICES, dtype=jnp.int32)

    def one_block(block_id):
        columns = lax.dynamic_slice_in_dim(acts_all, (block_id * block_rows).astype(jnp.int32), block_rows, 2)
        values = jnp.einsum("dtr,dtk->drk", columns.astype(jnp.float32), grads_all)
        for hop_index in range(levels):
            bit_pos = levels - 1 - hop_index
            partner = jnp.bitwise_xor(device_ids, jnp.int32(1 << bit_pos))
            factor = power_of_two(shifts[partner, hop_index])[:, None, None]
            packed = jnp.clip(values[partner] * factor, -clip_bound, clip_bound).astype(jnp.bfloat16)
            packed = lax.optimization_barrier(packed)
            values = values + packed.astype(jnp.float32) / factor
        return values[block_id]

    blocks = lax.map(one_block, device_ids)
    return blocks.reshape(D, KEYS)
```

```python
import functools

import jax
import jax.numpy as jnp
from jax import lax
from jax.experimental import pallas as pl
from jax.experimental.pallas import tpu as pltpu
from jax.sharding import PartitionSpec as P

MESH = pl.DeviceIdType.MESH
BOUND_ROWS = 16


def xor(a, b, bits):
    total = 0
    for bit in range(bits):
        step = 1 << bit
        total = total + step * lax.rem(lax.div(a, step) + lax.div(b, step), 2)
    return total


def clipped(values, bound):
    return jnp.clip(values, -bound, bound).astype(jnp.bfloat16).astype(jnp.float32)


def aligned(index):
    return pl.multiple_of(index, 16)


def round_up(value, unit):
    return -(-value // unit) * unit


def kernel(
    ni,
    no,
    parts,
    span,
    acts_hbm,
    grad_hbm,
    shifts_smem,
    out_ref,
    raw,
    acts_t,
    recv,
    relay,
    grads,
    sums,
    total,
    place,
    place_last,
    out_box,
    in_box,
    limit_box,
    limits_in,
    fetch_sem,
    grad_sem,
    ring_send,
    ring_recv,
    twin_send,
    twin_recv,
    block_send,
    block_recv,
    hop1_send,
    hop1_recv,
    hop2_send,
    hop2_recv,
    local_sem,
    out_send,
    out_recv,
    limit_send,
    limit_recv,
):
    tokens, width = raw.shape
    keys = grads.shape[2]
    block = width // ni
    rows = block // no
    nz = ni // 2
    half = nz // 2
    first = half // 2
    ibits = ni.bit_length() - 1
    obits = no.bit_length() - 1
    quarters = 4
    strip = width // quarters
    count = len(parts)

    i_at = lax.axis_index("inner")
    o_at = lax.axis_index("outer")
    z_at = lax.div(i_at, 2)
    core = lax.rem(i_at, 2)

    def z_off(step):
        return lax.rem(z_at + step + nz, nz)

    def at_inner(z, k):
        return (2 * z + k, o_at)

    def fetch(q):
        cols = pl.ds(q * strip, strip)
        return pltpu.make_async_copy(acts_hbm.at[:, cols], raw.at[:, cols], fetch_sem.at[q])

    grad_copy = pltpu.make_async_copy(grad_hbm, grads.at[i_at, pl.ds(0, tokens)], grad_sem)
    grad_copy.start()
    for q in range(quarters):
        fetch(q).start()

    barrier = pltpu.get_barrier_semaphore()
    for step in range(1, ni):
        pl.semaphore_signal(
            barrier, inc=1, device_id=(lax.rem(i_at + step, ni), o_at), device_id_type=MESH
        )
    for step in range(1, no):
        pl.semaphore_signal(
            barrier, inc=1, device_id=(i_at, lax.rem(o_at + step, no)), device_id_type=MESH
        )

    row_at = lax.broadcasted_iota(jnp.int32, (BOUND_ROWS, keys), 0)
    left_shift = jnp.zeros((BOUND_ROWS, keys), jnp.int32)
    for hop in range(ibits + obits):
        left_shift = jnp.where(row_at == hop, 12 - shifts_smem[0, hop], left_shift)
    own_limits = jnp.left_shift(jnp.ones_like(left_shift), left_shift).astype(jnp.float32) * 0.109375
    own_limits = own_limits.astype(jnp.bfloat16)
    limit_box[...] = own_limits

    def fill_place(ref, piece):
        size = ref.shape[0]
        row = lax.broadcasted_iota(jnp.int32, (size, 128), 0)
        lane = lax.broadcasted_iota(jnp.int32, (size, 128), 1)
        owner = lax.div(row, piece)
        offset = lane - (owner * rows + row - owner * piece)
        for n in range(span // 128):
            ref[:, pl.ds(n * 128, 128)] = offset + n * 128

    fill_place(place, parts[0][3])
    if place_last is not None:
        fill_place(place_last, parts[-1][3])

    grad_copy.wait()
    grads[i_at, pl.ds(tokens, BOUND_ROWS), :] = own_limits

    pl.semaphore_wait(barrier, ni + no - 2)

    grad_rows = grads.shape[1]
    cut = round_up(grad_rows // 2, 16)

    def ring(way, step):
        sign = 1 if way == 0 else -1
        source = 2 * z_off(sign * (1 - step)) + core
        if step < half:
            piece_at = pl.ds(0, grad_rows)
        else:
            piece_at = pl.ds(0, cut) if way == 0 else pl.ds(cut, grad_rows - cut)
        piece = grads.at[source, piece_at]
        return pltpu.make_async_remote_copy(
            src_ref=piece,
            dst_ref=piece,
            send_sem=ring_send.at[way, step - 1],
            recv_sem=ring_recv.at[way, step - 1],
            device_id=at_inner(z_off(sign), core),
            device_id_type=MESH,
        )

    def twin(offset, side):
        source = 2 * z_off(offset) + side
        return pltpu.make_async_remote_copy(
            src_ref=grads.at[source],
            dst_ref=grads.at[source],
            send_sem=twin_send.at[offset % nz],
            recv_sem=twin_recv.at[offset % nz],
            device_id=at_inner(z_at, 1 - core),
            device_id_type=MESH,
        )

    def ring_arrived(step):
        ring(0, step).wait_recv()
        ring(1, step).wait_recv()
        if step < half:
            ring(0, step + 1).start()
            ring(1, step + 1).start()
            twin(-step, core).start()
            twin(step, core).start()
        else:
            twin(half, core).start()

    def limit_copy(target):
        return pltpu.make_async_remote_copy(
            src_ref=limit_box,
            dst_ref=limits_in.at[o_at],
            send_sem=limit_send.at[target],
            recv_sem=limit_recv.at[o_at],
            device_id=(i_at, target),
            device_id_type=MESH,
        )

    def limit_arrival(source):
        return pltpu.make_async_remote_copy(
            src_ref=limit_box,
            dst_ref=limits_in.at[source],
            send_sem=limit_send.at[source],
            recv_sem=limit_recv.at[source],
            device_id=(i_at, source),
            device_id_type=MESH,
        )

    def turn(part, target):
        start, size, at, piece = parts[part]
        column = target * block
        tile = lax.div(column, 128)
        source = place if piece == parts[0][3] else place_last
        pick = (source[...] == column - tile * 128 + at).astype(jnp.bfloat16)
        window = raw[:, pl.ds(pl.multiple_of(tile * 128, 128), span)]
        acts_t[pl.ds(aligned(column + start), size), :] = lax.dot_general(
            pick, window, (((1,), (1,)), ((), ())), preferred_element_type=jnp.float32
        ).astype(jnp.bfloat16)

    def block_copy(part, target):
        start, size = parts[part][:2]
        slot = xor(i_at, target, ibits)
        return pltpu.make_async_remote_copy(
            src_ref=acts_t.at[pl.ds(aligned(target * block + start), size)],
            dst_ref=recv.at[slot, pl.ds(start, size)],
            send_sem=block_send.at[part, slot],
            recv_sem=block_recv.at[part, slot],
            device_id=(target, o_at),
            device_id_type=MESH,
        )

    def halves(part):
        start, size = parts[part][:2]
        low = round_up(size // 2, 16)
        return ((start, low), (start + low, size - low))

    def hop1(part, way, k):
        start, size = halves(part)[way]
        sign = 1 if way == 0 else -1
        target = 2 * z_off(half) + k
        return pltpu.make_async_remote_copy(
            src_ref=acts_t.at[pl.ds(aligned(target * block + start), size)],
            dst_ref=relay.at[k, pl.ds(start, size)],
            send_sem=hop1_send.at[part, way, k],
            recv_sem=hop1_recv.at[part, way, k],
            device_id=at_inner(z_off(sign * first), core),
            device_id_type=MESH,
        )

    def hop2(part, way, k):
        start, size = halves(part)[way]
        sign = 1 if way == 0 else -1
        differ = lax.rem(core + k, 2)
        return pltpu.make_async_remote_copy(
            src_ref=relay.at[k, pl.ds(start, size)],
            dst_ref=recv.at[2 * half + differ, pl.ds(start, size)],
            send_sem=hop2_send.at[part, way, differ],
            recv_sem=hop2_recv.at[part, way, differ],
            device_id=at_inner(z_off(sign * (half - first)), k),
            device_id_type=MESH,
        )

    def hop2_arrival(part, way, differ):
        start, size = halves(part)[way]
        piece = recv.at[2 * half + differ, pl.ds(start, size)]
        return pltpu.make_async_remote_copy(
            src_ref=piece,
            dst_ref=piece,
            send_sem=hop2_send.at[part, way, differ],
            recv_sem=hop2_recv.at[part, way, differ],
            device_id=at_inner(z_off(half), core),
            device_id_type=MESH,
        )

    def block_arrival(part, slot):
        start, size = parts[part][:2]
        piece = recv.at[slot, pl.ds(start, size)]
        return pltpu.make_async_remote_copy(
            src_ref=piece,
            dst_ref=piece,
            send_sem=block_send.at[part, slot],
            recv_sem=block_recv.at[part, slot],
            device_id=at_inner(z_at, 1 - core),
            device_id_type=MESH,
        )

    def local_copy(part):
        start, size = parts[part][:2]
        return pltpu.make_async_copy(
            acts_t.at[pl.ds(aligned(i_at * block + start), size)],
            recv.at[0, pl.ds(start, size)],
            local_sem.at[part],
        )

    def send_steps(part, low, high):
        def one(step, carry):
            odd = lax.rem(step, 2)
            offset = (2 * odd - 1) * (half - lax.div(step + odd, 2))
            z = z_off(offset)
            for k in range(2):
                turn(part, 2 * z + k)

            @pl.when(step == 0)
            def _():
                for way in range(2):
                    for k in range(2):
                        hop1(part, way, k).start()

            @pl.when(jnp.logical_and(step > 0, step < nz - 1))
            def _():
                for k in range(2):
                    block_copy(part, 2 * z + k).start()

            @pl.when(step == nz - 1)
            def _():
                block_copy(part, 2 * z_at + 1 - core).start()
                local_copy(part).start()

            return carry

        lax.fori_loop(low, high, one, 0)

    def forward(part):
        for way in range(2):
            for k in range(2):
                hop1(part, way, k).wait_recv()
                hop2(part, way, k).start()

    ring(0, 1).start()
    ring(1, 1).start()
    twin(0, core).start()
    for step in range(1, no):
        limit_copy(lax.rem(o_at + step, no)).start()
    for q in range(quarters):
        fetch(q).wait()
    done = 0
    for step in range(1, half):
        upto = 2 * step + 1 if step < half - 1 else nz
        send_steps(0, done, upto)
        ring_arrived(step)
        done = upto
    if half == 1:
        send_steps(0, 0, nz)
    send_steps(1, 0, 3)
    ring_arrived(half)
    send_steps(1, 3, nz)
    forward(0)

    def leaf(slot, start, size):
        source = xor(i_at, slot, ibits)
        value = jnp.dot(
            recv[slot, pl.ds(start, size), :],
            grads[source, pl.ds(0, tokens), :],
            preferred_element_type=jnp.float32,
        )
        limit = grads[source, pl.ds(tokens, BOUND_ROWS), :].astype(jnp.float32)
        return value, limit

    def out_copy(part, target):
        piece_at = pl.ds(parts[part][2], 16)
        return pltpu.make_async_remote_copy(
            src_ref=out_box.at[target, piece_at],
            dst_ref=in_box.at[o_at, piece_at],
            send_sem=out_send.at[part, target],
            recv_sem=out_recv.at[part, o_at],
            device_id=(i_at, target),
            device_id_type=MESH,
        )

    def out_arrival(part, source):
        piece_at = pl.ds(parts[part][2], 16)
        return pltpu.make_async_remote_copy(
            src_ref=in_box.at[source, piece_at],
            dst_ref=in_box.at[source, piece_at],
            send_sem=out_send.at[part, source],
            recv_sem=out_recv.at[part, source],
            device_id=(i_at, source),
            device_id_type=MESH,
        )

    quarter = ni // 4

    def work(part):
        start, size, at, piece = parts[part]

        def group(n, carry):
            kept, _ = leaf(n, start, size)
            given, limit = leaf(n + 2 * quarter, start, size)
            first_sum = kept + clipped(given, limit[0:1])
            kept, limit_1 = leaf(n + quarter, start, size)
            given, limit = leaf(n + 3 * quarter, start, size)
            second_sum = kept + clipped(given, limit[0:1])
            sums[n, pl.ds(0, size), :] = first_sum + clipped(second_sum, limit_1[1:2])
            return carry

        lax.fori_loop(0, quarter, group, 0)
        level = 2
        width_now = quarter
        while width_now > 1:
            width_now //= 2
            for n in range(width_now):
                source = xor(i_at, n + width_now, ibits)
                limit = grads[source, pl.ds(tokens, BOUND_ROWS), :].astype(jnp.float32)
                value = sums[n, pl.ds(0, size), :] + clipped(
                    sums[n + width_now, pl.ds(0, size), :], limit[level : level + 1]
                )
                if width_now == 1:
                    total[pl.ds(0, size), :] = value
                else:
                    sums[n, pl.ds(0, size), :] = value
            level += 1
        for owner in range(no):
            out_box[owner, pl.ds(at, 16), :] = total[pl.ds(owner * piece, 16), :].astype(
                jnp.bfloat16
            )
        for step in range(1, no):
            out_copy(part, lax.rem(o_at + step, no)).start()

    def finish(part):
        _, _, at, piece = parts[part]
        for step in range(1, no):
            out_arrival(part, lax.rem(o_at + step, no)).wait_recv()
        leaves = [out_box[o_at, pl.ds(at, 16), :].astype(jnp.float32)]
        limits = [None]
        for slot in range(1, no):
            source = xor(o_at, slot, obits)
            leaves.append(in_box[source, pl.ds(at, 16), :].astype(jnp.float32))
            limits.append(limits_in[source].astype(jnp.float32))
        many = no
        for hop in range(obits):
            many //= 2
            level = ibits + hop
            leaves = [
                leaves[n] + clipped(leaves[n + many], limits[n + many][level : level + 1])
                for n in range(many)
            ]
        out_ref[pl.ds(at, piece), :] = leaves[0][0:piece]

    for part in range(count):
        local_copy(part).wait()
        for slot in range(1, ni):
            if slot // 2 == half:
                for way in range(2):
                    hop2_arrival(part, way, slot % 2).wait_recv()
            else:
                block_arrival(part, slot).wait_recv()
        if part + 1 < count:
            forward(part + 1)
        if part + 2 < count:
            send_steps(part + 2, 0, nz)
        if part == 0:
            for offset in range(nz):
                twin(offset, 1 - core).wait_recv()
            for step in range(1, no):
                limit_arrival(lax.rem(o_at + step, no)).wait_recv()
        work(part)
        if part > 0:
            finish(part - 1)
    finish(count - 1)

    for way in range(2):
        for step in range(1, half + 1):
            ring(way, step).wait_send()
    for offset in range(nz):
        twin(offset, core).wait_send()
    for part in range(count):
        for slot in range(1, ni):
            if slot // 2 != half:
                block_arrival(part, slot).wait_send()
        for way in range(2):
            for k in range(2):
                hop1(part, way, k).wait_send()
                hop2(part, way, k).wait_send()
        for step in range(1, no):
            out_copy(part, lax.rem(o_at + step, no)).wait_send()
    for step in range(1, no):
        limit_copy(lax.rem(o_at + step, no)).wait_send()


def cut_parts(rows, no):
    return tuple(
        (no * at, no * min(16, rows - at), at, min(16, rows - at)) for at in range(0, rows, 16)
    )


def body(acts, key_grad, shifts):
    ni = lax.axis_size("inner")
    no = lax.axis_size("outer")
    tokens, width = acts.shape
    keys = key_grad.shape[1]
    block = width // ni
    rows = block // no
    nz = ni // 2
    half = nz // 2
    parts = cut_parts(rows, no)
    count = len(parts)
    widest = parts[0][1]
    span = max(
        round_up(block * (n + 1), 128) - block * n // 128 * 128 for n in range(ni)
    )
    padded = round_up(rows, 16)
    dma = pltpu.SemaphoreType.DMA
    return pl.pallas_call(
        functools.partial(kernel, ni, no, parts, span),
        out_shape=jax.ShapeDtypeStruct((rows, keys), jnp.float32),
        in_specs=[
            pl.BlockSpec(memory_space=pl.ANY),
            pl.BlockSpec(memory_space=pl.ANY),
            pl.BlockSpec(memory_space=pltpu.SMEM),
        ],
        out_specs=pl.BlockSpec(memory_space=pltpu.VMEM),
        scratch_shapes=[
            pltpu.VMEM((tokens, width), jnp.bfloat16),
            pltpu.VMEM((width, tokens), jnp.bfloat16),
            pltpu.VMEM((ni, block, tokens), jnp.bfloat16),
            pltpu.VMEM((2, block, tokens), jnp.bfloat16),
            pltpu.VMEM((ni, tokens + BOUND_ROWS, keys), jnp.bfloat16),
            pltpu.VMEM((ni // 4, widest, keys), jnp.float32),
            pltpu.VMEM((widest, keys), jnp.float32),
            pltpu.VMEM((widest, span), jnp.int32),
            pltpu.VMEM((parts[-1][1], span), jnp.int32),
            pltpu.VMEM((no, padded, keys), jnp.bfloat16),
            pltpu.VMEM((no, padded, keys), jnp.bfloat16),
            pltpu.VMEM((BOUND_ROWS, keys), jnp.bfloat16),
            pltpu.VMEM((no, BOUND_ROWS, keys), jnp.bfloat16),
            dma((4,)),
            dma,
            dma((2, half)),
            dma((2, half)),
            dma((nz,)),
            dma((nz,)),
            dma((count, ni)),
            dma((count, ni)),
            dma((count, 2, 2)),
            dma((count, 2, 2)),
            dma((count, 2, 2)),
            dma((count, 2, 2)),
            dma((count,)),
            dma((count, no)),
            dma((count, no)),
            dma((no,)),
            dma((no,)),
        ],
        compiler_params=pltpu.CompilerParams(
            collective_id=0, has_side_effects=True, vmem_limit_bytes=56 * 1024 * 1024
        ),
        cost_estimate=pl.CostEstimate(
            flops=2 * tokens * width * keys, bytes_accessed=2 * tokens * width, transcendentals=0
        ),
    )(acts, key_grad, shifts)


def solution(mesh):
    return jax.shard_map(
        body,
        mesh=mesh,
        in_specs=(
            P(("inner", "outer"), None),
            P(("inner", "outer"), None),
            P(("inner", "outer"), None),
        ),
        out_specs=P(("inner", "outer"), None),
        check_vma=False,
    )
```

```python
import functools

import jax
import jax.numpy as jnp
from jax import lax
from jax.experimental import pallas as pl
from jax.experimental.pallas import tpu as pltpu
from jax.sharding import PartitionSpec as P

MESH = pl.DeviceIdType.MESH
BOUND_ROWS = 16


def xor(a, b, bits):
    total = 0
    for bit in range(bits):
        step = 1 << bit
        total = total + step * lax.rem(lax.div(a, step) + lax.div(b, step), 2)
    return total


def clipped(values, bound):
    return jnp.clip(values, -bound, bound).astype(jnp.bfloat16).astype(jnp.float32)


def aligned(index):
    return pl.multiple_of(index, 16)


def round_up(value, unit):
    return -(-value // unit) * unit


def kernel(
    ni,
    no,
    parts,
    span,
    acts_hbm,
    grad_hbm,
    shifts_smem,
    out_ref,
    raw,
    acts_t,
    recv,
    relay,
    grads,
    sums,
    total,
    place,
    place_last,
    out_box,
    in_box,
    limit_box,
    limits_in,
    fetch_sem,
    grad_sem,
    ring_send,
    ring_recv,
    twin_send,
    twin_recv,
    block_send,
    block_recv,
    hop1_send,
    hop1_recv,
    hop2_send,
    hop2_recv,
    local_sem,
    out_send,
    out_recv,
    limit_send,
    limit_recv,
):
    tokens, width = raw.shape
    keys = grads.shape[2]
    block = width // ni
    rows = block // no
    nz = ni // 2
    half = nz // 2
    first = half // 2
    ibits = ni.bit_length() - 1
    obits = no.bit_length() - 1
    quarters = 4
    strip = width // quarters
    count = len(parts)

    i_at = lax.axis_index("inner")
    o_at = lax.axis_index("outer")
    z_at = lax.div(i_at, 2)
    core = lax.rem(i_at, 2)

    def z_off(step):
        return lax.rem(z_at + step + nz, nz)

    def at_inner(z, k):
        return (2 * z + k, o_at)

    def fetch(q):
        cols = pl.ds(q * strip, strip)
        return pltpu.make_async_copy(acts_hbm.at[:, cols], raw.at[:, cols], fetch_sem.at[q])

    grad_copy = pltpu.make_async_copy(grad_hbm, grads.at[i_at, pl.ds(0, tokens)], grad_sem)
    grad_copy.start()
    for q in range(quarters):
        fetch(q).start()

    barrier = pltpu.get_barrier_semaphore()
    for step in range(1, ni):
        pl.semaphore_signal(
            barrier, inc=1, device_id=(lax.rem(i_at + step, ni), o_at), device_id_type=MESH
        )
    for step in range(1, no):
        pl.semaphore_signal(
            barrier, inc=1, device_id=(i_at, lax.rem(o_at + step, no)), device_id_type=MESH
        )

    row_at = lax.broadcasted_iota(jnp.int32, (BOUND_ROWS, keys), 0)
    left_shift = jnp.zeros((BOUND_ROWS, keys), jnp.int32)
    for hop in range(ibits + obits):
        left_shift = jnp.where(row_at == hop, 12 - shifts_smem[0, hop], left_shift)
    own_limits = jnp.left_shift(jnp.ones_like(left_shift), left_shift).astype(jnp.float32) * 0.109375
    own_limits = own_limits.astype(jnp.bfloat16)
    limit_box[...] = own_limits

    def fill_place(ref, piece):
        size = ref.shape[0]
        row = lax.broadcasted_iota(jnp.int32, (size, 128), 0)
        lane = lax.broadcasted_iota(jnp.int32, (size, 128), 1)
        owner = lax.div(row, piece)
        offset = lane - (owner * rows + row - owner * piece)
        for n in range(span // 128):
            ref[:, pl.ds(n * 128, 128)] = offset + n * 128

    fill_place(place, parts[0][3])
    if place_last is not None:
        fill_place(place_last, parts[-1][3])

    grad_copy.wait()
    grads[i_at, pl.ds(tokens, BOUND_ROWS), :] = own_limits

    pl.semaphore_wait(barrier, ni + no - 2)

    grad_rows = grads.shape[1]
    cut = round_up(grad_rows // 2, 16)

    def ring(way, step):
        sign = 1 if way == 0 else -1
        source = 2 * z_off(sign * (1 - step)) + core
        if step < half:
            piece_at = pl.ds(0, grad_rows)
        else:
            piece_at = pl.ds(0, cut) if way == 0 else pl.ds(cut, grad_rows - cut)
        piece = grads.at[source, piece_at]
        return pltpu.make_async_remote_copy(
            src_ref=piece,
            dst_ref=piece,
            send_sem=ring_send.at[way, step - 1],
            recv_sem=ring_recv.at[way, step - 1],
            device_id=at_inner(z_off(sign), core),
            device_id_type=MESH,
        )

    def twin(offset, side):
        source = 2 * z_off(offset) + side
        return pltpu.make_async_remote_copy(
            src_ref=grads.at[source],
            dst_ref=grads.at[source],
            send_sem=twin_send.at[offset % nz],
            recv_sem=twin_recv.at[offset % nz],
            device_id=at_inner(z_at, 1 - core),
            device_id_type=MESH,
        )

    def ring_arrived(step):
        ring(0, step).wait_recv()
        ring(1, step).wait_recv()
        if step < half:
            ring(0, step + 1).start()
            ring(1, step + 1).start()
            twin(-step, core).start()
            twin(step, core).start()
        else:
            twin(half, core).start()

    def limit_copy(target):
        return pltpu.make_async_remote_copy(
            src_ref=limit_box,
            dst_ref=limits_in.at[o_at],
            send_sem=limit_send.at[target],
            recv_sem=limit_recv.at[o_at],
            device_id=(i_at, target),
            device_id_type=MESH,
        )

    def limit_arrival(source):
        return pltpu.make_async_remote_copy(
            src_ref=limit_box,
            dst_ref=limits_in.at[source],
            send_sem=limit_send.at[source],
            recv_sem=limit_recv.at[source],
            device_id=(i_at, source),
            device_id_type=MESH,
        )

    def turn(part, target):
        start, size, at, piece = parts[part]
        column = target * block
        tile = lax.div(column, 128)
        source = place if piece == parts[0][3] else place_last
        pick = (source[...] == column - tile * 128 + at).astype(jnp.bfloat16)
        window = raw[:, pl.ds(pl.multiple_of(tile * 128, 128), span)]
        acts_t[pl.ds(aligned(column + start), size), :] = lax.dot_general(
            pick, window, (((1,), (1,)), ((), ())), preferred_element_type=jnp.float32
        ).astype(jnp.bfloat16)

    def block_copy(part, target):
        start, size = parts[part][:2]
        slot = xor(i_at, target, ibits)
        return pltpu.make_async_remote_copy(
            src_ref=acts_t.at[pl.ds(aligned(target * block + start), size)],
            dst_ref=recv.at[slot, pl.ds(start, size)],
            send_sem=block_send.at[part, slot],
            recv_sem=block_recv.at[part, slot],
            device_id=(target, o_at),
            device_id_type=MESH,
        )

    def halves(part):
        start, size = parts[part][:2]
        low = round_up(size // 2, 16)
        return ((start, low), (start + low, size - low))

    def hop1(part, way, k):
        start, size = halves(part)[way]
        sign = 1 if way == 0 else -1
        target = 2 * z_off(half) + k
        return pltpu.make_async_remote_copy(
            src_ref=acts_t.at[pl.ds(aligned(target * block + start), size)],
            dst_ref=relay.at[k, pl.ds(start, size)],
            send_sem=hop1_send.at[part, way, k],
            recv_sem=hop1_recv.at[part, way, k],
            device_id=at_inner(z_off(sign * first), core),
            device_id_type=MESH,
        )

    def hop2(part, way, k):
        start, size = halves(part)[way]
        sign = 1 if way == 0 else -1
        differ = lax.rem(core + k, 2)
        return pltpu.make_async_remote_copy(
            src_ref=relay.at[k, pl.ds(start, size)],
            dst_ref=recv.at[2 * half + differ, pl.ds(start, size)],
            send_sem=hop2_send.at[part, way, differ],
            recv_sem=hop2_recv.at[part, way, differ],
            device_id=at_inner(z_off(sign * (half - first)), k),
            device_id_type=MESH,
        )

    def hop2_arrival(part, way, differ):
        start, size = halves(part)[way]
        piece = recv.at[2 * half + differ, pl.ds(start, size)]
        return pltpu.make_async_remote_copy(
            src_ref=piece,
            dst_ref=piece,
            send_sem=hop2_send.at[part, way, differ],
            recv_sem=hop2_recv.at[part, way, differ],
            device_id=at_inner(z_off(half), core),
            device_id_type=MESH,
        )

    def block_arrival(part, slot):
        start, size = parts[part][:2]
        piece = recv.at[slot, pl.ds(start, size)]
        return pltpu.make_async_remote_copy(
            src_ref=piece,
            dst_ref=piece,
            send_sem=block_send.at[part, slot],
            recv_sem=block_recv.at[part, slot],
            device_id=at_inner(z_at, 1 - core),
            device_id_type=MESH,
        )

    def local_copy(part):
        start, size = parts[part][:2]
        return pltpu.make_async_copy(
            acts_t.at[pl.ds(aligned(i_at * block + start), size)],
            recv.at[0, pl.ds(start, size)],
            local_sem.at[part],
        )

    def send_steps(part, low, high):
        def one(step, carry):
            odd = lax.rem(step, 2)
            offset = (2 * odd - 1) * (1 - 2 * core) * (half - lax.div(step + odd, 2))
            z = z_off(offset)
            for k in range(2):
                turn(part, 2 * z + k)

            @pl.when(step == 0)
            def _():
                for way in range(2):
                    for k in range(2):
                        hop1(part, way, k).start()

            @pl.when(jnp.logical_and(step > 0, step < nz - 1))
            def _():
                for k in range(2):
                    block_copy(part, 2 * z + k).start()

            @pl.when(step == nz - 1)
            def _():
                block_copy(part, 2 * z_at + 1 - core).start()
                local_copy(part).start()

            return carry

        lax.fori_loop(low, high, one, 0)

    def forward(part):
        for way in range(2):
            for k in range(2):
                hop1(part, way, k).wait_recv()
                hop2(part, way, k).start()

    ring(0, 1).start()
    ring(1, 1).start()
    twin(0, core).start()
    for step in range(1, no):
        limit_copy(lax.rem(o_at + step, no)).start()
    for q in range(quarters):
        fetch(q).wait()
    done = 0
    for step in range(1, half):
        upto = 2 * step + 1 if step < half - 1 else nz
        send_steps(0, done, upto)
        ring_arrived(step)
        done = upto
    if half == 1:
        send_steps(0, 0, nz)
    send_steps(1, 0, 3)
    ring_arrived(half)
    send_steps(1, 3, nz)
    forward(0)
    forward(1)

    def leaf(slot, start, size):
        source = xor(i_at, slot, ibits)
        value = jnp.dot(
            recv[slot, pl.ds(start, size), :],
            grads[source, pl.ds(0, tokens), :],
            preferred_element_type=jnp.float32,
        )
        limit = grads[source, pl.ds(tokens, BOUND_ROWS), :].astype(jnp.float32)
        return value, limit

    def out_copy(part, target):
        piece_at = pl.ds(parts[part][2], 16)
        return pltpu.make_async_remote_copy(
            src_ref=out_box.at[target, piece_at],
            dst_ref=in_box.at[o_at, piece_at],
            send_sem=out_send.at[part, target],
            recv_sem=out_recv.at[part, o_at],
            device_id=(i_at, target),
            device_id_type=MESH,
        )

    def out_arrival(part, source):
        piece_at = pl.ds(parts[part][2], 16)
        return pltpu.make_async_remote_copy(
            src_ref=in_box.at[source, piece_at],
            dst_ref=in_box.at[source, piece_at],
            send_sem=out_send.at[part, source],
            recv_sem=out_recv.at[part, source],
            device_id=(i_at, source),
            device_id_type=MESH,
        )

    quarter = ni // 4

    def arrived(part, n):
        @pl.when(n == 0)
        def _():
            local_copy(part).wait()

        @pl.when(n != 0)
        def _():
            block_arrival(part, n).wait_recv()

        for m in (1, 2, 3):
            slot = n + m * quarter
            if m * quarter != 2 * half:
                block_arrival(part, slot).wait_recv()
                continue

            @pl.when(n < 2)
            def _():
                for way in range(2):
                    hop2_arrival(part, way, n).wait_recv()

            @pl.when(n >= 2)
            def _():
                block_arrival(part, slot).wait_recv()

    def work(part):
        start, size, at, piece = parts[part]

        def group(n, carry):
            arrived(part, n)
            kept, _ = leaf(n, start, size)
            given, limit = leaf(n + 2 * quarter, start, size)
            first_sum = kept + clipped(given, limit[0:1])
            kept, limit_1 = leaf(n + quarter, start, size)
            given, limit = leaf(n + 3 * quarter, start, size)
            second_sum = kept + clipped(given, limit[0:1])
            sums[n, pl.ds(0, size), :] = first_sum + clipped(second_sum, limit_1[1:2])
            return carry

        lax.fori_loop(0, quarter, group, 0)
        level = 2
        width_now = quarter
        while width_now > 1:
            width_now //= 2
            for n in range(width_now):
                source = xor(i_at, n + width_now, ibits)
                limit = grads[source, pl.ds(tokens, BOUND_ROWS), :].astype(jnp.float32)
                value = sums[n, pl.ds(0, size), :] + clipped(
                    sums[n + width_now, pl.ds(0, size), :], limit[level : level + 1]
                )
                if width_now == 1:
                    total[pl.ds(0, size), :] = value
                else:
                    sums[n, pl.ds(0, size), :] = value
            level += 1
        for owner in range(no):
            out_box[owner, pl.ds(at, 16), :] = total[pl.ds(owner * piece, 16), :].astype(
                jnp.bfloat16
            )
        for step in range(1, no):
            out_copy(part, lax.rem(o_at + step, no)).start()

    def finish(part):
        _, _, at, piece = parts[part]
        for step in range(1, no):
            out_arrival(part, lax.rem(o_at + step, no)).wait_recv()
        leaves = [out_box[o_at, pl.ds(at, 16), :].astype(jnp.float32)]
        limits = [None]
        for slot in range(1, no):
            source = xor(o_at, slot, obits)
            leaves.append(in_box[source, pl.ds(at, 16), :].astype(jnp.float32))
            limits.append(limits_in[source].astype(jnp.float32))
        many = no
        for hop in range(obits):
            many //= 2
            level = ibits + hop
            leaves = [
                leaves[n] + clipped(leaves[n + many], limits[n + many][level : level + 1])
                for n in range(many)
            ]
        out_ref[pl.ds(at, piece), :] = leaves[0][0:piece]

    for part in range(count):
        if part == 0:
            for offset in range(nz):
                twin(offset, 1 - core).wait_recv()
            for step in range(1, no):
                limit_arrival(lax.rem(o_at + step, no)).wait_recv()
        work(part)
        if part + 2 < count:
            send_steps(part + 2, 0, nz)
        if part > 0:
            finish(part - 1)
        if part + 2 < count:
            forward(part + 2)
    finish(count - 1)

    for way in range(2):
        for step in range(1, half + 1):
            ring(way, step).wait_send()
    for offset in range(nz):
        twin(offset, core).wait_send()
    for part in range(count):
        for slot in range(1, ni):
            if slot // 2 != half:
                block_arrival(part, slot).wait_send()
        for way in range(2):
            for k in range(2):
                hop1(part, way, k).wait_send()
                hop2(part, way, k).wait_send()
        for step in range(1, no):
            out_copy(part, lax.rem(o_at + step, no)).wait_send()
    for step in range(1, no):
        limit_copy(lax.rem(o_at + step, no)).wait_send()


def cut_parts(rows, no):
    return tuple(
        (no * at, no * min(16, rows - at), at, min(16, rows - at)) for at in range(0, rows, 16)
    )


def body(acts, key_grad, shifts):
    ni = lax.axis_size("inner")
    no = lax.axis_size("outer")
    tokens, width = acts.shape
    keys = key_grad.shape[1]
    block = width // ni
    rows = block // no
    nz = ni // 2
    half = nz // 2
    parts = cut_parts(rows, no)
    count = len(parts)
    widest = parts[0][1]
    span = max(
        round_up(block * (n + 1), 128) - block * n // 128 * 128 for n in range(ni)
    )
    padded = round_up(rows, 16)
    dma = pltpu.SemaphoreType.DMA
    return pl.pallas_call(
        functools.partial(kernel, ni, no, parts, span),
        out_shape=jax.ShapeDtypeStruct((rows, keys), jnp.float32),
        in_specs=[
            pl.BlockSpec(memory_space=pl.ANY),
            pl.BlockSpec(memory_space=pl.ANY),
            pl.BlockSpec(memory_space=pltpu.SMEM),
        ],
        out_specs=pl.BlockSpec(memory_space=pltpu.VMEM),
        scratch_shapes=[
            pltpu.VMEM((tokens, width), jnp.bfloat16),
            pltpu.VMEM((width, tokens), jnp.bfloat16),
            pltpu.VMEM((ni, block, tokens), jnp.bfloat16),
            pltpu.VMEM((2, block, tokens), jnp.bfloat16),
            pltpu.VMEM((ni, tokens + BOUND_ROWS, keys), jnp.bfloat16),
            pltpu.VMEM((ni // 4, widest, keys), jnp.float32),
            pltpu.VMEM((widest, keys), jnp.float32),
            pltpu.VMEM((widest, span), jnp.int32),
            pltpu.VMEM((parts[-1][1], span), jnp.int32),
            pltpu.VMEM((no, padded, keys), jnp.bfloat16),
            pltpu.VMEM((no, padded, keys), jnp.bfloat16),
            pltpu.VMEM((BOUND_ROWS, keys), jnp.bfloat16),
            pltpu.VMEM((no, BOUND_ROWS, keys), jnp.bfloat16),
            dma((4,)),
            dma,
            dma((2, half)),
            dma((2, half)),
            dma((nz,)),
            dma((nz,)),
            dma((count, ni)),
            dma((count, ni)),
            dma((count, 2, 2)),
            dma((count, 2, 2)),
            dma((count, 2, 2)),
            dma((count, 2, 2)),
            dma((count,)),
            dma((count, no)),
            dma((count, no)),
            dma((no,)),
            dma((no,)),
        ],
        compiler_params=pltpu.CompilerParams(
            collective_id=0, has_side_effects=True, vmem_limit_bytes=56 * 1024 * 1024
        ),
        cost_estimate=pl.CostEstimate(
            flops=2 * tokens * width * keys, bytes_accessed=2 * tokens * width, transcendentals=0
        ),
    )(acts, key_grad, shifts)


def solution(mesh):
    return jax.shard_map(
        body,
        mesh=mesh,
        in_specs=(
            P(("inner", "outer"), None),
            P(("inner", "outer"), None),
            P(("inner", "outer"), None),
        ),
        out_specs=P(("inner", "outer"), None),
        check_vma=False,
    )
```

```python
import functools

import jax
import jax.numpy as jnp
from jax import lax
from jax.experimental import pallas as pl
from jax.experimental.pallas import tpu as pltpu
from jax.sharding import PartitionSpec as P

MESH = pl.DeviceIdType.MESH
BOUND_ROWS = 16


def xor(a, b, bits):
    total = 0
    for bit in range(bits):
        step = 1 << bit
        total = total + step * lax.rem(lax.div(a, step) + lax.div(b, step), 2)
    return total


def clipped(values, bound):
    return jnp.clip(values, -bound, bound).astype(jnp.bfloat16).astype(jnp.float32)


def aligned(index):
    return pl.multiple_of(index, 16)


def round_up(value, unit):
    return -(-value // unit) * unit


def kernel(
    ni,
    no,
    parts,
    span,
    acts_hbm,
    grad_hbm,
    shifts_smem,
    out_ref,
    raw,
    acts_t,
    recv,
    relay,
    grads,
    sums,
    total,
    place,
    place_last,
    out_box,
    in_box,
    limit_box,
    limits_in,
    fetch_sem,
    grad_sem,
    ring_send,
    ring_recv,
    twin_send,
    twin_recv,
    block_send,
    block_recv,
    hop1_send,
    hop1_recv,
    hop2_send,
    hop2_recv,
    local_sem,
    out_send,
    out_recv,
    limit_send,
    limit_recv,
):
    tokens, width = raw.shape
    keys = grads.shape[2]
    block = width // ni
    rows = block // no
    nz = ni // 2
    half = nz // 2
    first = half // 2
    ibits = ni.bit_length() - 1
    obits = no.bit_length() - 1
    quarters = 4
    strip = width // quarters
    count = len(parts)

    i_at = lax.axis_index("inner")
    o_at = lax.axis_index("outer")
    z_at = lax.div(i_at, 2)
    core = lax.rem(i_at, 2)

    def z_off(step):
        return lax.rem(z_at + step + nz, nz)

    def at_inner(z, k):
        return (2 * z + k, o_at)

    def fetch(q):
        cols = pl.ds(q * strip, strip)
        return pltpu.make_async_copy(acts_hbm.at[:, cols], raw.at[:, cols], fetch_sem.at[q])

    grad_copy = pltpu.make_async_copy(grad_hbm, grads.at[i_at, pl.ds(0, tokens)], grad_sem)
    grad_copy.start()
    for q in range(quarters):
        fetch(q).start()

    barrier = pltpu.get_barrier_semaphore()
    for step in range(1, ni):
        pl.semaphore_signal(
            barrier, inc=1, device_id=(lax.rem(i_at + step, ni), o_at), device_id_type=MESH
        )
    for step in range(1, no):
        pl.semaphore_signal(
            barrier, inc=1, device_id=(i_at, lax.rem(o_at + step, no)), device_id_type=MESH
        )

    row_at = lax.broadcasted_iota(jnp.int32, (BOUND_ROWS, keys), 0)
    left_shift = jnp.zeros((BOUND_ROWS, keys), jnp.int32)
    for hop in range(ibits + obits):
        left_shift = jnp.where(row_at == hop, 12 - shifts_smem[0, hop], left_shift)
    own_limits = jnp.left_shift(jnp.ones_like(left_shift), left_shift).astype(jnp.float32) * 0.109375
    own_limits = own_limits.astype(jnp.bfloat16)
    limit_box[...] = own_limits

    def fill_place(ref, piece):
        size = ref.shape[0]
        row = lax.broadcasted_iota(jnp.int32, (size, 128), 0)
        lane = lax.broadcasted_iota(jnp.int32, (size, 128), 1)
        owner = lax.div(row, piece)
        offset = lane - (owner * rows + row - owner * piece)
        for n in range(span // 128):
            ref[:, pl.ds(n * 128, 128)] = offset + n * 128

    fill_place(place, parts[0][3])
    if place_last is not None:
        fill_place(place_last, parts[-1][3])

    grad_copy.wait()
    grads[i_at, pl.ds(tokens, BOUND_ROWS), :] = own_limits

    pl.semaphore_wait(barrier, ni + no - 2)

    grad_rows = grads.shape[1]
    cut = round_up(grad_rows // 2, 16)

    def ring(way, step):
        sign = 1 if way == 0 else -1
        source = 2 * z_off(sign * (1 - step)) + core
        if step < half:
            piece_at = pl.ds(0, grad_rows)
        else:
            piece_at = pl.ds(0, cut) if way == 0 else pl.ds(cut, grad_rows - cut)
        piece = grads.at[source, piece_at]
        return pltpu.make_async_remote_copy(
            src_ref=piece,
            dst_ref=piece,
            send_sem=ring_send.at[way, step - 1],
            recv_sem=ring_recv.at[way, step - 1],
            device_id=at_inner(z_off(sign), core),
            device_id_type=MESH,
        )

    def twin(offset, side):
        source = 2 * z_off(offset) + side
        return pltpu.make_async_remote_copy(
            src_ref=grads.at[source],
            dst_ref=grads.at[source],
            send_sem=twin_send.at[offset % nz],
            recv_sem=twin_recv.at[offset % nz],
            device_id=at_inner(z_at, 1 - core),
            device_id_type=MESH,
        )

    def ring_arrived(step):
        ring(0, step).wait_recv()
        ring(1, step).wait_recv()
        if step < half:
            ring(0, step + 1).start()
            ring(1, step + 1).start()
            twin(-step, core).start()
            twin(step, core).start()
        else:
            twin(half, core).start()

    def limit_copy(target):
        return pltpu.make_async_remote_copy(
            src_ref=limit_box,
            dst_ref=limits_in.at[o_at],
            send_sem=limit_send.at[target],
            recv_sem=limit_recv.at[o_at],
            device_id=(i_at, target),
            device_id_type=MESH,
        )

    def limit_arrival(source):
        return pltpu.make_async_remote_copy(
            src_ref=limit_box,
            dst_ref=limits_in.at[source],
            send_sem=limit_send.at[source],
            recv_sem=limit_recv.at[source],
            device_id=(i_at, source),
            device_id_type=MESH,
        )

    def turn(part, target):
        start, size, at, piece = parts[part]
        column = target * block
        tile = lax.div(column, 128)
        source = place if piece == parts[0][3] else place_last
        pick = (source[...] == column - tile * 128 + at).astype(jnp.bfloat16)
        window = raw[:, pl.ds(pl.multiple_of(tile * 128, 128), span)]
        acts_t[pl.ds(aligned(column + start), size), :] = lax.dot_general(
            pick, window, (((1,), (1,)), ((), ())), preferred_element_type=jnp.float32
        ).astype(jnp.bfloat16)

    def block_copy(part, target):
        start, size = parts[part][:2]
        slot = xor(i_at, target, ibits)
        return pltpu.make_async_remote_copy(
            src_ref=acts_t.at[pl.ds(aligned(target * block + start), size)],
            dst_ref=recv.at[slot, pl.ds(start, size)],
            send_sem=block_send.at[part, slot],
            recv_sem=block_recv.at[part, slot],
            device_id=(target, o_at),
            device_id_type=MESH,
        )

    def halves(part):
        start, size = parts[part][:2]
        low = round_up(size // 2, 16)
        return ((start, low), (start + low, size - low))

    def hop1(part, way, k):
        start, size = halves(part)[way]
        sign = 1 if way == 0 else -1
        target = 2 * z_off(half) + k
        return pltpu.make_async_remote_copy(
            src_ref=acts_t.at[pl.ds(aligned(target * block + start), size)],
            dst_ref=relay.at[k, pl.ds(start, size)],
            send_sem=hop1_send.at[part, way, k],
            recv_sem=hop1_recv.at[part, way, k],
            device_id=at_inner(z_off(sign * first), core),
            device_id_type=MESH,
        )

    def hop2(part, way, k):
        start, size = halves(part)[way]
        sign = 1 if way == 0 else -1
        differ = lax.rem(core + k, 2)
        return pltpu.make_async_remote_copy(
            src_ref=relay.at[k, pl.ds(start, size)],
            dst_ref=recv.at[2 * half + differ, pl.ds(start, size)],
            send_sem=hop2_send.at[part, way, differ],
            recv_sem=hop2_recv.at[part, way, differ],
            device_id=at_inner(z_off(sign * (half - first)), k),
            device_id_type=MESH,
        )

    def hop2_arrival(part, way, differ):
        start, size = halves(part)[way]
        piece = recv.at[2 * half + differ, pl.ds(start, size)]
        return pltpu.make_async_remote_copy(
            src_ref=piece,
            dst_ref=piece,
            send_sem=hop2_send.at[part, way, differ],
            recv_sem=hop2_recv.at[part, way, differ],
            device_id=at_inner(z_off(half), core),
            device_id_type=MESH,
        )

    def block_arrival(part, slot):
        start, size = parts[part][:2]
        piece = recv.at[slot, pl.ds(start, size)]
        return pltpu.make_async_remote_copy(
            src_ref=piece,
            dst_ref=piece,
            send_sem=block_send.at[part, slot],
            recv_sem=block_recv.at[part, slot],
            device_id=at_inner(z_at, 1 - core),
            device_id_type=MESH,
        )

    def local_copy(part):
        start, size = parts[part][:2]
        return pltpu.make_async_copy(
            acts_t.at[pl.ds(aligned(i_at * block + start), size)],
            recv.at[0, pl.ds(start, size)],
            local_sem.at[part],
        )

    def send_steps(part, low, high):
        def one(step, carry):
            odd = lax.rem(step, 2)
            offset = (2 * odd - 1) * (1 - 2 * core) * (half - lax.div(step + odd, 2))
            z = z_off(offset)
            for k in range(2):
                turn(part, 2 * z + k)

            @pl.when(step == 0)
            def _():
                for way in range(2):
                    for k in range(2):
                        hop1(part, way, k).start()

            @pl.when(jnp.logical_and(step > 0, step < nz - 1))
            def _():
                for k in range(2):
                    block_copy(part, 2 * z + k).start()

            @pl.when(step == nz - 1)
            def _():
                block_copy(part, 2 * z_at + 1 - core).start()
                local_copy(part).start()

            return carry

        lax.fori_loop(low, high, one, 0)

    def forward(part):
        for way in range(2):
            for k in range(2):
                hop1(part, way, k).wait_recv()
                hop2(part, way, k).start()

    ring(0, 1).start()
    ring(1, 1).start()
    twin(0, core).start()
    for step in range(1, no):
        limit_copy(lax.rem(o_at + step, no)).start()
    for q in range(quarters):
        fetch(q).wait()
    ahead = min(3, count)
    turns = [(0, 0, 3), (0, 3, 5), (0, 5, nz), (1, 0, 3), (1, 3, nz)]
    turns = [(part, low, min(high, nz)) for part, low, high in turns if low < nz and part < ahead]
    turns += [(part, 0, nz) for part in range(2, ahead)]
    waits = {0: 1, 1: 2, 3: 3, 4: 4}
    for turn_at, (part, low, high) in enumerate(turns):
        send_steps(part, low, high)
        if waits.get(turn_at, half + 1) <= half:
            ring_arrived(waits[turn_at])
    for part in range(ahead):
        forward(part)

    def leaf(slot, start, size):
        source = xor(i_at, slot, ibits)
        value = jnp.dot(
            recv[slot, pl.ds(start, size), :],
            grads[source, pl.ds(0, tokens), :],
            preferred_element_type=jnp.float32,
        )
        limit = grads[source, pl.ds(tokens, BOUND_ROWS), :].astype(jnp.float32)
        return value, limit

    def out_copy(part, target):
        piece_at = pl.ds(parts[part][2], 16)
        return pltpu.make_async_remote_copy(
            src_ref=out_box.at[target, piece_at],
            dst_ref=in_box.at[o_at, piece_at],
            send_sem=out_send.at[part, target],
            recv_sem=out_recv.at[part, o_at],
            device_id=(i_at, target),
            device_id_type=MESH,
        )

    def out_arrival(part, source):
        piece_at = pl.ds(parts[part][2], 16)
        return pltpu.make_async_remote_copy(
            src_ref=in_box.at[source, piece_at],
            dst_ref=in_box.at[source, piece_at],
            send_sem=out_send.at[part, source],
            recv_sem=out_recv.at[part, source],
            device_id=(i_at, source),
            device_id_type=MESH,
        )

    quarter = ni // 4

    def arrived(part, n):
        @pl.when(n == 0)
        def _():
            local_copy(part).wait()

        @pl.when(n != 0)
        def _():
            block_arrival(part, n).wait_recv()

        for m in (1, 2, 3):
            slot = n + m * quarter
            if m * quarter != 2 * half:
                block_arrival(part, slot).wait_recv()
                continue

            @pl.when(n < 2)
            def _():
                for way in range(2):
                    hop2_arrival(part, way, n).wait_recv()

            @pl.when(n >= 2)
            def _():
                block_arrival(part, slot).wait_recv()

    def work(part):
        start, size, at, piece = parts[part]

        def group(n, carry):
            arrived(part, n)
            kept, _ = leaf(n, start, size)
            given, limit = leaf(n + 2 * quarter, start, size)
            first_sum = kept + clipped(given, limit[0:1])
            kept, limit_1 = leaf(n + quarter, start, size)
            given, limit = leaf(n + 3 * quarter, start, size)
            second_sum = kept + clipped(given, limit[0:1])
            sums[n, pl.ds(0, size), :] = first_sum + clipped(second_sum, limit_1[1:2])
            return carry

        lax.fori_loop(0, quarter, group, 0)
        level = 2
        width_now = quarter
        while width_now > 1:
            width_now //= 2
            for n in range(width_now):
                source = xor(i_at, n + width_now, ibits)
                limit = grads[source, pl.ds(tokens, BOUND_ROWS), :].astype(jnp.float32)
                value = sums[n, pl.ds(0, size), :] + clipped(
                    sums[n + width_now, pl.ds(0, size), :], limit[level : level + 1]
                )
                if width_now == 1:
                    total[pl.ds(0, size), :] = value
                else:
                    sums[n, pl.ds(0, size), :] = value
            level += 1
        for owner in range(no):
            out_box[owner, pl.ds(at, 16), :] = total[pl.ds(owner * piece, 16), :].astype(
                jnp.bfloat16
            )
        for step in range(1, no):
            out_copy(part, lax.rem(o_at + step, no)).start()

    def finish(part):
        _, _, at, piece = parts[part]
        for step in range(1, no):
            out_arrival(part, lax.rem(o_at + step, no)).wait_recv()
        leaves = [out_box[o_at, pl.ds(at, 16), :].astype(jnp.float32)]
        limits = [None]
        for slot in range(1, no):
            source = xor(o_at, slot, obits)
            leaves.append(in_box[source, pl.ds(at, 16), :].astype(jnp.float32))
            limits.append(limits_in[source].astype(jnp.float32))
        many = no
        for hop in range(obits):
            many //= 2
            level = ibits + hop
            leaves = [
                leaves[n] + clipped(leaves[n + many], limits[n + many][level : level + 1])
                for n in range(many)
            ]
        out_ref[pl.ds(at, piece), :] = leaves[0][0:piece]

    def sent(part):
        for slot in range(1, ni):
            if slot // 2 != half:
                block_arrival(part, slot).wait_send()
        for way in range(2):
            for k in range(2):
                hop1(part, way, k).wait_send()
                hop2(part, way, k).wait_send()
        for step in range(1, no):
            out_copy(part, lax.rem(o_at + step, no)).wait_send()

    for part in range(count):
        if part == 0:
            for offset in range(nz):
                twin(offset, 1 - core).wait_recv()
            for step in range(1, no):
                limit_arrival(lax.rem(o_at + step, no)).wait_recv()
        if part + 1 == count:
            for way in range(2):
                for step in range(1, half + 1):
                    ring(way, step).wait_send()
            for offset in range(nz):
                twin(offset, core).wait_send()
            for step in range(1, no):
                limit_copy(lax.rem(o_at + step, no)).wait_send()
            for early in range(part):
                sent(early)
            if part > 0:
                finish(part - 1)
        work(part)
        if part + ahead < count:
            send_steps(part + ahead, 0, nz)
        if 0 < part < count - 1:
            finish(part - 1)
        if part + ahead < count:
            forward(part + ahead)
    finish(count - 1)
    sent(count - 1)


def cut_parts(rows, no):
    return tuple(
        (no * at, no * min(16, rows - at), at, min(16, rows - at)) for at in range(0, rows, 16)
    )


def body(acts, key_grad, shifts):
    ni = lax.axis_size("inner")
    no = lax.axis_size("outer")
    tokens, width = acts.shape
    keys = key_grad.shape[1]
    block = width // ni
    rows = block // no
    nz = ni // 2
    half = nz // 2
    parts = cut_parts(rows, no)
    count = len(parts)
    widest = parts[0][1]
    span = max(
        round_up(block * (n + 1), 128) - block * n // 128 * 128 for n in range(ni)
    )
    padded = round_up(rows, 16)
    dma = pltpu.SemaphoreType.DMA
    return pl.pallas_call(
        functools.partial(kernel, ni, no, parts, span),
        out_shape=jax.ShapeDtypeStruct((rows, keys), jnp.float32),
        in_specs=[
            pl.BlockSpec(memory_space=pl.ANY),
            pl.BlockSpec(memory_space=pl.ANY),
            pl.BlockSpec(memory_space=pltpu.SMEM),
        ],
        out_specs=pl.BlockSpec(memory_space=pltpu.VMEM),
        scratch_shapes=[
            pltpu.VMEM((tokens, width), jnp.bfloat16),
            pltpu.VMEM((width, tokens), jnp.bfloat16),
            pltpu.VMEM((ni, block, tokens), jnp.bfloat16),
            pltpu.VMEM((2, block, tokens), jnp.bfloat16),
            pltpu.VMEM((ni, tokens + BOUND_ROWS, keys), jnp.bfloat16),
            pltpu.VMEM((ni // 4, widest, keys), jnp.float32),
            pltpu.VMEM((widest, keys), jnp.float32),
            pltpu.VMEM((widest, span), jnp.int32),
            pltpu.VMEM((parts[-1][1], span), jnp.int32),
            pltpu.VMEM((no, padded, keys), jnp.bfloat16),
            pltpu.VMEM((no, padded, keys), jnp.bfloat16),
            pltpu.VMEM((BOUND_ROWS, keys), jnp.bfloat16),
            pltpu.VMEM((no, BOUND_ROWS, keys), jnp.bfloat16),
            dma((4,)),
            dma,
            dma((2, half)),
            dma((2, half)),
            dma((nz,)),
            dma((nz,)),
            dma((count, ni)),
            dma((count, ni)),
            dma((count, 2, 2)),
            dma((count, 2, 2)),
            dma((count, 2, 2)),
            dma((count, 2, 2)),
            dma((count,)),
            dma((count, no)),
            dma((count, no)),
            dma((no,)),
            dma((no,)),
        ],
        compiler_params=pltpu.CompilerParams(
            collective_id=0, has_side_effects=True, vmem_limit_bytes=56 * 1024 * 1024
        ),
        cost_estimate=pl.CostEstimate(
            flops=2 * tokens * width * keys, bytes_accessed=2 * tokens * width, transcendentals=0
        ),
    )(acts, key_grad, shifts)


def solution(mesh):
    return jax.shard_map(
        body,
        mesh=mesh,
        in_specs=(
            P(("inner", "outer"), None),
            P(("inner", "outer"), None),
            P(("inner", "outer"), None),
        ),
        out_specs=P(("inner", "outer"), None),
        check_vma=False,
    )
```

```python
import functools

import jax
import jax.numpy as jnp
from jax import lax
from jax.experimental import pallas as pl
from jax.experimental.pallas import tpu as pltpu
from jax.sharding import PartitionSpec as P

MESH = pl.DeviceIdType.MESH
BOUND_ROWS = 16


def xor(a, b, bits):
    total = 0
    for bit in range(bits):
        step = 1 << bit
        total = total + step * lax.rem(lax.div(a, step) + lax.div(b, step), 2)
    return total


def clipped(values, bound):
    return jnp.clip(values, -bound, bound).astype(jnp.bfloat16).astype(jnp.float32)


def aligned(index):
    return pl.multiple_of(index, 16)


def round_up(value, unit):
    return -(-value // unit) * unit


def kernel(
    ni,
    no,
    parts,
    span,
    acts_hbm,
    grad_hbm,
    shifts_hbm,
    out_ref,
    raw,
    acts_t,
    recv,
    relay,
    grads,
    limits,
    sums,
    total,
    place,
    place_last,
    out_box,
    in_box,
    limit_box,
    limits_in,
    shifts_smem,
    shift_sem,
    fetch_sem,
    grad_sem,
    ring_send,
    ring_recv,
    tile_send,
    tile_recv,
    twin_send,
    twin_recv,
    twin_tile_send,
    twin_tile_recv,
    block_send,
    block_recv,
    hop1_send,
    hop1_recv,
    hop2_send,
    hop2_recv,
    local_sem,
    out_send,
    out_recv,
    limit_send,
    limit_recv,
):
    tokens, width = raw.shape
    keys = grads.shape[2]
    block = width // ni
    rows = block // no
    nz = ni // 2
    half = nz // 2
    first = half // 2
    ibits = ni.bit_length() - 1
    obits = no.bit_length() - 1
    quarters = 4
    strip = width // quarters
    count = len(parts)

    i_at = lax.axis_index("inner")
    o_at = lax.axis_index("outer")
    z_at = lax.div(i_at, 2)
    core = lax.rem(i_at, 2)

    def z_off(step):
        return lax.rem(z_at + step + nz, nz)

    def at_inner(z, k):
        return (2 * z + k, o_at)

    def fetch(q):
        cols = pl.ds(q * strip, strip)
        return pltpu.make_async_copy(acts_hbm.at[:, cols], raw.at[:, cols], fetch_sem.at[q])

    shift_copy = pltpu.make_async_copy(shifts_hbm, shifts_smem, shift_sem)
    shift_copy.start()
    grad_copy = pltpu.make_async_copy(grad_hbm, grads.at[i_at, pl.ds(0, tokens)], grad_sem)
    grad_copy.start()
    for q in range(quarters):
        fetch(q).start()

    barrier = pltpu.get_barrier_semaphore()
    for step in range(1, ni):
        pl.semaphore_signal(
            barrier, inc=1, device_id=(lax.rem(i_at + step, ni), o_at), device_id_type=MESH
        )
    for step in range(1, no):
        pl.semaphore_signal(
            barrier, inc=1, device_id=(i_at, lax.rem(o_at + step, no)), device_id_type=MESH
        )

    row_at = lax.broadcasted_iota(jnp.int32, (BOUND_ROWS, 128), 0)
    left_shift = jnp.zeros((BOUND_ROWS, 128), jnp.int32)
    shift_copy.wait()
    for hop in range(ibits + obits):
        left_shift = jnp.where(row_at == hop, 12 - shifts_smem[0, hop], left_shift)
    own_limits = jnp.left_shift(jnp.ones_like(left_shift), left_shift).astype(jnp.float32) * 0.109375
    own_limits = own_limits.astype(jnp.bfloat16)
    limits[i_at, :, :] = own_limits
    limit_box[...] = own_limits

    def fill_place(ref, piece):
        size = ref.shape[0]
        row = lax.broadcasted_iota(jnp.int32, (size, 128), 0)
        lane = lax.broadcasted_iota(jnp.int32, (size, 128), 1)
        owner = lax.div(row, piece)
        offset = lane - (owner * rows + row - owner * piece)
        for n in range(span // 128):
            ref[:, pl.ds(n * 128, 128)] = offset + n * 128

    fill_place(place, parts[0][3])
    if place_last is not None:
        fill_place(place_last, parts[-1][3])

    grad_copy.wait()
    pl.semaphore_wait(barrier, ni + no - 2)

    cut = tokens // 2

    def ring(way, step):
        sign = 1 if way == 0 else -1
        source = 2 * z_off(sign * (1 - step)) + core
        target = at_inner(z_off(sign), core)
        if step < half:
            piece = grads.at[source]
        else:
            piece = grads.at[source, pl.ds(way * cut, cut)]
        copies = [
            pltpu.make_async_remote_copy(
                src_ref=piece,
                dst_ref=piece,
                send_sem=ring_send.at[way, step - 1],
                recv_sem=ring_recv.at[way, step - 1],
                device_id=target,
                device_id_type=MESH,
            )
        ]
        if step < half or way == 0:
            copies.append(
                pltpu.make_async_remote_copy(
                    src_ref=limits.at[source],
                    dst_ref=limits.at[source],
                    send_sem=tile_send.at[way, step - 1],
                    recv_sem=tile_recv.at[way, step - 1],
                    device_id=target,
                    device_id_type=MESH,
                )
            )
        return copies

    def twin(offset, side):
        source = 2 * z_off(offset) + side
        return [
            pltpu.make_async_remote_copy(
                src_ref=ref.at[source],
                dst_ref=ref.at[source],
                send_sem=send.at[offset % nz],
                recv_sem=recv_at.at[offset % nz],
                device_id=at_inner(z_at, 1 - core),
                device_id_type=MESH,
            )
            for ref, send, recv_at in (
                (grads, twin_send, twin_recv),
                (limits, twin_tile_send, twin_tile_recv),
            )
        ]

    def start_all(copies):
        for copy in copies:
            copy.start()

    def wait_sent(copies):
        for copy in copies:
            copy.wait_send()

    def wait_arrived(copies):
        for copy in copies:
            copy.wait_recv()

    def ring_arrived(step):
        wait_arrived(ring(0, step))
        wait_arrived(ring(1, step))
        if step < half:
            start_all(ring(0, step + 1))
            start_all(ring(1, step + 1))
            start_all(twin(-step, core))
            start_all(twin(step, core))
        else:
            start_all(twin(half, core))

    def limit_copy(target):
        return pltpu.make_async_remote_copy(
            src_ref=limit_box,
            dst_ref=limits_in.at[o_at],
            send_sem=limit_send.at[target],
            recv_sem=limit_recv.at[o_at],
            device_id=(i_at, target),
            device_id_type=MESH,
        )

    def limit_arrival(source):
        return pltpu.make_async_remote_copy(
            src_ref=limit_box,
            dst_ref=limits_in.at[source],
            send_sem=limit_send.at[source],
            recv_sem=limit_recv.at[source],
            device_id=(i_at, source),
            device_id_type=MESH,
        )

    def turn(part, target):
        start, size, at, piece = parts[part]
        column = target * block
        tile = lax.div(column, 128)
        source = place if piece == parts[0][3] else place_last
        pick = (source[...] == column - tile * 128 + at).astype(jnp.bfloat16)
        window = raw[:, pl.ds(pl.multiple_of(tile * 128, 128), span)]
        acts_t[pl.ds(aligned(column + start), size), :] = lax.dot_general(
            pick, window, (((1,), (1,)), ((), ())), preferred_element_type=jnp.float32
        ).astype(jnp.bfloat16)

    def block_copy(part, target):
        start, size = parts[part][:2]
        slot = xor(i_at, target, ibits)
        return pltpu.make_async_remote_copy(
            src_ref=acts_t.at[pl.ds(aligned(target * block + start), size)],
            dst_ref=recv.at[slot, pl.ds(start, size)],
            send_sem=block_send.at[part, slot],
            recv_sem=block_recv.at[part, slot],
            device_id=(target, o_at),
            device_id_type=MESH,
        )

    def halves(part):
        start, size = parts[part][:2]
        low = round_up(size // 2, 16)
        return ((start, low), (start + low, size - low))

    def hop1(part, way, k):
        start, size = halves(part)[way]
        sign = 1 if way == 0 else -1
        target = 2 * z_off(half) + k
        return pltpu.make_async_remote_copy(
            src_ref=acts_t.at[pl.ds(aligned(target * block + start), size)],
            dst_ref=relay.at[k, pl.ds(start, size)],
            send_sem=hop1_send.at[part, way, k],
            recv_sem=hop1_recv.at[part, way, k],
            device_id=at_inner(z_off(sign * first), core),
            device_id_type=MESH,
        )

    def hop2(part, way, k):
        start, size = halves(part)[way]
        sign = 1 if way == 0 else -1
        differ = lax.rem(core + k, 2)
        return pltpu.make_async_remote_copy(
            src_ref=relay.at[k, pl.ds(start, size)],
            dst_ref=recv.at[2 * half + differ, pl.ds(start, size)],
            send_sem=hop2_send.at[part, way, differ],
            recv_sem=hop2_recv.at[part, way, differ],
            device_id=at_inner(z_off(sign * (half - first)), k),
            device_id_type=MESH,
        )

    def hop2_arrival(part, way, differ):
        start, size = halves(part)[way]
        piece = recv.at[2 * half + differ, pl.ds(start, size)]
        return pltpu.make_async_remote_copy(
            src_ref=piece,
            dst_ref=piece,
            send_sem=hop2_send.at[part, way, differ],
            recv_sem=hop2_recv.at[part, way, differ],
            device_id=at_inner(z_off(half), core),
            device_id_type=MESH,
        )

    def block_arrival(part, slot):
        start, size = parts[part][:2]
        piece = recv.at[slot, pl.ds(start, size)]
        return pltpu.make_async_remote_copy(
            src_ref=piece,
            dst_ref=piece,
            send_sem=block_send.at[part, slot],
            recv_sem=block_recv.at[part, slot],
            device_id=at_inner(z_at, 1 - core),
            device_id_type=MESH,
        )

    def local_copy(part):
        start, size = parts[part][:2]
        return pltpu.make_async_copy(
            acts_t.at[pl.ds(aligned(i_at * block + start), size)],
            recv.at[0, pl.ds(start, size)],
            local_sem.at[part],
        )

    def send_steps(part, low, high):
        def one(step, carry):
            odd = lax.rem(step, 2)
            offset = (2 * odd - 1) * (1 - 2 * core) * (half - lax.div(step + odd, 2))
            z = z_off(offset)
            for k in range(2):
                turn(part, 2 * z + k)

            @pl.when(step == 0)
            def _():
                for way in range(2):
                    for k in range(2):
                        hop1(part, way, k).start()

            @pl.when(jnp.logical_and(step > 0, step < nz - 1))
            def _():
                for k in range(2):
                    block_copy(part, 2 * z + k).start()

            @pl.when(step == nz - 1)
            def _():
                block_copy(part, 2 * z_at + 1 - core).start()
                local_copy(part).start()

            return carry

        lax.fori_loop(low, high, one, 0)

    def forward(part):
        for way in range(2):
            for k in range(2):
                hop1(part, way, k).wait_recv()
                hop2(part, way, k).start()

    start_all(ring(0, 1))
    start_all(ring(1, 1))
    start_all(twin(0, core))
    for step in range(1, no):
        limit_copy(lax.rem(o_at + step, no)).start()
    for q in range(quarters):
        fetch(q).wait()
    ahead = min(3, count)
    turns = [(0, 0, 3), (0, 3, 5), (0, 5, nz), (1, 0, 3), (1, 3, nz)]
    turns = [(part, low, min(high, nz)) for part, low, high in turns if low < nz and part < ahead]
    turns += [(part, 0, nz) for part in range(2, ahead)]
    waits = {0: 1, 1: 2, 3: 3, 4: 4}
    for turn_at, (part, low, high) in enumerate(turns):
        send_steps(part, low, high)
        if waits.get(turn_at, half + 1) <= half:
            ring_arrived(waits[turn_at])
    for part in range(ahead):
        forward(part)

    def wide(tile):
        return jnp.tile(tile.astype(jnp.float32), (1, keys // 128))

    def leaf(slot, start, size):
        source = xor(i_at, slot, ibits)
        value = jnp.dot(
            recv[slot, pl.ds(start, size), :],
            grads[source],
            preferred_element_type=jnp.float32,
        )
        return value, wide(limits[source])

    def out_copy(part, target):
        piece_at = pl.ds(parts[part][2], 16)
        return pltpu.make_async_remote_copy(
            src_ref=out_box.at[target, piece_at],
            dst_ref=in_box.at[o_at, piece_at],
            send_sem=out_send.at[part, target],
            recv_sem=out_recv.at[part, o_at],
            device_id=(i_at, target),
            device_id_type=MESH,
        )

    def out_arrival(part, source):
        piece_at = pl.ds(parts[part][2], 16)
        return pltpu.make_async_remote_copy(
            src_ref=in_box.at[source, piece_at],
            dst_ref=in_box.at[source, piece_at],
            send_sem=out_send.at[part, source],
            recv_sem=out_recv.at[part, source],
            device_id=(i_at, source),
            device_id_type=MESH,
        )

    quarter = ni // 4

    def arrived(part, n):
        @pl.when(n == 0)
        def _():
            local_copy(part).wait()

        @pl.when(n != 0)
        def _():
            block_arrival(part, n).wait_recv()

        for m in (1, 2, 3):
            slot = n + m * quarter
            if m * quarter != 2 * half:
                block_arrival(part, slot).wait_recv()
                continue

            @pl.when(n < 2)
            def _():
                for way in range(2):
                    hop2_arrival(part, way, n).wait_recv()

            @pl.when(n >= 2)
            def _():
                block_arrival(part, slot).wait_recv()

    def work(part):
        start, size, at, piece = parts[part]

        def group(n, carry):
            arrived(part, n)
            kept, _ = leaf(n, start, size)
            given, limit = leaf(n + 2 * quarter, start, size)
            first_sum = kept + clipped(given, limit[0:1])
            kept, limit_1 = leaf(n + quarter, start, size)
            given, limit = leaf(n + 3 * quarter, start, size)
            second_sum = kept + clipped(given, limit[0:1])
            sums[n, pl.ds(0, size), :] = first_sum + clipped(second_sum, limit_1[1:2])
            return carry

        lax.fori_loop(0, quarter, group, 0)
        level = 2
        width_now = quarter
        while width_now > 1:
            width_now //= 2
            for n in range(width_now):
                source = xor(i_at, n + width_now, ibits)
                limit = wide(limits[source])
                value = sums[n, pl.ds(0, size), :] + clipped(
                    sums[n + width_now, pl.ds(0, size), :], limit[level : level + 1]
                )
                if width_now == 1:
                    total[pl.ds(0, size), :] = value
                else:
                    sums[n, pl.ds(0, size), :] = value
            level += 1
        for owner in range(no):
            out_box[owner, pl.ds(at, 16), :] = total[pl.ds(owner * piece, 16), :].astype(
                jnp.bfloat16
            )
        for step in range(1, no):
            out_copy(part, lax.rem(o_at + step, no)).start()

    def finish(part):
        _, _, at, piece = parts[part]
        for step in range(1, no):
            out_arrival(part, lax.rem(o_at + step, no)).wait_recv()
        leaves = [out_box[o_at, pl.ds(at, 16), :].astype(jnp.float32)]
        caps = [None]
        for slot in range(1, no):
            source = xor(o_at, slot, obits)
            leaves.append(in_box[source, pl.ds(at, 16), :].astype(jnp.float32))
            caps.append(wide(limits_in[source]))
        many = no
        for hop in range(obits):
            many //= 2
            level = ibits + hop
            leaves = [
                leaves[n] + clipped(leaves[n + many], caps[n + many][level : level + 1])
                for n in range(many)
            ]
        out_ref[pl.ds(at, piece), :] = leaves[0][0:piece]

    def blocks_sent(part):
        for slot in range(1, ni):
            if slot // 2 != half:
                block_arrival(part, slot).wait_send()
        for way in range(2):
            for k in range(2):
                hop1(part, way, k).wait_send()
                hop2(part, way, k).wait_send()

    def pieces_sent(part):
        for step in range(1, no):
            out_copy(part, lax.rem(o_at + step, no)).wait_send()

    for part in range(count):
        if part == 0:
            for offset in range(nz):
                wait_arrived(twin(offset, 1 - core))
            for step in range(1, no):
                limit_arrival(lax.rem(o_at + step, no)).wait_recv()
        if part + 1 == count:
            for way in range(2):
                for step in range(1, half + 1):
                    wait_sent(ring(way, step))
            for offset in range(nz):
                wait_sent(twin(offset, core))
            for step in range(1, no):
                limit_copy(lax.rem(o_at + step, no)).wait_send()
            for early in range(part):
                blocks_sent(early)
                pieces_sent(early)
            if part > 0:
                finish(part - 1)
        work(part)
        if part + ahead < count:
            send_steps(part + ahead, 0, nz)
        if 0 < part < count - 1:
            finish(part - 1)
        if part + ahead < count:
            forward(part + ahead)
    blocks_sent(count - 1)
    finish(count - 1)
    pieces_sent(count - 1)


def cut_parts(rows, no):
    return tuple(
        (no * at, no * min(16, rows - at), at, min(16, rows - at)) for at in range(0, rows, 16)
    )


def body(acts, key_grad, shifts):
    ni = lax.axis_size("inner")
    no = lax.axis_size("outer")
    tokens, width = acts.shape
    keys = key_grad.shape[1]
    block = width // ni
    rows = block // no
    nz = ni // 2
    half = nz // 2
    parts = cut_parts(rows, no)
    count = len(parts)
    widest = parts[0][1]
    span = max(
        round_up(block * (n + 1), 128) - block * n // 128 * 128 for n in range(ni)
    )
    padded = round_up(rows, 16)
    dma = pltpu.SemaphoreType.DMA
    return pl.pallas_call(
        functools.partial(kernel, ni, no, parts, span),
        out_shape=pltpu.VMEM((rows, keys), jnp.float32),
        in_specs=[
            pl.BlockSpec(memory_space=pl.ANY),
            pl.BlockSpec(memory_space=pl.ANY),
            pl.BlockSpec(memory_space=pl.ANY),
        ],
        out_specs=pl.BlockSpec(memory_space=pltpu.VMEM),
        scratch_shapes=[
            pltpu.VMEM((tokens, width), jnp.bfloat16),
            pltpu.VMEM((width, tokens), jnp.bfloat16),
            pltpu.VMEM((ni, block, tokens), jnp.bfloat16),
            pltpu.VMEM((2, block, tokens), jnp.bfloat16),
            pltpu.VMEM((ni, tokens, keys), jnp.bfloat16),
            pltpu.VMEM((ni, BOUND_ROWS, 128), jnp.bfloat16),
            pltpu.VMEM((ni // 4, widest, keys), jnp.float32),
            pltpu.VMEM((widest, keys), jnp.float32),
            pltpu.VMEM((widest, span), jnp.int32),
            pltpu.VMEM((parts[-1][1], span), jnp.int32),
            pltpu.VMEM((no, padded, keys), jnp.bfloat16),
            pltpu.VMEM((no, padded, keys), jnp.bfloat16),
            pltpu.VMEM((BOUND_ROWS, 128), jnp.bfloat16),
            pltpu.VMEM((no, BOUND_ROWS, 128), jnp.bfloat16),
            pltpu.SMEM(shifts.shape, jnp.int32),
            dma,
            dma((4,)),
            dma,
            dma((2, half)),
            dma((2, half)),
            dma((2, half)),
            dma((2, half)),
            dma((nz,)),
            dma((nz,)),
            dma((nz,)),
            dma((nz,)),
            dma((count, ni)),
            dma((count, ni)),
            dma((count, 2, 2)),
            dma((count, 2, 2)),
            dma((count, 2, 2)),
            dma((count, 2, 2)),
            dma((count,)),
            dma((count, no)),
            dma((count, no)),
            dma((no,)),
            dma((no,)),
        ],
        compiler_params=pltpu.CompilerParams(
            collective_id=0, has_side_effects=True, vmem_limit_bytes=56 * 1024 * 1024
        ),
        cost_estimate=pl.CostEstimate(
            flops=2 * tokens * width * keys, bytes_accessed=2 * tokens * width, transcendentals=0
        ),
    )(acts, key_grad, shifts)


def solution(mesh):
    return jax.shard_map(
        body,
        mesh=mesh,
        in_specs=(
            P(("inner", "outer"), None),
            P(("inner", "outer"), None),
            P(("inner", "outer"), None),
        ),
        out_specs=P(("inner", "outer"), None),
        check_vma=False,
    )
```

```python
import functools

import jax
import jax.numpy as jnp
from jax import lax
from jax.experimental import pallas as pl
from jax.experimental.pallas import tpu as pltpu
from jax.sharding import PartitionSpec as P

MESH = pl.DeviceIdType.MESH
BOUND_ROWS = 16


def xor(a, b, bits):
    total = 0
    for bit in range(bits):
        step = 1 << bit
        total = total + step * lax.rem(lax.div(a, step) + lax.div(b, step), 2)
    return total


def clipped(values, bound):
    return jnp.clip(values, -bound, bound).astype(jnp.bfloat16).astype(jnp.float32)


def aligned(index):
    return pl.multiple_of(index, 16)


def round_up(value, unit):
    return -(-value // unit) * unit


def kernel(
    ni,
    no,
    parts,
    span,
    acts_hbm,
    grad_hbm,
    shifts_hbm,
    out_ref,
    raw,
    acts_t,
    recv,
    relay,
    grads,
    limits,
    sums,
    total,
    place,
    place_last,
    out_box,
    in_box,
    limit_box,
    limits_in,
    shifts_smem,
    shift_sem,
    fetch_sem,
    grad_sem,
    ring_send,
    ring_recv,
    tile_send,
    tile_recv,
    twin_send,
    twin_recv,
    twin_tile_send,
    twin_tile_recv,
    block_send,
    block_recv,
    hop1_send,
    hop1_recv,
    hop2_send,
    hop2_recv,
    local_sem,
    out_send,
    out_recv,
    limit_send,
    limit_recv,
):
    tokens, width = raw.shape
    keys = grads.shape[2]
    block = width // ni
    rows = block // no
    nz = ni // 2
    half = nz // 2
    first = half // 2
    ibits = ni.bit_length() - 1
    obits = no.bit_length() - 1
    quarters = 4
    strip = width // quarters
    count = len(parts)

    i_at = lax.axis_index("inner")
    o_at = lax.axis_index("outer")
    z_at = lax.div(i_at, 2)
    core = lax.rem(i_at, 2)

    def z_off(step):
        return lax.rem(z_at + step + nz, nz)

    def at_inner(z, k):
        return (2 * z + k, o_at)

    def fetch(q):
        cols = pl.ds(q * strip, strip)
        return pltpu.make_async_copy(acts_hbm.at[:, cols], raw.at[:, cols], fetch_sem.at[q])

    shift_copy = pltpu.make_async_copy(shifts_hbm, shifts_smem, shift_sem)
    shift_copy.start()
    grad_copy = pltpu.make_async_copy(grad_hbm, grads.at[i_at, pl.ds(0, tokens)], grad_sem)
    grad_copy.start()
    for q in range(quarters):
        fetch(q).start()

    barrier = pltpu.get_barrier_semaphore()
    for step in range(1, ni):
        pl.semaphore_signal(
            barrier, inc=1, device_id=(lax.rem(i_at + step, ni), o_at), device_id_type=MESH
        )
    for step in range(1, no):
        pl.semaphore_signal(
            barrier, inc=1, device_id=(i_at, lax.rem(o_at + step, no)), device_id_type=MESH
        )

    row_at = lax.broadcasted_iota(jnp.int32, (BOUND_ROWS, 128), 0)
    left_shift = jnp.zeros((BOUND_ROWS, 128), jnp.int32)
    shift_copy.wait()
    for hop in range(ibits + obits):
        left_shift = jnp.where(row_at == hop, 12 - shifts_smem[0, hop], left_shift)
    own_limits = jnp.left_shift(jnp.ones_like(left_shift), left_shift).astype(jnp.float32) * 0.109375
    own_limits = own_limits.astype(jnp.bfloat16)
    limits[i_at, :, :] = own_limits
    limit_box[...] = own_limits

    def fill_place(ref, piece):
        size = ref.shape[0]
        row = lax.broadcasted_iota(jnp.int32, (size, 128), 0)
        lane = lax.broadcasted_iota(jnp.int32, (size, 128), 1)
        owner = lax.div(row, piece)
        offset = lane - (owner * rows + row - owner * piece)
        for n in range(span // 128):
            ref[:, pl.ds(n * 128, 128)] = offset + n * 128

    fill_place(place, parts[0][3])
    if place_last is not None:
        fill_place(place_last, parts[-1][3])

    grad_copy.wait()
    pl.semaphore_wait(barrier, ni + no - 2)

    cut = tokens // 2

    def ring(way, step):
        sign = 1 if way == 0 else -1
        source = 2 * z_off(sign * (1 - step)) + core
        target = at_inner(z_off(sign), core)
        if step < half:
            piece = grads.at[source]
        else:
            piece = grads.at[source, pl.ds(way * cut, cut)]
        copies = [
            pltpu.make_async_remote_copy(
                src_ref=piece,
                dst_ref=piece,
                send_sem=ring_send.at[way, step - 1],
                recv_sem=ring_recv.at[way, step - 1],
                device_id=target,
                device_id_type=MESH,
            )
        ]
        if step < half or way == 0:
            copies.append(
                pltpu.make_async_remote_copy(
                    src_ref=limits.at[source],
                    dst_ref=limits.at[source],
                    send_sem=tile_send.at[way, step - 1],
                    recv_sem=tile_recv.at[way, step - 1],
                    device_id=target,
                    device_id_type=MESH,
                )
            )
        return copies

    def twin(offset, side):
        source = 2 * z_off(offset) + side
        return [
            pltpu.make_async_remote_copy(
                src_ref=ref.at[source],
                dst_ref=ref.at[source],
                send_sem=send.at[offset % nz],
                recv_sem=recv_at.at[offset % nz],
                device_id=at_inner(z_at, 1 - core),
                device_id_type=MESH,
            )
            for ref, send, recv_at in (
                (grads, twin_send, twin_recv),
                (limits, twin_tile_send, twin_tile_recv),
            )
        ]

    def start_all(copies):
        for copy in copies:
            copy.start()

    def wait_sent(copies):
        for copy in copies:
            copy.wait_send()

    def wait_arrived(copies):
        for copy in copies:
            copy.wait_recv()

    def ring_arrived(step):
        wait_arrived(ring(0, step))
        wait_arrived(ring(1, step))
        if step < half:
            start_all(ring(0, step + 1))
            start_all(ring(1, step + 1))
            start_all(twin(-step, core))
            start_all(twin(step, core))
        else:
            start_all(twin(half, core))

    def limit_copy(target):
        return pltpu.make_async_remote_copy(
            src_ref=limit_box,
            dst_ref=limits_in.at[o_at],
            send_sem=limit_send.at[target],
            recv_sem=limit_recv.at[o_at],
            device_id=(i_at, target),
            device_id_type=MESH,
        )

    def limit_arrival(source):
        return pltpu.make_async_remote_copy(
            src_ref=limit_box,
            dst_ref=limits_in.at[source],
            send_sem=limit_send.at[source],
            recv_sem=limit_recv.at[source],
            device_id=(i_at, source),
            device_id_type=MESH,
        )

    def turn(part, target):
        start, size, at, piece = parts[part]
        column = target * block
        tile = lax.div(column, 128)
        source = place if piece == parts[0][3] else place_last
        pick = (source[...] == column - tile * 128 + at).astype(jnp.bfloat16)
        window = raw[:, pl.ds(pl.multiple_of(tile * 128, 128), span)]
        acts_t[pl.ds(aligned(column + start), size), :] = lax.dot_general(
            pick, window, (((1,), (1,)), ((), ())), preferred_element_type=jnp.float32
        ).astype(jnp.bfloat16)

    def block_copy(part, target):
        start, size = parts[part][:2]
        slot = xor(i_at, target, ibits)
        return pltpu.make_async_remote_copy(
            src_ref=acts_t.at[pl.ds(aligned(target * block + start), size)],
            dst_ref=recv.at[slot, pl.ds(start, size)],
            send_sem=block_send.at[part, slot],
            recv_sem=block_recv.at[part, slot],
            device_id=(target, o_at),
            device_id_type=MESH,
        )

    def halves(part):
        start, size = parts[part][:2]
        low = round_up(size // 2, 16)
        return ((start, low), (start + low, size - low))

    def hop1(part, way, k):
        start, size = halves(part)[way]
        sign = 1 if way == 0 else -1
        target = 2 * z_off(half) + k
        return pltpu.make_async_remote_copy(
            src_ref=acts_t.at[pl.ds(aligned(target * block + start), size)],
            dst_ref=relay.at[k, pl.ds(start, size)],
            send_sem=hop1_send.at[part, way, k],
            recv_sem=hop1_recv.at[part, way, k],
            device_id=at_inner(z_off(sign * first), core),
            device_id_type=MESH,
        )

    def hop2(part, way, k):
        start, size = halves(part)[way]
        sign = 1 if way == 0 else -1
        differ = lax.rem(core + k, 2)
        return pltpu.make_async_remote_copy(
            src_ref=relay.at[k, pl.ds(start, size)],
            dst_ref=recv.at[2 * half + differ, pl.ds(start, size)],
            send_sem=hop2_send.at[part, way, differ],
            recv_sem=hop2_recv.at[part, way, differ],
            device_id=at_inner(z_off(sign * (half - first)), k),
            device_id_type=MESH,
        )

    def hop2_arrival(part, way, differ):
        start, size = halves(part)[way]
        piece = recv.at[2 * half + differ, pl.ds(start, size)]
        return pltpu.make_async_remote_copy(
            src_ref=piece,
            dst_ref=piece,
            send_sem=hop2_send.at[part, way, differ],
            recv_sem=hop2_recv.at[part, way, differ],
            device_id=at_inner(z_off(half), core),
            device_id_type=MESH,
        )

    def block_arrival(part, slot):
        start, size = parts[part][:2]
        piece = recv.at[slot, pl.ds(start, size)]
        return pltpu.make_async_remote_copy(
            src_ref=piece,
            dst_ref=piece,
            send_sem=block_send.at[part, slot],
            recv_sem=block_recv.at[part, slot],
            device_id=at_inner(z_at, 1 - core),
            device_id_type=MESH,
        )

    def local_copy(part):
        start, size = parts[part][:2]
        return pltpu.make_async_copy(
            acts_t.at[pl.ds(aligned(i_at * block + start), size)],
            recv.at[0, pl.ds(start, size)],
            local_sem.at[part],
        )

    def z_of_step(step):
        odd = lax.rem(step, 2)
        return z_off((2 * odd - 1) * (1 - 2 * core) * (half - lax.div(step + odd, 2)))

    def turn_steps(part, low, high):
        def one(step, carry):
            z = z_of_step(step)
            for k in range(2):
                turn(part, 2 * z + k)
            return carry

        lax.fori_loop(low, high, one, 0)

    def send_steps(part, low, high, turning=False):
        def one(step, carry):
            z = z_of_step(step)
            if turning:
                for k in range(2):
                    turn(part, 2 * z + k)

            @pl.when(step == 0)
            def _():
                for way in range(2):
                    for k in range(2):
                        hop1(part, way, k).start()

            @pl.when(jnp.logical_and(step > 0, step < nz - 1))
            def _():
                for k in range(2):
                    block_copy(part, 2 * z + k).start()

            @pl.when(step == nz - 1)
            def _():
                block_copy(part, 2 * z_at + 1 - core).start()
                local_copy(part).start()

            return carry

        lax.fori_loop(low, high, one, 0)

    def forward(part):
        for way in range(2):
            for k in range(2):
                hop1(part, way, k).wait_recv()
                hop2(part, way, k).start()

    start_all(ring(0, 1))
    start_all(ring(1, 1))
    start_all(twin(0, core))
    for step in range(1, no):
        limit_copy(lax.rem(o_at + step, no)).start()
    for q in range(quarters):
        fetch(q).wait()
    far = min(3, nz)
    near = min(5, nz)
    send_steps(0, 0, far, turning=True)
    ring_arrived(1)
    send_steps(0, far, near, turning=True)
    if half > 1:
        ring_arrived(2)
    send_steps(0, near, nz, turning=True)
    if count > 1:
        send_steps(1, 0, far, turning=True)
    for step in range(3, half + 1):
        ring_arrived(step)
    forward(0)
    if count > 1:
        turn_steps(1, far, nz)
    for part in range(2, count):
        turn_steps(part, 0, nz)

    def wide(tile):
        return jnp.tile(tile.astype(jnp.float32), (1, keys // 128))

    def leaf(slot, start, size):
        source = xor(i_at, slot, ibits)
        value = jnp.dot(
            recv[slot, pl.ds(start, size), :],
            grads[source],
            preferred_element_type=jnp.float32,
        )
        return value, wide(limits[source])

    def out_copy(part, target):
        piece_at = pl.ds(parts[part][2], 16)
        return pltpu.make_async_remote_copy(
            src_ref=out_box.at[target, piece_at],
            dst_ref=in_box.at[o_at, piece_at],
            send_sem=out_send.at[part, target],
            recv_sem=out_recv.at[part, o_at],
            device_id=(i_at, target),
            device_id_type=MESH,
        )

    def out_arrival(part, source):
        piece_at = pl.ds(parts[part][2], 16)
        return pltpu.make_async_remote_copy(
            src_ref=in_box.at[source, piece_at],
            dst_ref=in_box.at[source, piece_at],
            send_sem=out_send.at[part, source],
            recv_sem=out_recv.at[part, source],
            device_id=(i_at, source),
            device_id_type=MESH,
        )

    quarter = ni // 4

    def arrived(part, n):
        @pl.when(n == 0)
        def _():
            local_copy(part).wait()

        @pl.when(n != 0)
        def _():
            block_arrival(part, n).wait_recv()

        for m in (1, 2, 3):
            slot = n + m * quarter
            if m * quarter != 2 * half:
                block_arrival(part, slot).wait_recv()
                continue

            @pl.when(n < 2)
            def _():
                for way in range(2):
                    hop2_arrival(part, way, n).wait_recv()

            @pl.when(n >= 2)
            def _():
                block_arrival(part, slot).wait_recv()

    def work(part):
        start, size, at, piece = parts[part]

        def group(n, carry):
            if part + 1 == count:
                arrived(part, n)
            kept, _ = leaf(n, start, size)
            given, limit = leaf(n + 2 * quarter, start, size)
            first_sum = kept + clipped(given, limit[0:1])
            kept, limit_1 = leaf(n + quarter, start, size)
            given, limit = leaf(n + 3 * quarter, start, size)
            second_sum = kept + clipped(given, limit[0:1])
            sums[n, pl.ds(0, size), :] = first_sum + clipped(second_sum, limit_1[1:2])
            return carry

        lax.fori_loop(0, quarter, group, 0)
        level = 2
        width_now = quarter
        while width_now > 1:
            width_now //= 2
            for n in range(width_now):
                source = xor(i_at, n + width_now, ibits)
                limit = wide(limits[source])
                value = sums[n, pl.ds(0, size), :] + clipped(
                    sums[n + width_now, pl.ds(0, size), :], limit[level : level + 1]
                )
                if width_now == 1:
                    total[pl.ds(0, size), :] = value
                else:
                    sums[n, pl.ds(0, size), :] = value
            level += 1
        for owner in range(no):
            out_box[owner, pl.ds(at, 16), :] = total[pl.ds(owner * piece, 16), :].astype(
                jnp.bfloat16
            )
        for step in range(1, no):
            out_copy(part, lax.rem(o_at + step, no)).start()

    def finish(part):
        _, _, at, piece = parts[part]
        for step in range(1, no):
            out_arrival(part, lax.rem(o_at + step, no)).wait_recv()
        leaves = [out_box[o_at, pl.ds(at, 16), :].astype(jnp.float32)]
        caps = [None]
        for slot in range(1, no):
            source = xor(o_at, slot, obits)
            leaves.append(in_box[source, pl.ds(at, 16), :].astype(jnp.float32))
            caps.append(wide(limits_in[source]))
        many = no
        for hop in range(obits):
            many //= 2
            level = ibits + hop
            leaves = [
                leaves[n] + clipped(leaves[n + many], caps[n + many][level : level + 1])
                for n in range(many)
            ]
        out_ref[pl.ds(at, piece), :] = leaves[0][0:piece]

    def blocks_sent(part):
        for slot in range(1, ni):
            if slot // 2 != half:
                block_arrival(part, slot).wait_send()
        for way in range(2):
            for k in range(2):
                hop1(part, way, k).wait_send()
                hop2(part, way, k).wait_send()

    def pieces_sent(part):
        for step in range(1, no):
            out_copy(part, lax.rem(o_at + step, no)).wait_send()

    for part in range(count):
        if part + 1 == count:
            for way in range(2):
                for step in range(1, half + 1):
                    wait_sent(ring(way, step))
            for offset in range(nz):
                wait_sent(twin(offset, core))
            for step in range(1, no):
                limit_copy(lax.rem(o_at + step, no)).wait_send()
            for early in range(part):
                blocks_sent(early)
                pieces_sent(early)
            if part > 0:
                finish(part - 1)
        else:
            for n in range(quarter):
                arrived(part, jnp.int32(n))
            forward(part + 1)
            send_steps(part + 1, far, nz)
            if part + 2 < count:
                send_steps(part + 2, 0, far)
        if part == 0:
            for offset in range(nz):
                wait_arrived(twin(offset, 1 - core))
            for step in range(1, no):
                limit_arrival(lax.rem(o_at + step, no)).wait_recv()
        work(part)
        if 0 < part < count - 1:
            finish(part - 1)
    blocks_sent(count - 1)
    finish(count - 1)
    pieces_sent(count - 1)


def cut_parts(rows, no):
    return tuple(
        (no * at, no * min(16, rows - at), at, min(16, rows - at)) for at in range(0, rows, 16)
    )


def body(acts, key_grad, shifts):
    ni = lax.axis_size("inner")
    no = lax.axis_size("outer")
    tokens, width = acts.shape
    keys = key_grad.shape[1]
    block = width // ni
    rows = block // no
    nz = ni // 2
    half = nz // 2
    parts = cut_parts(rows, no)
    count = len(parts)
    widest = parts[0][1]
    span = max(
        round_up(block * (n + 1), 128) - block * n // 128 * 128 for n in range(ni)
    )
    padded = round_up(rows, 16)
    dma = pltpu.SemaphoreType.DMA
    return pl.pallas_call(
        functools.partial(kernel, ni, no, parts, span),
        out_shape=pltpu.VMEM((rows, keys), jnp.float32),
        in_specs=[
            pl.BlockSpec(memory_space=pl.ANY),
            pl.BlockSpec(memory_space=pl.ANY),
            pl.BlockSpec(memory_space=pl.ANY),
        ],
        out_specs=pl.BlockSpec(memory_space=pltpu.VMEM),
        scratch_shapes=[
            pltpu.VMEM((tokens, width), jnp.bfloat16),
            pltpu.VMEM((width, tokens), jnp.bfloat16),
            pltpu.VMEM((ni, block, tokens), jnp.bfloat16),
            pltpu.VMEM((2, block, tokens), jnp.bfloat16),
            pltpu.VMEM((ni, tokens, keys), jnp.bfloat16),
            pltpu.VMEM((ni, BOUND_ROWS, 128), jnp.bfloat16),
            pltpu.VMEM((ni // 4, widest, keys), jnp.float32),
            pltpu.VMEM((widest, keys), jnp.float32),
            pltpu.VMEM((widest, span), jnp.int32),
            pltpu.VMEM((parts[-1][1], span), jnp.int32),
            pltpu.VMEM((no, padded, keys), jnp.bfloat16),
            pltpu.VMEM((no, padded, keys), jnp.bfloat16),
            pltpu.VMEM((BOUND_ROWS, 128), jnp.bfloat16),
            pltpu.VMEM((no, BOUND_ROWS, 128), jnp.bfloat16),
            pltpu.SMEM(shifts.shape, jnp.int32),
            dma,
            dma((4,)),
            dma,
            dma((2, half)),
            dma((2, half)),
            dma((2, half)),
            dma((2, half)),
            dma((nz,)),
            dma((nz,)),
            dma((nz,)),
            dma((nz,)),
            dma((count, ni)),
            dma((count, ni)),
            dma((count, 2, 2)),
            dma((count, 2, 2)),
            dma((count, 2, 2)),
            dma((count, 2, 2)),
            dma((count,)),
            dma((count, no)),
            dma((count, no)),
            dma((no,)),
            dma((no,)),
        ],
        compiler_params=pltpu.CompilerParams(
            collective_id=0, has_side_effects=True, vmem_limit_bytes=56 * 1024 * 1024
        ),
        cost_estimate=pl.CostEstimate(
            flops=2 * tokens * width * keys, bytes_accessed=2 * tokens * width, transcendentals=0
        ),
    )(acts, key_grad, shifts)


def solution(mesh):
    return jax.shard_map(
        body,
        mesh=mesh,
        in_specs=(
            P(("inner", "outer"), None),
            P(("inner", "outer"), None),
            P(("inner", "outer"), None),
        ),
        out_specs=P(("inner", "outer"), None),
        check_vma=False,
    )
```

```python
import functools

import jax
import jax.numpy as jnp
from jax import lax
from jax.experimental import pallas as pl
from jax.experimental.pallas import tpu as pltpu
from jax.sharding import PartitionSpec as P

MESH = pl.DeviceIdType.MESH
BOUND_ROWS = 16


def xor(a, b, bits):
    total = 0
    for bit in range(bits):
        step = 1 << bit
        total = total + step * lax.rem(lax.div(a, step) + lax.div(b, step), 2)
    return total


def clipped(values, bound):
    return jnp.clip(values, -bound, bound).astype(jnp.bfloat16).astype(jnp.float32)


def aligned(index):
    return pl.multiple_of(index, 16)


def round_up(value, unit):
    return -(-value // unit) * unit


def kernel(
    ni,
    no,
    parts,
    span,
    acts_hbm,
    grad_hbm,
    shifts_hbm,
    out_ref,
    raw,
    acts_t,
    recv,
    relay,
    grads,
    limits,
    sums,
    total,
    place,
    place_last,
    out_box,
    in_box,
    limit_box,
    limits_in,
    shifts_smem,
    shift_sem,
    fetch_sem,
    grad_sem,
    ring_send,
    ring_recv,
    tile_send,
    tile_recv,
    twin_send,
    twin_recv,
    twin_tile_send,
    twin_tile_recv,
    block_send,
    block_recv,
    hop1_send,
    hop1_recv,
    hop2_send,
    hop2_recv,
    local_sem,
    out_send,
    out_recv,
    limit_send,
    limit_recv,
):
    tokens, width = raw.shape
    keys = grads.shape[2]
    block = width // ni
    rows = block // no
    nz = ni // 2
    half = nz // 2
    first = half // 2
    ibits = ni.bit_length() - 1
    obits = no.bit_length() - 1
    quarters = 4
    strip = width // quarters
    count = len(parts)

    i_at = lax.axis_index("inner")
    o_at = lax.axis_index("outer")
    z_at = lax.div(i_at, 2)
    core = lax.rem(i_at, 2)

    def z_off(step):
        return lax.rem(z_at + step + nz, nz)

    def at_inner(z, k):
        return (2 * z + k, o_at)

    def fetch(q):
        cols = pl.ds(q * strip, strip)
        return pltpu.make_async_copy(acts_hbm.at[:, cols], raw.at[:, cols], fetch_sem.at[q])

    shift_copy = pltpu.make_async_copy(shifts_hbm, shifts_smem, shift_sem)
    shift_copy.start()
    grad_copy = pltpu.make_async_copy(grad_hbm, grads.at[i_at, pl.ds(0, tokens)], grad_sem)
    grad_copy.start()
    for q in range(quarters):
        fetch(q).start()

    barrier = pltpu.get_barrier_semaphore()
    for step in range(1, ni):
        pl.semaphore_signal(
            barrier, inc=1, device_id=(lax.rem(i_at + step, ni), o_at), device_id_type=MESH
        )
    for step in range(1, no):
        pl.semaphore_signal(
            barrier, inc=1, device_id=(i_at, lax.rem(o_at + step, no)), device_id_type=MESH
        )

    row_at = lax.broadcasted_iota(jnp.int32, (BOUND_ROWS, 128), 0)
    left_shift = jnp.zeros((BOUND_ROWS, 128), jnp.int32)
    shift_copy.wait()
    for hop in range(ibits + obits):
        left_shift = jnp.where(row_at == hop, 12 - shifts_smem[0, hop], left_shift)
    own_limits = jnp.left_shift(jnp.ones_like(left_shift), left_shift).astype(jnp.float32) * 0.109375
    own_limits = own_limits.astype(jnp.bfloat16)
    limits[i_at, :, :] = own_limits
    limit_box[...] = own_limits

    def fill_place(ref, piece):
        size = ref.shape[0]
        row = lax.broadcasted_iota(jnp.int32, (size, 128), 0)
        lane = lax.broadcasted_iota(jnp.int32, (size, 128), 1)
        owner = lax.div(row, piece)
        offset = lane - (owner * rows + row - owner * piece)
        for n in range(span // 128):
            ref[:, pl.ds(n * 128, 128)] = offset + n * 128

    fill_place(place, parts[0][3])
    if place_last is not None:
        fill_place(place_last, parts[-1][3])

    grad_copy.wait()
    pl.semaphore_wait(barrier, ni + no - 2)

    cut = tokens // 2

    def ring(way, step):
        sign = 1 if way == 0 else -1
        source = 2 * z_off(sign * (1 - step)) + core
        target = at_inner(z_off(sign), core)
        if step < half:
            piece = grads.at[source]
        else:
            piece = grads.at[source, pl.ds(way * cut, cut)]
        copies = [
            pltpu.make_async_remote_copy(
                src_ref=piece,
                dst_ref=piece,
                send_sem=ring_send.at[way, step - 1],
                recv_sem=ring_recv.at[way, step - 1],
                device_id=target,
                device_id_type=MESH,
            )
        ]
        if step < half or way == 0:
            copies.append(
                pltpu.make_async_remote_copy(
                    src_ref=limits.at[source],
                    dst_ref=limits.at[source],
                    send_sem=tile_send.at[way, step - 1],
                    recv_sem=tile_recv.at[way, step - 1],
                    device_id=target,
                    device_id_type=MESH,
                )
            )
        return copies

    def twin(offset, side):
        source = 2 * z_off(offset) + side
        return [
            pltpu.make_async_remote_copy(
                src_ref=ref.at[source],
                dst_ref=ref.at[source],
                send_sem=send.at[offset % nz],
                recv_sem=recv_at.at[offset % nz],
                device_id=at_inner(z_at, 1 - core),
                device_id_type=MESH,
            )
            for ref, send, recv_at in (
                (grads, twin_send, twin_recv),
                (limits, twin_tile_send, twin_tile_recv),
            )
        ]

    def start_all(copies):
        for copy in copies:
            copy.start()

    def wait_sent(copies):
        for copy in copies:
            copy.wait_send()

    def wait_arrived(copies):
        for copy in copies:
            copy.wait_recv()

    def ring_arrived(step):
        wait_arrived(ring(0, step))
        wait_arrived(ring(1, step))
        if step < half:
            start_all(ring(0, step + 1))
            start_all(ring(1, step + 1))
            start_all(twin(-step, core))
            start_all(twin(step, core))
        else:
            start_all(twin(half, core))

    def limit_copy(target):
        return pltpu.make_async_remote_copy(
            src_ref=limit_box,
            dst_ref=limits_in.at[o_at],
            send_sem=limit_send.at[target],
            recv_sem=limit_recv.at[o_at],
            device_id=(i_at, target),
            device_id_type=MESH,
        )

    def limit_arrival(source):
        return pltpu.make_async_remote_copy(
            src_ref=limit_box,
            dst_ref=limits_in.at[source],
            send_sem=limit_send.at[source],
            recv_sem=limit_recv.at[source],
            device_id=(i_at, source),
            device_id_type=MESH,
        )

    def turn(part, target):
        start, size, at, piece = parts[part]
        column = target * block
        tile = lax.div(column, 128)
        source = place if piece == parts[0][3] else place_last
        pick = (source[...] == column - tile * 128 + at).astype(jnp.bfloat16)
        window = raw[:, pl.ds(pl.multiple_of(tile * 128, 128), span)]
        acts_t[pl.ds(aligned(column + start), size), :] = lax.dot_general(
            pick, window, (((1,), (1,)), ((), ())), preferred_element_type=jnp.float32
        ).astype(jnp.bfloat16)

    def block_copy(part, target):
        start, size = parts[part][:2]
        slot = xor(i_at, target, ibits)
        return pltpu.make_async_remote_copy(
            src_ref=acts_t.at[pl.ds(aligned(target * block + start), size)],
            dst_ref=recv.at[slot, pl.ds(start, size)],
            send_sem=block_send.at[part, slot],
            recv_sem=block_recv.at[part, slot],
            device_id=(target, o_at),
            device_id_type=MESH,
        )

    def halves(part):
        start, size = parts[part][:2]
        low = round_up(size // 2, 16)
        return ((start, low), (start + low, size - low))

    def hop1(part, way, k):
        start, size = halves(part)[way]
        sign = 1 if way == 0 else -1
        target = 2 * z_off(half) + k
        return pltpu.make_async_remote_copy(
            src_ref=acts_t.at[pl.ds(aligned(target * block + start), size)],
            dst_ref=relay.at[k, pl.ds(start, size)],
            send_sem=hop1_send.at[part, way, k],
            recv_sem=hop1_recv.at[part, way, k],
            device_id=at_inner(z_off(sign * first), core),
            device_id_type=MESH,
        )

    def hop2(part, way, k):
        start, size = halves(part)[way]
        sign = 1 if way == 0 else -1
        differ = lax.rem(core + k, 2)
        return pltpu.make_async_remote_copy(
            src_ref=relay.at[k, pl.ds(start, size)],
            dst_ref=recv.at[2 * half + differ, pl.ds(start, size)],
            send_sem=hop2_send.at[part, way, differ],
            recv_sem=hop2_recv.at[part, way, differ],
            device_id=at_inner(z_off(sign * (half - first)), k),
            device_id_type=MESH,
        )

    def hop2_arrival(part, way, differ):
        start, size = halves(part)[way]
        piece = recv.at[2 * half + differ, pl.ds(start, size)]
        return pltpu.make_async_remote_copy(
            src_ref=piece,
            dst_ref=piece,
            send_sem=hop2_send.at[part, way, differ],
            recv_sem=hop2_recv.at[part, way, differ],
            device_id=at_inner(z_off(half), core),
            device_id_type=MESH,
        )

    def block_arrival(part, slot):
        start, size = parts[part][:2]
        piece = recv.at[slot, pl.ds(start, size)]
        return pltpu.make_async_remote_copy(
            src_ref=piece,
            dst_ref=piece,
            send_sem=block_send.at[part, slot],
            recv_sem=block_recv.at[part, slot],
            device_id=at_inner(z_at, 1 - core),
            device_id_type=MESH,
        )

    def local_copy(part):
        start, size = parts[part][:2]
        return pltpu.make_async_copy(
            acts_t.at[pl.ds(aligned(i_at * block + start), size)],
            recv.at[0, pl.ds(start, size)],
            local_sem.at[part],
        )

    def send_steps(part, low, high):
        def one(step, carry):
            odd = lax.rem(step, 2)
            offset = (2 * odd - 1) * (1 - 2 * core) * (half - lax.div(step + odd, 2))
            z = z_off(offset)
            for k in range(2):
                turn(part, 2 * z + k)

            @pl.when(step == 0)
            def _():
                for way in range(2):
                    for k in range(2):
                        hop1(part, way, k).start()

            @pl.when(jnp.logical_and(step > 0, step < nz - 1))
            def _():
                for k in range(2):
                    block_copy(part, 2 * z + k).start()

            @pl.when(step == nz - 1)
            def _():
                block_copy(part, 2 * z_at + 1 - core).start()
                local_copy(part).start()

            return carry

        lax.fori_loop(low, high, one, 0)

    def forward(part):
        for way in range(2):
            for k in range(2):
                hop1(part, way, k).wait_recv()
                hop2(part, way, k).start()

    start_all(ring(0, 1))
    start_all(ring(1, 1))
    start_all(twin(0, core))
    for step in range(1, no):
        limit_copy(lax.rem(o_at + step, no)).start()
    for q in range(quarters):
        fetch(q).wait()
    ahead = count
    turns = [(0, 0, 3), (0, 3, 5), (0, 5, nz), (1, 0, 3), (1, 3, nz)]
    turns = [(part, low, min(high, nz)) for part, low, high in turns if low < nz and part < ahead]
    turns += [(part, 0, nz) for part in range(2, ahead)]
    waits = {0: 1, 1: 2, 3: 3, 4: 4}
    for turn_at, (part, low, high) in enumerate(turns):
        send_steps(part, low, high)
        if waits.get(turn_at, half + 1) <= half:
            ring_arrived(waits[turn_at])
    for part in range(ahead):
        forward(part)

    def wide(tile):
        return jnp.tile(tile.astype(jnp.float32), (1, keys // 128))

    def leaf(slot, start, size):
        source = xor(i_at, slot, ibits)
        value = jnp.dot(
            recv[slot, pl.ds(start, size), :],
            grads[source],
            preferred_element_type=jnp.float32,
        )
        return value, wide(limits[source])

    def out_copy(part, target):
        piece_at = pl.ds(parts[part][2], 16)
        return pltpu.make_async_remote_copy(
            src_ref=out_box.at[target, piece_at],
            dst_ref=in_box.at[o_at, piece_at],
            send_sem=out_send.at[part, target],
            recv_sem=out_recv.at[part, o_at],
            device_id=(i_at, target),
            device_id_type=MESH,
        )

    def out_arrival(part, source):
        piece_at = pl.ds(parts[part][2], 16)
        return pltpu.make_async_remote_copy(
            src_ref=in_box.at[source, piece_at],
            dst_ref=in_box.at[source, piece_at],
            send_sem=out_send.at[part, source],
            recv_sem=out_recv.at[part, source],
            device_id=(i_at, source),
            device_id_type=MESH,
        )

    quarter = ni // 4

    def arrived(part, n):
        @pl.when(n == 0)
        def _():
            local_copy(part).wait()

        @pl.when(n != 0)
        def _():
            block_arrival(part, n).wait_recv()

        for m in (1, 2, 3):
            slot = n + m * quarter
            if m * quarter != 2 * half:
                block_arrival(part, slot).wait_recv()
                continue

            @pl.when(n < 2)
            def _():
                for way in range(2):
                    hop2_arrival(part, way, n).wait_recv()

            @pl.when(n >= 2)
            def _():
                block_arrival(part, slot).wait_recv()

    def work(part):
        start, size, at, piece = parts[part]

        def group(n, carry):
            arrived(part, n)
            kept, _ = leaf(n, start, size)
            given, limit = leaf(n + 2 * quarter, start, size)
            first_sum = kept + clipped(given, limit[0:1])
            kept, limit_1 = leaf(n + quarter, start, size)
            given, limit = leaf(n + 3 * quarter, start, size)
            second_sum = kept + clipped(given, limit[0:1])
            sums[n, pl.ds(0, size), :] = first_sum + clipped(second_sum, limit_1[1:2])
            return carry

        lax.fori_loop(0, quarter, group, 0)
        level = 2
        width_now = quarter
        while width_now > 1:
            width_now //= 2
            for n in range(width_now):
                source = xor(i_at, n + width_now, ibits)
                limit = wide(limits[source])
                value = sums[n, pl.ds(0, size), :] + clipped(
                    sums[n + width_now, pl.ds(0, size), :], limit[level : level + 1]
                )
                if width_now == 1:
                    total[pl.ds(0, size), :] = value
                else:
                    sums[n, pl.ds(0, size), :] = value
            level += 1
        for owner in range(no):
            out_box[owner, pl.ds(at, 16), :] = total[pl.ds(owner * piece, 16), :].astype(
                jnp.bfloat16
            )
        for step in range(1, no):
            out_copy(part, lax.rem(o_at + step, no)).start()

    def finish(part):
        _, _, at, piece = parts[part]
        for step in range(1, no):
            out_arrival(part, lax.rem(o_at + step, no)).wait_recv()
        leaves = [out_box[o_at, pl.ds(at, 16), :].astype(jnp.float32)]
        caps = [None]
        for slot in range(1, no):
            source = xor(o_at, slot, obits)
            leaves.append(in_box[source, pl.ds(at, 16), :].astype(jnp.float32))
            caps.append(wide(limits_in[source]))
        many = no
        for hop in range(obits):
            many //= 2
            level = ibits + hop
            leaves = [
                leaves[n] + clipped(leaves[n + many], caps[n + many][level : level + 1])
                for n in range(many)
            ]
        out_ref[pl.ds(at, piece), :] = leaves[0][0:piece]

    def blocks_sent(part):
        for slot in range(1, ni):
            if slot // 2 != half:
                block_arrival(part, slot).wait_send()
        for way in range(2):
            for k in range(2):
                hop1(part, way, k).wait_send()
                hop2(part, way, k).wait_send()

    def pieces_sent(part):
        for step in range(1, no):
            out_copy(part, lax.rem(o_at + step, no)).wait_send()

    for part in range(count):
        if part == 0:
            for offset in range(nz):
                wait_arrived(twin(offset, 1 - core))
            for step in range(1, no):
                limit_arrival(lax.rem(o_at + step, no)).wait_recv()
        if part + 1 == count:
            for way in range(2):
                for step in range(1, half + 1):
                    wait_sent(ring(way, step))
            for offset in range(nz):
                wait_sent(twin(offset, core))
            for step in range(1, no):
                limit_copy(lax.rem(o_at + step, no)).wait_send()
            for early in range(part):
                blocks_sent(early)
                pieces_sent(early)
            if part > 0:
                finish(part - 1)
        work(part)
        if part + ahead < count:
            send_steps(part + ahead, 0, nz)
        if 0 < part < count - 1:
            finish(part - 1)
        if part + ahead < count:
            forward(part + ahead)
    blocks_sent(count - 1)
    finish(count - 1)
    pieces_sent(count - 1)


def cut_parts(rows, no):
    return tuple(
        (no * at, no * min(16, rows - at), at, min(16, rows - at)) for at in range(0, rows, 16)
    )


def body(acts, key_grad, shifts):
    ni = lax.axis_size("inner")
    no = lax.axis_size("outer")
    tokens, width = acts.shape
    keys = key_grad.shape[1]
    block = width // ni
    rows = block // no
    nz = ni // 2
    half = nz // 2
    parts = cut_parts(rows, no)
    count = len(parts)
    widest = parts[0][1]
    span = max(
        round_up(block * (n + 1), 128) - block * n // 128 * 128 for n in range(ni)
    )
    padded = round_up(rows, 16)
    dma = pltpu.SemaphoreType.DMA
    return pl.pallas_call(
        functools.partial(kernel, ni, no, parts, span),
        out_shape=pltpu.VMEM((rows, keys), jnp.float32),
        in_specs=[
            pl.BlockSpec(memory_space=pl.ANY),
            pl.BlockSpec(memory_space=pl.ANY),
            pl.BlockSpec(memory_space=pl.ANY),
        ],
        out_specs=pl.BlockSpec(memory_space=pltpu.VMEM),
        scratch_shapes=[
            pltpu.VMEM((tokens, width), jnp.bfloat16),
            pltpu.VMEM((width, tokens), jnp.bfloat16),
            pltpu.VMEM((ni, block, tokens), jnp.bfloat16),
            pltpu.VMEM((2, block, tokens), jnp.bfloat16),
            pltpu.VMEM((ni, tokens, keys), jnp.bfloat16),
            pltpu.VMEM((ni, BOUND_ROWS, 128), jnp.bfloat16),
            pltpu.VMEM((ni // 4, widest, keys), jnp.float32),
            pltpu.VMEM((widest, keys), jnp.float32),
            pltpu.VMEM((widest, span), jnp.int32),
            pltpu.VMEM((parts[-1][1], span), jnp.int32),
            pltpu.VMEM((no, padded, keys), jnp.bfloat16),
            pltpu.VMEM((no, padded, keys), jnp.bfloat16),
            pltpu.VMEM((BOUND_ROWS, 128), jnp.bfloat16),
            pltpu.VMEM((no, BOUND_ROWS, 128), jnp.bfloat16),
            pltpu.SMEM(shifts.shape, jnp.int32),
            dma,
            dma((4,)),
            dma,
            dma((2, half)),
            dma((2, half)),
            dma((2, half)),
            dma((2, half)),
            dma((nz,)),
            dma((nz,)),
            dma((nz,)),
            dma((nz,)),
            dma((count, ni)),
            dma((count, ni)),
            dma((count, 2, 2)),
            dma((count, 2, 2)),
            dma((count, 2, 2)),
            dma((count, 2, 2)),
            dma((count,)),
            dma((count, no)),
            dma((count, no)),
            dma((no,)),
            dma((no,)),
        ],
        compiler_params=pltpu.CompilerParams(
            collective_id=0, has_side_effects=True, vmem_limit_bytes=56 * 1024 * 1024
        ),
        cost_estimate=pl.CostEstimate(
            flops=2 * tokens * width * keys, bytes_accessed=2 * tokens * width, transcendentals=0
        ),
    )(acts, key_grad, shifts)


def solution(mesh):
    return jax.shard_map(
        body,
        mesh=mesh,
        in_specs=(
            P(("inner", "outer"), None),
            P(("inner", "outer"), None),
            P(("inner", "outer"), None),
        ),
        out_specs=P(("inner", "outer"), None),
        check_vma=False,
    )
```

```python
import functools

import jax
import jax.numpy as jnp
from jax import lax
from jax.experimental import pallas as pl
from jax.experimental.pallas import tpu as pltpu
from jax.sharding import PartitionSpec as P

MESH = pl.DeviceIdType.MESH
BOUND_ROWS = 16


def xor(a, b, bits):
    total = 0
    for bit in range(bits):
        step = 1 << bit
        total = total + step * lax.rem(lax.div(a, step) + lax.div(b, step), 2)
    return total


def clipped(values, bound):
    return jnp.clip(values, -bound, bound).astype(jnp.bfloat16).astype(jnp.float32)


def aligned(index):
    return pl.multiple_of(index, 16)


def round_up(value, unit):
    return -(-value // unit) * unit


def kernel(
    ni,
    no,
    parts,
    span,
    acts_hbm,
    grad_hbm,
    shifts_hbm,
    out_ref,
    raw,
    acts_t,
    recv,
    relay,
    grads,
    limits,
    sums,
    total,
    place,
    place_last,
    out_box,
    in_box,
    limit_box,
    limits_in,
    shifts_smem,
    shift_sem,
    fetch_sem,
    grad_sem,
    ring_send,
    ring_recv,
    tile_send,
    tile_recv,
    twin_send,
    twin_recv,
    twin_tile_send,
    twin_tile_recv,
    block_send,
    block_recv,
    hop1_send,
    hop1_recv,
    hop2_send,
    hop2_recv,
    local_sem,
    out_send,
    out_recv,
    limit_send,
    limit_recv,
):
    tokens, width = raw.shape
    keys = grads.shape[2]
    block = width // ni
    rows = block // no
    nz = ni // 2
    half = nz // 2
    first = half // 2
    ibits = ni.bit_length() - 1
    obits = no.bit_length() - 1
    quarters = 4
    strip = width // quarters
    count = len(parts)

    i_at = lax.axis_index("inner")
    o_at = lax.axis_index("outer")
    z_at = lax.div(i_at, 2)
    core = lax.rem(i_at, 2)

    def z_off(step):
        return lax.rem(z_at + step + nz, nz)

    def at_inner(z, k):
        return (2 * z + k, o_at)

    def fetch(q):
        cols = pl.ds(q * strip, strip)
        return pltpu.make_async_copy(acts_hbm.at[:, cols], raw.at[:, cols], fetch_sem.at[q])

    shift_copy = pltpu.make_async_copy(shifts_hbm, shifts_smem, shift_sem)
    shift_copy.start()
    grad_copy = pltpu.make_async_copy(grad_hbm, grads.at[i_at, pl.ds(0, tokens)], grad_sem)
    grad_copy.start()
    for q in range(quarters):
        fetch(q).start()

    barrier = pltpu.get_barrier_semaphore()
    for step in range(1, ni):
        pl.semaphore_signal(
            barrier, inc=1, device_id=(lax.rem(i_at + step, ni), o_at), device_id_type=MESH
        )
    for step in range(1, no):
        pl.semaphore_signal(
            barrier, inc=1, device_id=(i_at, lax.rem(o_at + step, no)), device_id_type=MESH
        )

    row_at = lax.broadcasted_iota(jnp.int32, (BOUND_ROWS, 128), 0)
    left_shift = jnp.zeros((BOUND_ROWS, 128), jnp.int32)
    shift_copy.wait()
    for hop in range(ibits + obits):
        left_shift = jnp.where(row_at == hop, 12 - shifts_smem[0, hop], left_shift)
    own_limits = jnp.left_shift(jnp.ones_like(left_shift), left_shift).astype(jnp.float32) * 0.109375
    own_limits = own_limits.astype(jnp.bfloat16)
    limits[i_at, :, :] = own_limits
    limit_box[...] = own_limits

    def fill_place(ref, piece):
        size = ref.shape[0]
        row = lax.broadcasted_iota(jnp.int32, (size, 128), 0)
        lane = lax.broadcasted_iota(jnp.int32, (size, 128), 1)
        owner = lax.div(row, piece)
        offset = lane - (owner * rows + row - owner * piece)
        for n in range(span // 128):
            ref[:, pl.ds(n * 128, 128)] = offset + n * 128

    fill_place(place, parts[0][3])
    if place_last is not None:
        fill_place(place_last, parts[-1][3])

    grad_copy.wait()
    pl.semaphore_wait(barrier, ni + no - 2)

    cut = tokens // 2

    def ring(way, step):
        sign = 1 if way == 0 else -1
        source = 2 * z_off(sign * (1 - step)) + core
        target = at_inner(z_off(sign), core)
        if step < half:
            piece = grads.at[source]
        else:
            piece = grads.at[source, pl.ds(way * cut, cut)]
        copies = [
            pltpu.make_async_remote_copy(
                src_ref=piece,
                dst_ref=piece,
                send_sem=ring_send.at[way, step - 1],
                recv_sem=ring_recv.at[way, step - 1],
                device_id=target,
                device_id_type=MESH,
            )
        ]
        if step < half or way == 0:
            copies.append(
                pltpu.make_async_remote_copy(
                    src_ref=limits.at[source],
                    dst_ref=limits.at[source],
                    send_sem=tile_send.at[way, step - 1],
                    recv_sem=tile_recv.at[way, step - 1],
                    device_id=target,
                    device_id_type=MESH,
                )
            )
        return copies

    def twin(offset, side):
        source = 2 * z_off(offset) + side
        return [
            pltpu.make_async_remote_copy(
                src_ref=ref.at[source],
                dst_ref=ref.at[source],
                send_sem=send.at[offset % nz],
                recv_sem=recv_at.at[offset % nz],
                device_id=at_inner(z_at, 1 - core),
                device_id_type=MESH,
            )
            for ref, send, recv_at in (
                (grads, twin_send, twin_recv),
                (limits, twin_tile_send, twin_tile_recv),
            )
        ]

    def start_all(copies):
        for copy in copies:
            copy.start()

    def wait_sent(copies):
        for copy in copies:
            copy.wait_send()

    def wait_arrived(copies):
        for copy in copies:
            copy.wait_recv()

    def ring_arrived(step):
        wait_arrived(ring(0, step))
        wait_arrived(ring(1, step))
        if step < half:
            start_all(ring(0, step + 1))
            start_all(ring(1, step + 1))
            start_all(twin(-step, core))
            start_all(twin(step, core))
        else:
            start_all(twin(half, core))

    def limit_copy(target):
        return pltpu.make_async_remote_copy(
            src_ref=limit_box,
            dst_ref=limits_in.at[o_at],
            send_sem=limit_send.at[target],
            recv_sem=limit_recv.at[o_at],
            device_id=(i_at, target),
            device_id_type=MESH,
        )

    def limit_arrival(source):
        return pltpu.make_async_remote_copy(
            src_ref=limit_box,
            dst_ref=limits_in.at[source],
            send_sem=limit_send.at[source],
            recv_sem=limit_recv.at[source],
            device_id=(i_at, source),
            device_id_type=MESH,
        )

    def turn(part, target):
        start, size, at, piece = parts[part]
        column = target * block
        tile = lax.div(column, 128)
        source = place if piece == parts[0][3] else place_last
        pick = (source[...] == column - tile * 128 + at).astype(jnp.bfloat16)
        window = raw[:, pl.ds(pl.multiple_of(tile * 128, 128), span)]
        acts_t[pl.ds(aligned(column + start), size), :] = lax.dot_general(
            pick, window, (((1,), (1,)), ((), ())), preferred_element_type=jnp.float32
        ).astype(jnp.bfloat16)

    def block_copy(part, target):
        start, size = parts[part][:2]
        slot = xor(i_at, target, ibits)
        return pltpu.make_async_remote_copy(
            src_ref=acts_t.at[pl.ds(aligned(target * block + start), size)],
            dst_ref=recv.at[slot, pl.ds(start, size)],
            send_sem=block_send.at[part, slot],
            recv_sem=block_recv.at[part, slot],
            device_id=(target, o_at),
            device_id_type=MESH,
        )

    def halves(part):
        start, size = parts[part][:2]
        low = round_up(size // 2, 16)
        return ((start, low), (start + low, size - low))

    def hop1(part, way, k):
        start, size = halves(part)[way]
        sign = 1 if way == 0 else -1
        target = 2 * z_off(half) + k
        return pltpu.make_async_remote_copy(
            src_ref=acts_t.at[pl.ds(aligned(target * block + start), size)],
            dst_ref=relay.at[k, pl.ds(start, size)],
            send_sem=hop1_send.at[part, way, k],
            recv_sem=hop1_recv.at[part, way, k],
            device_id=at_inner(z_off(sign * first), core),
            device_id_type=MESH,
        )

    def hop2(part, way, k):
        start, size = halves(part)[way]
        sign = 1 if way == 0 else -1
        differ = lax.rem(core + k, 2)
        return pltpu.make_async_remote_copy(
            src_ref=relay.at[k, pl.ds(start, size)],
            dst_ref=recv.at[2 * half + differ, pl.ds(start, size)],
            send_sem=hop2_send.at[part, way, differ],
            recv_sem=hop2_recv.at[part, way, differ],
            device_id=at_inner(z_off(sign * (half - first)), k),
            device_id_type=MESH,
        )

    def hop2_arrival(part, way, differ):
        start, size = halves(part)[way]
        piece = recv.at[2 * half + differ, pl.ds(start, size)]
        return pltpu.make_async_remote_copy(
            src_ref=piece,
            dst_ref=piece,
            send_sem=hop2_send.at[part, way, differ],
            recv_sem=hop2_recv.at[part, way, differ],
            device_id=at_inner(z_off(half), core),
            device_id_type=MESH,
        )

    def block_arrival(part, slot):
        start, size = parts[part][:2]
        piece = recv.at[slot, pl.ds(start, size)]
        return pltpu.make_async_remote_copy(
            src_ref=piece,
            dst_ref=piece,
            send_sem=block_send.at[part, slot],
            recv_sem=block_recv.at[part, slot],
            device_id=at_inner(z_at, 1 - core),
            device_id_type=MESH,
        )

    def local_copy(part):
        start, size = parts[part][:2]
        return pltpu.make_async_copy(
            acts_t.at[pl.ds(aligned(i_at * block + start), size)],
            recv.at[0, pl.ds(start, size)],
            local_sem.at[part],
        )

    def z_of_step(step):
        odd = lax.rem(step, 2)
        return z_off((2 * odd - 1) * (1 - 2 * core) * (half - lax.div(step + odd, 2)))

    def by_step(part, step, act):
        z = z_of_step(step)

        @pl.when(step == 0)
        def _():
            for way in range(2):
                for k in range(2):
                    act(hop1(part, way, k))

        @pl.when(jnp.logical_and(step > 0, step < nz - 1))
        def _():
            for k in range(2):
                act(block_copy(part, 2 * z + k))

        @pl.when(step == nz - 1)
        def _():
            act(block_copy(part, 2 * z_at + 1 - core))

    def start(copy):
        copy.start()

    def leave(copy):
        copy.wait_send()

    def turn_steps(part, low, high):
        def one(step, carry):
            z = z_of_step(step)
            for k in range(2):
                turn(part, 2 * z + k)
            return carry

        lax.fori_loop(low, high, one, 0)
        if high == nz:
            local_copy(part).start()

    def first_steps(part, low, high):
        def one(step, carry):
            z = z_of_step(step)
            for k in range(2):
                turn(part, 2 * z + k)
            by_step(part, step, start)
            return carry

        lax.fori_loop(low, high, one, 0)
        if high == nz:
            local_copy(part).start()

    def wait_steps(part, low, high):
        def one(step, carry):
            by_step(part, step, leave)
            return carry

        lax.fori_loop(low, high, one, 0)

    def next_steps(part, low, high, part_before, low_before):
        def one(step, carry):
            by_step(part_before, step - low + low_before, leave)
            by_step(part, step, start)
            return carry

        lax.fori_loop(low, high, one, 0)

    def forward(part):
        for way in range(2):
            for k in range(2):
                hop1(part, way, k).wait_recv()
                hop2(part, way, k).start()

    start_all(ring(0, 1))
    start_all(ring(1, 1))
    start_all(twin(0, core))
    for step in range(1, no):
        limit_copy(lax.rem(o_at + step, no)).start()
    for q in range(quarters):
        fetch(q).wait()
    far = min(3, nz)
    near = min(5, nz)
    first_steps(0, 0, far)
    ring_arrived(1)
    first_steps(0, far, near)
    if half > 1:
        ring_arrived(2)
    first_steps(0, near, nz)
    if count > 1:
        first_steps(1, 0, far)
    for step in range(3, half + 1):
        ring_arrived(step)
    forward(0)
    if count > 1:
        turn_steps(1, far, nz)
    if count > 2:
        turn_steps(2, 0, nz)

    def wide(tile):
        return jnp.tile(tile.astype(jnp.float32), (1, keys // 128))

    def leaf(slot, start, size):
        source = xor(i_at, slot, ibits)
        value = jnp.dot(
            recv[slot, pl.ds(start, size), :],
            grads[source],
            preferred_element_type=jnp.float32,
        )
        return value, wide(limits[source])

    def out_copy(part, target):
        piece_at = pl.ds(parts[part][2], 16)
        return pltpu.make_async_remote_copy(
            src_ref=out_box.at[target, piece_at],
            dst_ref=in_box.at[o_at, piece_at],
            send_sem=out_send.at[part, target],
            recv_sem=out_recv.at[part, o_at],
            device_id=(i_at, target),
            device_id_type=MESH,
        )

    def out_arrival(part, source):
        piece_at = pl.ds(parts[part][2], 16)
        return pltpu.make_async_remote_copy(
            src_ref=in_box.at[source, piece_at],
            dst_ref=in_box.at[source, piece_at],
            send_sem=out_send.at[part, source],
            recv_sem=out_recv.at[part, source],
            device_id=(i_at, source),
            device_id_type=MESH,
        )

    quarter = ni // 4

    def arrived(part, n):
        @pl.when(n == 0)
        def _():
            local_copy(part).wait()

        @pl.when(n != 0)
        def _():
            block_arrival(part, n).wait_recv()

        for m in (1, 2, 3):
            slot = n + m * quarter
            if m * quarter != 2 * half:
                block_arrival(part, slot).wait_recv()
                continue

            @pl.when(n < 2)
            def _():
                for way in range(2):
                    hop2_arrival(part, way, n).wait_recv()

            @pl.when(n >= 2)
            def _():
                block_arrival(part, slot).wait_recv()

    def work(part):
        start, size, at, piece = parts[part]

        def group(n, carry):
            arrived(part, n)
            kept, _ = leaf(n, start, size)
            given, limit = leaf(n + 2 * quarter, start, size)
            first_sum = kept + clipped(given, limit[0:1])
            kept, limit_1 = leaf(n + quarter, start, size)
            given, limit = leaf(n + 3 * quarter, start, size)
            second_sum = kept + clipped(given, limit[0:1])
            sums[n, pl.ds(0, size), :] = first_sum + clipped(second_sum, limit_1[1:2])
            return carry

        lax.fori_loop(0, quarter, group, 0)
        level = 2
        width_now = quarter
        while width_now > 1:
            width_now //= 2
            for n in range(width_now):
                source = xor(i_at, n + width_now, ibits)
                limit = wide(limits[source])
                value = sums[n, pl.ds(0, size), :] + clipped(
                    sums[n + width_now, pl.ds(0, size), :], limit[level : level + 1]
                )
                if width_now == 1:
                    total[pl.ds(0, size), :] = value
                else:
                    sums[n, pl.ds(0, size), :] = value
            level += 1
        for owner in range(no):
            out_box[owner, pl.ds(at, 16), :] = total[pl.ds(owner * piece, 16), :].astype(
                jnp.bfloat16
            )
        for step in range(1, no):
            out_copy(part, lax.rem(o_at + step, no)).start()

    def finish(part):
        _, _, at, piece = parts[part]
        for step in range(1, no):
            out_arrival(part, lax.rem(o_at + step, no)).wait_recv()
        leaves = [out_box[o_at, pl.ds(at, 16), :].astype(jnp.float32)]
        caps = [None]
        for slot in range(1, no):
            source = xor(o_at, slot, obits)
            leaves.append(in_box[source, pl.ds(at, 16), :].astype(jnp.float32))
            caps.append(wide(limits_in[source]))
        many = no
        for hop in range(obits):
            many //= 2
            level = ibits + hop
            leaves = [
                leaves[n] + clipped(leaves[n + many], caps[n + many][level : level + 1])
                for n in range(many)
            ]
        out_ref[pl.ds(at, piece), :] = leaves[0][0:piece]

    def pieces_sent(part):
        for step in range(1, no):
            out_copy(part, lax.rem(o_at + step, no)).wait_send()

    def relays_sent(part):
        for way in range(2):
            for k in range(2):
                hop2(part, way, k).wait_send()

    for part in range(count):
        if part + 1 < count:
            next_steps(part + 1, far, nz, part, 0)
            forward(part + 1)
        if part + 2 < count:
            next_steps(part + 2, 0, far, part, nz - far)
        if part == 0:
            for offset in range(nz):
                wait_arrived(twin(offset, 1 - core))
            for step in range(1, no):
                limit_arrival(lax.rem(o_at + step, no)).wait_recv()
        if part + 1 == count:
            for way in range(2):
                for step in range(1, half + 1):
                    wait_sent(ring(way, step))
            for offset in range(nz):
                wait_sent(twin(offset, core))
            for step in range(1, no):
                limit_copy(lax.rem(o_at + step, no)).wait_send()
            if part > 0:
                wait_steps(part - 1, nz - far, nz)
            for early in range(part):
                relays_sent(early)
                pieces_sent(early)
            if part > 0:
                finish(part - 1)
        work(part)
        if 0 < part < count - 1:
            finish(part - 1)
        if part + 3 < count:
            turn_steps(part + 3, 0, nz)
    wait_steps(count - 1, 0, nz)
    relays_sent(count - 1)
    finish(count - 1)
    pieces_sent(count - 1)


def cut_parts(rows, no):
    return tuple(
        (no * at, no * min(16, rows - at), at, min(16, rows - at)) for at in range(0, rows, 16)
    )


def body(acts, key_grad, shifts):
    ni = lax.axis_size("inner")
    no = lax.axis_size("outer")
    tokens, width = acts.shape
    keys = key_grad.shape[1]
    block = width // ni
    rows = block // no
    nz = ni // 2
    half = nz // 2
    parts = cut_parts(rows, no)
    count = len(parts)
    widest = parts[0][1]
    span = max(
        round_up(block * (n + 1), 128) - block * n // 128 * 128 for n in range(ni)
    )
    padded = round_up(rows, 16)
    dma = pltpu.SemaphoreType.DMA
    return pl.pallas_call(
        functools.partial(kernel, ni, no, parts, span),
        out_shape=pltpu.VMEM((rows, keys), jnp.float32),
        in_specs=[
            pl.BlockSpec(memory_space=pl.ANY),
            pl.BlockSpec(memory_space=pl.ANY),
            pl.BlockSpec(memory_space=pl.ANY),
        ],
        out_specs=pl.BlockSpec(memory_space=pltpu.VMEM),
        scratch_shapes=[
            pltpu.VMEM((tokens, width), jnp.bfloat16),
            pltpu.VMEM((width, tokens), jnp.bfloat16),
            pltpu.VMEM((ni, block, tokens), jnp.bfloat16),
            pltpu.VMEM((2, block, tokens), jnp.bfloat16),
            pltpu.VMEM((ni, tokens, keys), jnp.bfloat16),
            pltpu.VMEM((ni, BOUND_ROWS, 128), jnp.bfloat16),
            pltpu.VMEM((ni // 4, widest, keys), jnp.float32),
            pltpu.VMEM((widest, keys), jnp.float32),
            pltpu.VMEM((widest, span), jnp.int32),
            pltpu.VMEM((parts[-1][1], span), jnp.int32),
            pltpu.VMEM((no, padded, keys), jnp.bfloat16),
            pltpu.VMEM((no, padded, keys), jnp.bfloat16),
            pltpu.VMEM((BOUND_ROWS, 128), jnp.bfloat16),
            pltpu.VMEM((no, BOUND_ROWS, 128), jnp.bfloat16),
            pltpu.SMEM(shifts.shape, jnp.int32),
            dma,
            dma((4,)),
            dma,
            dma((2, half)),
            dma((2, half)),
            dma((2, half)),
            dma((2, half)),
            dma((nz,)),
            dma((nz,)),
            dma((nz,)),
            dma((nz,)),
            dma((count, ni)),
            dma((count, ni)),
            dma((count, 2, 2)),
            dma((count, 2, 2)),
            dma((count, 2, 2)),
            dma((count, 2, 2)),
            dma((count,)),
            dma((count, no)),
            dma((count, no)),
            dma((no,)),
            dma((no,)),
        ],
        compiler_params=pltpu.CompilerParams(
            collective_id=0, has_side_effects=True, vmem_limit_bytes=56 * 1024 * 1024
        ),
        cost_estimate=pl.CostEstimate(
            flops=2 * tokens * width * keys, bytes_accessed=2 * tokens * width, transcendentals=0
        ),
    )(acts, key_grad, shifts)


def solution(mesh):
    return jax.shard_map(
        body,
        mesh=mesh,
        in_specs=(
            P(("inner", "outer"), None),
            P(("inner", "outer"), None),
            P(("inner", "outer"), None),
        ),
        out_specs=P(("inner", "outer"), None),
        check_vma=False,
    )
```

```python
import functools

import jax
import jax.numpy as jnp
from jax import lax
from jax.experimental import pallas as pl
from jax.experimental.pallas import tpu as pltpu
from jax.sharding import PartitionSpec as P

MESH = pl.DeviceIdType.MESH
BOUND_ROWS = 16


def xor(a, b, bits):
    total = 0
    for bit in range(bits):
        step = 1 << bit
        total = total + step * lax.rem(lax.div(a, step) + lax.div(b, step), 2)
    return total


def clipped(values, bound):
    return jnp.clip(values, -bound, bound)


def rounded(values, bound):
    return jnp.clip(values, -bound, bound).astype(jnp.bfloat16).astype(jnp.float32)


def aligned(index):
    return pl.multiple_of(index, 16)


def round_up(value, unit):
    return -(-value // unit) * unit


def kernel(
    ni,
    no,
    parts,
    span,
    acts_hbm,
    grad_hbm,
    shifts_hbm,
    out_ref,
    raw,
    acts_t,
    recv,
    relay,
    grads,
    limits,
    sums,
    total,
    place,
    place_last,
    out_box,
    in_box,
    limit_box,
    limits_in,
    shifts_smem,
    shift_sem,
    fetch_sem,
    grad_sem,
    ring_send,
    ring_recv,
    tile_send,
    tile_recv,
    twin_send,
    twin_recv,
    twin_tile_send,
    twin_tile_recv,
    block_send,
    block_recv,
    hop1_send,
    hop1_recv,
    hop2_send,
    hop2_recv,
    local_sem,
    out_send,
    out_recv,
    limit_send,
    limit_recv,
):
    tokens, width = raw.shape
    keys = grads.shape[2]
    block = width // ni
    rows = block // no
    nz = ni // 2
    half = nz // 2
    first = half // 2
    ibits = ni.bit_length() - 1
    obits = no.bit_length() - 1
    quarters = 4
    strip = width // quarters
    count = len(parts)

    i_at = lax.axis_index("inner")
    o_at = lax.axis_index("outer")
    z_at = lax.div(i_at, 2)
    core = lax.rem(i_at, 2)

    def z_off(step):
        return lax.rem(z_at + step + nz, nz)

    def at_inner(z, k):
        return (2 * z + k, o_at)

    def fetch(q):
        cols = pl.ds(q * strip, strip)
        return pltpu.make_async_copy(acts_hbm.at[:, cols], raw.at[:, cols], fetch_sem.at[q])

    shift_copy = pltpu.make_async_copy(shifts_hbm, shifts_smem, shift_sem)
    shift_copy.start()
    grad_copy = pltpu.make_async_copy(grad_hbm, grads.at[i_at, pl.ds(0, tokens)], grad_sem)
    grad_copy.start()
    for q in range(quarters):
        fetch(q).start()

    barrier = pltpu.get_barrier_semaphore()
    for step in range(1, ni):
        pl.semaphore_signal(
            barrier, inc=1, device_id=(lax.rem(i_at + step, ni), o_at), device_id_type=MESH
        )
    for step in range(1, no):
        pl.semaphore_signal(
            barrier, inc=1, device_id=(i_at, lax.rem(o_at + step, no)), device_id_type=MESH
        )

    row_at = lax.broadcasted_iota(jnp.int32, (BOUND_ROWS, 128), 0)
    left_shift = jnp.zeros((BOUND_ROWS, 128), jnp.int32)
    shift_copy.wait()
    for hop in range(ibits + obits):
        left_shift = jnp.where(row_at == hop, 12 - shifts_smem[0, hop], left_shift)
    own_limits = jnp.left_shift(jnp.ones_like(left_shift), left_shift).astype(jnp.float32) * 0.109375
    own_limits = own_limits.astype(jnp.bfloat16)
    limits[i_at, :, :] = own_limits
    limit_box[...] = own_limits

    def fill_place(ref, piece):
        size = ref.shape[0]
        row = lax.broadcasted_iota(jnp.int32, (size, 128), 0)
        lane = lax.broadcasted_iota(jnp.int32, (size, 128), 1)
        owner = lax.div(row, piece)
        offset = lane - (owner * rows + row - owner * piece)
        for n in range(span // 128):
            ref[:, pl.ds(n * 128, 128)] = offset + n * 128

    fill_place(place, parts[0][3])
    if place_last is not None:
        fill_place(place_last, parts[-1][3])

    grad_copy.wait()
    pl.semaphore_wait(barrier, ni + no - 2)

    cut = tokens // 2

    def ring(way, step):
        sign = 1 if way == 0 else -1
        source = 2 * z_off(sign * (1 - step)) + core
        target = at_inner(z_off(sign), core)
        if step < half:
            piece = grads.at[source]
        else:
            piece = grads.at[source, pl.ds(way * cut, cut)]
        copies = [
            pltpu.make_async_remote_copy(
                src_ref=piece,
                dst_ref=piece,
                send_sem=ring_send.at[way, step - 1],
                recv_sem=ring_recv.at[way, step - 1],
                device_id=target,
                device_id_type=MESH,
            )
        ]
        if step < half or way == 0:
            copies.append(
                pltpu.make_async_remote_copy(
                    src_ref=limits.at[source],
                    dst_ref=limits.at[source],
                    send_sem=tile_send.at[way, step - 1],
                    recv_sem=tile_recv.at[way, step - 1],
                    device_id=target,
                    device_id_type=MESH,
                )
            )
        return copies

    def twin(offset, side):
        source = 2 * z_off(offset) + side
        return [
            pltpu.make_async_remote_copy(
                src_ref=ref.at[source],
                dst_ref=ref.at[source],
                send_sem=send.at[offset % nz],
                recv_sem=recv_at.at[offset % nz],
                device_id=at_inner(z_at, 1 - core),
                device_id_type=MESH,
            )
            for ref, send, recv_at in (
                (grads, twin_send, twin_recv),
                (limits, twin_tile_send, twin_tile_recv),
            )
        ]

    def start_all(copies):
        for copy in copies:
            copy.start()

    def wait_sent(copies):
        for copy in copies:
            copy.wait_send()

    def wait_arrived(copies):
        for copy in copies:
            copy.wait_recv()

    def ring_arrived(step):
        wait_arrived(ring(0, step))
        wait_arrived(ring(1, step))
        if step < half:
            start_all(ring(0, step + 1))
            start_all(ring(1, step + 1))
            start_all(twin(-step, core))
            start_all(twin(step, core))
        else:
            start_all(twin(half, core))

    def limit_copy(target):
        return pltpu.make_async_remote_copy(
            src_ref=limit_box,
            dst_ref=limits_in.at[o_at],
            send_sem=limit_send.at[target],
            recv_sem=limit_recv.at[o_at],
            device_id=(i_at, target),
            device_id_type=MESH,
        )

    def limit_arrival(source):
        return pltpu.make_async_remote_copy(
            src_ref=limit_box,
            dst_ref=limits_in.at[source],
            send_sem=limit_send.at[source],
            recv_sem=limit_recv.at[source],
            device_id=(i_at, source),
            device_id_type=MESH,
        )

    def turn(part, target):
        start, size, at, piece = parts[part]
        column = target * block
        tile = lax.div(column, 128)
        source = place if piece == parts[0][3] else place_last
        pick = (source[...] == column - tile * 128 + at).astype(jnp.bfloat16)
        window = raw[:, pl.ds(pl.multiple_of(tile * 128, 128), span)]
        acts_t[pl.ds(aligned(column + start), size), :] = lax.dot_general(
            pick, window, (((1,), (1,)), ((), ())), preferred_element_type=jnp.float32
        ).astype(jnp.bfloat16)

    def block_copy(part, target):
        start, size = parts[part][:2]
        slot = xor(i_at, target, ibits)
        return pltpu.make_async_remote_copy(
            src_ref=acts_t.at[pl.ds(aligned(target * block + start), size)],
            dst_ref=recv.at[slot, pl.ds(start, size)],
            send_sem=block_send.at[part, slot],
            recv_sem=block_recv.at[part, slot],
            device_id=(target, o_at),
            device_id_type=MESH,
        )

    def halves(part):
        start, size = parts[part][:2]
        low = round_up(size // 2, 16)
        return ((start, low), (start + low, size - low))

    def hop1(part, way, k):
        start, size = halves(part)[way]
        sign = 1 if way == 0 else -1
        target = 2 * z_off(half) + k
        return pltpu.make_async_remote_copy(
            src_ref=acts_t.at[pl.ds(aligned(target * block + start), size)],
            dst_ref=relay.at[k, pl.ds(start, size)],
            send_sem=hop1_send.at[part, way, k],
            recv_sem=hop1_recv.at[part, way, k],
            device_id=at_inner(z_off(sign * first), core),
            device_id_type=MESH,
        )

    def hop2(part, way, k):
        start, size = halves(part)[way]
        sign = 1 if way == 0 else -1
        differ = lax.rem(core + k, 2)
        return pltpu.make_async_remote_copy(
            src_ref=relay.at[k, pl.ds(start, size)],
            dst_ref=recv.at[2 * half + differ, pl.ds(start, size)],
            send_sem=hop2_send.at[part, way, differ],
            recv_sem=hop2_recv.at[part, way, differ],
            device_id=at_inner(z_off(sign * (half - first)), k),
            device_id_type=MESH,
        )

    def hop2_arrival(part, way, differ):
        start, size = halves(part)[way]
        piece = recv.at[2 * half + differ, pl.ds(start, size)]
        return pltpu.make_async_remote_copy(
            src_ref=piece,
            dst_ref=piece,
            send_sem=hop2_send.at[part, way, differ],
            recv_sem=hop2_recv.at[part, way, differ],
            device_id=at_inner(z_off(half), core),
            device_id_type=MESH,
        )

    def block_arrival(part, slot):
        start, size = parts[part][:2]
        piece = recv.at[slot, pl.ds(start, size)]
        return pltpu.make_async_remote_copy(
            src_ref=piece,
            dst_ref=piece,
            send_sem=block_send.at[part, slot],
            recv_sem=block_recv.at[part, slot],
            device_id=at_inner(z_at, 1 - core),
            device_id_type=MESH,
        )

    def local_copy(part):
        start, size = parts[part][:2]
        return pltpu.make_async_copy(
            acts_t.at[pl.ds(aligned(i_at * block + start), size)],
            recv.at[0, pl.ds(start, size)],
            local_sem.at[part],
        )

    def z_of_step(step):
        odd = lax.rem(step, 2)
        return z_off((2 * odd - 1) * (1 - 2 * core) * (half - lax.div(step + odd, 2)))

    def by_step(part, step, act):
        z = z_of_step(step)

        @pl.when(step == 0)
        def _():
            for way in range(2):
                for k in range(2):
                    act(hop1(part, way, k))

        @pl.when(jnp.logical_and(step > 0, step < nz - 1))
        def _():
            for k in range(2):
                act(block_copy(part, 2 * z + k))

        @pl.when(step == nz - 1)
        def _():
            act(block_copy(part, 2 * z_at + 1 - core))

    def start(copy):
        copy.start()

    def leave(copy):
        copy.wait_send()

    def turn_steps(part, low, high):
        def one(step, carry):
            z = z_of_step(step)
            for k in range(2):
                turn(part, 2 * z + k)
            return carry

        lax.fori_loop(low, high, one, 0)
        if high == nz:
            local_copy(part).start()

    def first_steps(part, low, high):
        def one(step, carry):
            z = z_of_step(step)
            for k in range(2):
                turn(part, 2 * z + k)
            by_step(part, step, start)
            return carry

        lax.fori_loop(low, high, one, 0)
        if high == nz:
            local_copy(part).start()

    def wait_steps(part, low, high):
        def one(step, carry):
            by_step(part, step, leave)
            return carry

        lax.fori_loop(low, high, one, 0)

    def next_steps(part, low, high, part_before, low_before):
        def one(step, carry):
            by_step(part_before, step - low + low_before, leave)
            by_step(part, step, start)
            return carry

        lax.fori_loop(low, high, one, 0)

    def forward(part):
        for way in range(2):
            for k in range(2):
                hop1(part, way, k).wait_recv()
                hop2(part, way, k).start()

    start_all(ring(0, 1))
    start_all(ring(1, 1))
    start_all(twin(0, core))
    for step in range(1, no):
        limit_copy(lax.rem(o_at + step, no)).start()
    for q in range(quarters):
        fetch(q).wait()
    far = min(3, nz)
    near = min(5, nz)
    first_steps(0, 0, far)
    ring_arrived(1)
    first_steps(0, far, near)
    if half > 1:
        ring_arrived(2)
    first_steps(0, near, nz)
    if count > 1:
        first_steps(1, 0, far)
    if half > 2:
        ring_arrived(3)
    if count > 1:
        first_steps(1, far, nz)
    for step in range(4, half + 1):
        ring_arrived(step)
    forward(0)
    if count > 2:
        first_steps(2, 0, far)
    if count > 1:
        forward(1)
    if count > 2:
        turn_steps(2, far, nz)
    for part in range(3, count):
        turn_steps(part, 0, nz)

    def wide(tile):
        return jnp.tile(tile.astype(jnp.float32), (1, keys // 128))

    def leaf(slot, start, size):
        source = xor(i_at, slot, ibits)
        value = jnp.dot(
            recv[slot, pl.ds(start, size), :],
            grads[source],
            preferred_element_type=jnp.float32,
        )
        return value, wide(limits[source])

    def out_copy(part, target):
        piece_at = pl.ds(parts[part][2], 16)
        return pltpu.make_async_remote_copy(
            src_ref=out_box.at[target, piece_at],
            dst_ref=in_box.at[o_at, piece_at],
            send_sem=out_send.at[part, target],
            recv_sem=out_recv.at[part, o_at],
            device_id=(i_at, target),
            device_id_type=MESH,
        )

    def out_arrival(part, source):
        piece_at = pl.ds(parts[part][2], 16)
        return pltpu.make_async_remote_copy(
            src_ref=in_box.at[source, piece_at],
            dst_ref=in_box.at[source, piece_at],
            send_sem=out_send.at[part, source],
            recv_sem=out_recv.at[part, source],
            device_id=(i_at, source),
            device_id_type=MESH,
        )

    quarter = ni // 4

    def arrived(part, n):
        @pl.when(n == 0)
        def _():
            local_copy(part).wait()

        @pl.when(n != 0)
        def _():
            block_arrival(part, n).wait_recv()

        for m in (1, 2, 3):
            slot = n + m * quarter
            if m * quarter != 2 * half:
                block_arrival(part, slot).wait_recv()
                continue

            @pl.when(n < 2)
            def _():
                for way in range(2):
                    hop2_arrival(part, way, n).wait_recv()

            @pl.when(n >= 2)
            def _():
                block_arrival(part, slot).wait_recv()

    def work(part):
        start, size, at, piece = parts[part]

        def group(n, carry):
            arrived(part, n)
            kept, _ = leaf(n, start, size)
            given, limit = leaf(n + 2 * quarter, start, size)
            first_sum = kept + clipped(given, limit[0:1])
            kept, limit_1 = leaf(n + quarter, start, size)
            given, limit = leaf(n + 3 * quarter, start, size)
            second_sum = kept + clipped(given, limit[0:1])
            sums[n, pl.ds(0, size), :] = first_sum + clipped(second_sum, limit_1[1:2])
            return carry

        lax.fori_loop(0, quarter, group, 0)
        level = 2
        width_now = quarter
        while width_now > 1:
            width_now //= 2
            for n in range(width_now):
                source = xor(i_at, n + width_now, ibits)
                limit = wide(limits[source])
                value = sums[n, pl.ds(0, size), :] + clipped(
                    sums[n + width_now, pl.ds(0, size), :], limit[level : level + 1]
                )
                if width_now == 1:
                    total[pl.ds(0, size), :] = value
                else:
                    sums[n, pl.ds(0, size), :] = value
            level += 1
        for owner in range(no):
            out_box[owner, pl.ds(at, 16), :] = total[pl.ds(owner * piece, 16), :].astype(
                jnp.bfloat16
            )
        for step in range(1, no):
            out_copy(part, lax.rem(o_at + step, no)).start()

    def finish(part):
        _, _, at, piece = parts[part]
        for step in range(1, no):
            out_arrival(part, lax.rem(o_at + step, no)).wait_recv()
        leaves = [out_box[o_at, pl.ds(at, 16), :].astype(jnp.float32)]
        caps = [None]
        for slot in range(1, no):
            source = xor(o_at, slot, obits)
            leaves.append(in_box[source, pl.ds(at, 16), :].astype(jnp.float32))
            caps.append(wide(limits_in[source]))
        many = no
        for hop in range(obits):
            many //= 2
            level = ibits + hop
            leaves = [
                leaves[n] + rounded(leaves[n + many], caps[n + many][level : level + 1])
                for n in range(many)
            ]
        out_ref[pl.ds(at, piece), :] = leaves[0][0:piece]

    def pieces_sent(part):
        for step in range(1, no):
            out_copy(part, lax.rem(o_at + step, no)).wait_send()

    def relays_sent(part):
        for way in range(2):
            for k in range(2):
                hop2(part, way, k).wait_send()

    for part in range(count):
        if part + 2 < count:
            next_steps(part + 2, far, nz, part, 0)
            forward(part + 2)
        if part + 3 < count:
            next_steps(part + 3, 0, far, part, nz - far)
        if part == 0:
            for offset in range(nz):
                wait_arrived(twin(offset, 1 - core))
            for step in range(1, no):
                limit_arrival(lax.rem(o_at + step, no)).wait_recv()
        if part + 1 == count:
            for way in range(2):
                for step in range(1, half + 1):
                    wait_sent(ring(way, step))
            for offset in range(nz):
                wait_sent(twin(offset, core))
            for step in range(1, no):
                limit_copy(lax.rem(o_at + step, no)).wait_send()
            if part > 1:
                wait_steps(part - 2, nz - far, nz)
            if part > 0:
                wait_steps(part - 1, 0, nz)
            for early in range(part):
                relays_sent(early)
                pieces_sent(early)
            if part > 0:
                finish(part - 1)
        work(part)
        if 0 < part < count - 1:
            finish(part - 1)
    wait_steps(count - 1, 0, nz)
    relays_sent(count - 1)
    finish(count - 1)
    pieces_sent(count - 1)


def cut_parts(rows, no):
    return tuple(
        (no * at, no * min(16, rows - at), at, min(16, rows - at)) for at in range(0, rows, 16)
    )


def body(acts, key_grad, shifts):
    ni = lax.axis_size("inner")
    no = lax.axis_size("outer")
    tokens, width = acts.shape
    keys = key_grad.shape[1]
    block = width // ni
    rows = block // no
    nz = ni // 2
    half = nz // 2
    parts = cut_parts(rows, no)
    count = len(parts)
    widest = parts[0][1]
    span = max(
        round_up(block * (n + 1), 128) - block * n // 128 * 128 for n in range(ni)
    )
    padded = round_up(rows, 16)
    dma = pltpu.SemaphoreType.DMA
    return pl.pallas_call(
        functools.partial(kernel, ni, no, parts, span),
        out_shape=pltpu.VMEM((rows, keys), jnp.float32),
        in_specs=[
            pl.BlockSpec(memory_space=pl.ANY),
            pl.BlockSpec(memory_space=pl.ANY),
            pl.BlockSpec(memory_space=pl.ANY),
        ],
        out_specs=pl.BlockSpec(memory_space=pltpu.VMEM),
        scratch_shapes=[
            pltpu.VMEM((tokens, width), jnp.bfloat16),
            pltpu.VMEM((width, tokens), jnp.bfloat16),
            pltpu.VMEM((ni, block, tokens), jnp.bfloat16),
            pltpu.VMEM((2, block, tokens), jnp.bfloat16),
            pltpu.VMEM((ni, tokens, keys), jnp.bfloat16),
            pltpu.VMEM((ni, BOUND_ROWS, 128), jnp.bfloat16),
            pltpu.VMEM((ni // 4, widest, keys), jnp.float32),
            pltpu.VMEM((widest, keys), jnp.float32),
            pltpu.VMEM((widest, span), jnp.int32),
            pltpu.VMEM((parts[-1][1], span), jnp.int32),
            pltpu.VMEM((no, padded, keys), jnp.bfloat16),
            pltpu.VMEM((no, padded, keys), jnp.bfloat16),
            pltpu.VMEM((BOUND_ROWS, 128), jnp.bfloat16),
            pltpu.VMEM((no, BOUND_ROWS, 128), jnp.bfloat16),
            pltpu.SMEM(shifts.shape, jnp.int32),
            dma,
            dma((4,)),
            dma,
            dma((2, half)),
            dma((2, half)),
            dma((2, half)),
            dma((2, half)),
            dma((nz,)),
            dma((nz,)),
            dma((nz,)),
            dma((nz,)),
            dma((count, ni)),
            dma((count, ni)),
            dma((count, 2, 2)),
            dma((count, 2, 2)),
            dma((count, 2, 2)),
            dma((count, 2, 2)),
            dma((count,)),
            dma((count, no)),
            dma((count, no)),
            dma((no,)),
            dma((no,)),
        ],
        compiler_params=pltpu.CompilerParams(
            collective_id=0, has_side_effects=True, vmem_limit_bytes=56 * 1024 * 1024
        ),
        cost_estimate=pl.CostEstimate(
            flops=2 * tokens * width * keys, bytes_accessed=2 * tokens * width, transcendentals=0
        ),
    )(acts, key_grad, shifts)


def solution(mesh):
    return jax.shard_map(
        body,
        mesh=mesh,
        in_specs=(
            P(("inner", "outer"), None),
            P(("inner", "outer"), None),
            P(("inner", "outer"), None),
        ),
        out_specs=P(("inner", "outer"), None),
        check_vma=False,
    )
```

```python
import functools

import jax
import jax.numpy as jnp
from jax import lax
from jax.experimental import pallas as pl
from jax.experimental.pallas import tpu as pltpu
from jax.sharding import PartitionSpec as P

MESH = pl.DeviceIdType.MESH
BOUND_ROWS = 16


def xor(a, b, bits):
    total = 0
    for bit in range(bits):
        step = 1 << bit
        total = total + step * lax.rem(lax.div(a, step) + lax.div(b, step), 2)
    return total


def clipped(values, bound):
    return jnp.clip(values, -bound, bound).astype(jnp.bfloat16).astype(jnp.float32)


def aligned(index):
    return pl.multiple_of(index, 16)


def round_up(value, unit):
    return -(-value // unit) * unit


def kernel(
    ni,
    no,
    parts,
    span,
    acts_hbm,
    grad_hbm,
    shifts_hbm,
    out_ref,
    raw,
    acts_t,
    recv,
    relay,
    grads,
    limits,
    sums,
    total,
    place,
    place_last,
    out_box,
    in_box,
    limit_box,
    limits_in,
    shifts_smem,
    shift_sem,
    fetch_sem,
    grad_sem,
    ring_send,
    ring_recv,
    tile_send,
    tile_recv,
    twin_send,
    twin_recv,
    twin_tile_send,
    twin_tile_recv,
    block_send,
    block_recv,
    hop1_send,
    hop1_recv,
    hop2_send,
    hop2_recv,
    local_sem,
    out_send,
    out_recv,
    limit_send,
    limit_recv,
):
    tokens, width = raw.shape
    keys = grads.shape[2]
    block = width // ni
    rows = block // no
    nz = ni // 2
    half = nz // 2
    first = half // 2
    ibits = ni.bit_length() - 1
    obits = no.bit_length() - 1
    quarters = 4
    strip = width // quarters
    count = len(parts)

    i_at = lax.axis_index("inner")
    o_at = lax.axis_index("outer")
    z_at = lax.div(i_at, 2)
    core = lax.rem(i_at, 2)

    def z_off(step):
        return lax.rem(z_at + step + nz, nz)

    def at_inner(z, k):
        return (2 * z + k, o_at)

    def fetch(q):
        cols = pl.ds(q * strip, strip)
        return pltpu.make_async_copy(acts_hbm.at[:, cols], raw.at[:, cols], fetch_sem.at[q])

    shift_copy = pltpu.make_async_copy(shifts_hbm, shifts_smem, shift_sem)
    shift_copy.start()
    grad_copy = pltpu.make_async_copy(grad_hbm, grads.at[i_at, pl.ds(0, tokens)], grad_sem)
    grad_copy.start()
    for q in range(quarters):
        fetch(q).start()

    barrier = pltpu.get_barrier_semaphore()
    for step in range(1, ni):
        pl.semaphore_signal(
            barrier, inc=1, device_id=(lax.rem(i_at + step, ni), o_at), device_id_type=MESH
        )
    for step in range(1, no):
        pl.semaphore_signal(
            barrier, inc=1, device_id=(i_at, lax.rem(o_at + step, no)), device_id_type=MESH
        )

    row_at = lax.broadcasted_iota(jnp.int32, (BOUND_ROWS, 128), 0)
    left_shift = jnp.zeros((BOUND_ROWS, 128), jnp.int32)
    shift_copy.wait()
    for hop in range(ibits + obits):
        left_shift = jnp.where(row_at == hop, 12 - shifts_smem[0, hop], left_shift)
    own_limits = jnp.left_shift(jnp.ones_like(left_shift), left_shift).astype(jnp.float32) * 0.109375
    own_limits = own_limits.astype(jnp.bfloat16)
    limits[i_at, :, :] = own_limits
    limit_box[...] = own_limits

    def fill_place(ref, piece):
        size = ref.shape[0]
        row = lax.broadcasted_iota(jnp.int32, (size, 128), 0)
        lane = lax.broadcasted_iota(jnp.int32, (size, 128), 1)
        owner = lax.div(row, piece)
        offset = lane - (owner * rows + row - owner * piece)
        for n in range(span // 128):
            ref[:, pl.ds(n * 128, 128)] = offset + n * 128

    fill_place(place, parts[0][3])
    if place_last is not None:
        fill_place(place_last, parts[-1][3])

    grad_copy.wait()
    pl.semaphore_wait(barrier, ni + no - 2)

    cut = tokens // 2

    def ring(way, step):
        sign = 1 if way == 0 else -1
        source = 2 * z_off(sign * (1 - step)) + core
        target = at_inner(z_off(sign), core)
        pieces = (0, 1) if step < half else (way,)
        copies = []
        for n in pieces:
            piece = grads.at[source, pl.ds(n * cut, cut)]
            copies.append(
                pltpu.make_async_remote_copy(
                    src_ref=piece,
                    dst_ref=piece,
                    send_sem=ring_send.at[way, step - 1, n],
                    recv_sem=ring_recv.at[way, step - 1, n],
                    device_id=target,
                    device_id_type=MESH,
                )
            )
        if step < half or way == 0:
            copies.append(
                pltpu.make_async_remote_copy(
                    src_ref=limits.at[source],
                    dst_ref=limits.at[source],
                    send_sem=tile_send.at[way, step - 1],
                    recv_sem=tile_recv.at[way, step - 1],
                    device_id=target,
                    device_id_type=MESH,
                )
            )
        return copies

    def twin(offset, side):
        source = 2 * z_off(offset) + side
        return [
            pltpu.make_async_remote_copy(
                src_ref=ref.at[source],
                dst_ref=ref.at[source],
                send_sem=send.at[offset % nz],
                recv_sem=recv_at.at[offset % nz],
                device_id=at_inner(z_at, 1 - core),
                device_id_type=MESH,
            )
            for ref, send, recv_at in (
                (grads, twin_send, twin_recv),
                (limits, twin_tile_send, twin_tile_recv),
            )
        ]

    def start_all(copies):
        for copy in copies:
            copy.start()

    def wait_sent(copies):
        for copy in copies:
            copy.wait_send()

    def wait_arrived(copies):
        for copy in copies:
            copy.wait_recv()

    def ring_arrived(step):
        wait_arrived(ring(0, step))
        wait_arrived(ring(1, step))
        if step < half:
            start_all(ring(0, step + 1))
            start_all(ring(1, step + 1))
            start_all(twin(-step, core))
            start_all(twin(step, core))
        else:
            start_all(twin(half, core))

    def limit_copy(target):
        return pltpu.make_async_remote_copy(
            src_ref=limit_box,
            dst_ref=limits_in.at[o_at],
            send_sem=limit_send.at[target],
            recv_sem=limit_recv.at[o_at],
            device_id=(i_at, target),
            device_id_type=MESH,
        )

    def limit_arrival(source):
        return pltpu.make_async_remote_copy(
            src_ref=limit_box,
            dst_ref=limits_in.at[source],
            send_sem=limit_send.at[source],
            recv_sem=limit_recv.at[source],
            device_id=(i_at, source),
            device_id_type=MESH,
        )

    def turn(part, target):
        start, size, at, piece = parts[part]
        column = target * block
        tile = lax.div(column, 128)
        source = place if piece == parts[0][3] else place_last
        pick = (source[...] == column - tile * 128 + at).astype(jnp.bfloat16)
        window = raw[:, pl.ds(pl.multiple_of(tile * 128, 128), span)]
        acts_t[pl.ds(aligned(column + start), size), :] = lax.dot_general(
            pick, window, (((1,), (1,)), ((), ())), preferred_element_type=jnp.float32
        ).astype(jnp.bfloat16)

    def block_copy(part, target):
        start, size = parts[part][:2]
        slot = xor(i_at, target, ibits)
        return pltpu.make_async_remote_copy(
            src_ref=acts_t.at[pl.ds(aligned(target * block + start), size)],
            dst_ref=recv.at[slot, pl.ds(start, size)],
            send_sem=block_send.at[part, slot],
            recv_sem=block_recv.at[part, slot],
            device_id=(target, o_at),
            device_id_type=MESH,
        )

    def halves(part):
        start, size = parts[part][:2]
        low = round_up(size // 2, 16)
        return ((start, low), (start + low, size - low))

    def hop1(part, way, k):
        start, size = halves(part)[way]
        sign = 1 if way == 0 else -1
        target = 2 * z_off(half) + k
        return pltpu.make_async_remote_copy(
            src_ref=acts_t.at[pl.ds(aligned(target * block + start), size)],
            dst_ref=relay.at[k, pl.ds(start, size)],
            send_sem=hop1_send.at[part, way, k],
            recv_sem=hop1_recv.at[part, way, k],
            device_id=at_inner(z_off(sign * first), core),
            device_id_type=MESH,
        )

    def hop2(part, way, k):
        start, size = halves(part)[way]
        sign = 1 if way == 0 else -1
        differ = lax.rem(core + k, 2)
        return pltpu.make_async_remote_copy(
            src_ref=relay.at[k, pl.ds(start, size)],
            dst_ref=recv.at[2 * half + differ, pl.ds(start, size)],
            send_sem=hop2_send.at[part, way, differ],
            recv_sem=hop2_recv.at[part, way, differ],
            device_id=at_inner(z_off(sign * (half - first)), k),
            device_id_type=MESH,
        )

    def hop2_arrival(part, way, differ):
        start, size = halves(part)[way]
        piece = recv.at[2 * half + differ, pl.ds(start, size)]
        return pltpu.make_async_remote_copy(
            src_ref=piece,
            dst_ref=piece,
            send_sem=hop2_send.at[part, way, differ],
            recv_sem=hop2_recv.at[part, way, differ],
            device_id=at_inner(z_off(half), core),
            device_id_type=MESH,
        )

    def block_arrival(part, slot):
        start, size = parts[part][:2]
        piece = recv.at[slot, pl.ds(start, size)]
        return pltpu.make_async_remote_copy(
            src_ref=piece,
            dst_ref=piece,
            send_sem=block_send.at[part, slot],
            recv_sem=block_recv.at[part, slot],
            device_id=at_inner(z_at, 1 - core),
            device_id_type=MESH,
        )

    def local_copy(part):
        start, size = parts[part][:2]
        return pltpu.make_async_copy(
            acts_t.at[pl.ds(aligned(i_at * block + start), size)],
            recv.at[0, pl.ds(start, size)],
            local_sem.at[part],
        )

    def z_of_step(step):
        odd = lax.rem(step, 2)
        return z_off((2 * odd - 1) * (1 - 2 * core) * (half - lax.div(step + odd, 2)))

    def by_step(part, step, act):
        z = z_of_step(step)

        @pl.when(step == 0)
        def _():
            for way in range(2):
                for k in range(2):
                    act(hop1(part, way, k))

        @pl.when(jnp.logical_and(step > 0, step < nz - 1))
        def _():
            for k in range(2):
                act(block_copy(part, 2 * z + k))

        @pl.when(step == nz - 1)
        def _():
            act(block_copy(part, 2 * z_at + 1 - core))

    def start(copy):
        copy.start()

    def leave(copy):
        copy.wait_send()

    def turn_steps(part, low, high):
        def one(step, carry):
            z = z_of_step(step)
            for k in range(2):
                turn(part, 2 * z + k)
            return carry

        lax.fori_loop(low, high, one, 0)
        if high == nz:
            local_copy(part).start()

    def first_steps(part, low, high):
        def one(step, carry):
            z = z_of_step(step)
            for k in range(2):
                turn(part, 2 * z + k)
            by_step(part, step, start)
            return carry

        lax.fori_loop(low, high, one, 0)
        if high == nz:
            local_copy(part).start()

    def wait_steps(part, low, high):
        def one(step, carry):
            by_step(part, step, leave)
            return carry

        lax.fori_loop(low, high, one, 0)

    def next_steps(part, low, high, part_before, low_before):
        def one(step, carry):
            by_step(part_before, step - low + low_before, leave)
            by_step(part, step, start)
            return carry

        lax.fori_loop(low, high, one, 0)

    def forward(part):
        for way in range(2):
            for k in range(2):
                hop1(part, way, k).wait_recv()
                hop2(part, way, k).start()

    start_all(ring(0, 1))
    start_all(ring(1, 1))
    start_all(twin(0, core))
    for step in range(1, no):
        limit_copy(lax.rem(o_at + step, no)).start()
    for q in range(quarters):
        fetch(q).wait()
    far = min(3, nz)
    first_steps(0, 0, nz)
    ring_arrived(1)
    forward(0)
    if count > 1:
        first_steps(1, 0, far)
    if half > 1:
        ring_arrived(2)
    if count > 1:
        first_steps(1, far, nz)
    if half > 2:
        ring_arrived(3)
    if count > 1:
        forward(1)
    if count > 2:
        first_steps(2, 0, far)
    for step in range(4, half + 1):
        ring_arrived(step)
    if count > 2:
        turn_steps(2, far, nz)
    for part in range(3, count):
        turn_steps(part, 0, nz)

    def wide(tile):
        return jnp.tile(tile.astype(jnp.float32), (1, keys // 128))

    def leaf(slot, start, size):
        source = xor(i_at, slot, ibits)
        value = jnp.dot(
            recv[slot, pl.ds(start, size), :],
            grads[source],
            preferred_element_type=jnp.float32,
        )
        return value, wide(limits[source])

    def out_copy(part, target):
        piece_at = pl.ds(parts[part][2], 16)
        return pltpu.make_async_remote_copy(
            src_ref=out_box.at[target, piece_at],
            dst_ref=in_box.at[o_at, piece_at],
            send_sem=out_send.at[part, target],
            recv_sem=out_recv.at[part, o_at],
            device_id=(i_at, target),
            device_id_type=MESH,
        )

    def out_arrival(part, source):
        piece_at = pl.ds(parts[part][2], 16)
        return pltpu.make_async_remote_copy(
            src_ref=in_box.at[source, piece_at],
            dst_ref=in_box.at[source, piece_at],
            send_sem=out_send.at[part, source],
            recv_sem=out_recv.at[part, source],
            device_id=(i_at, source),
            device_id_type=MESH,
        )

    quarter = ni // 4

    def arrived(part, n):
        @pl.when(n == 0)
        def _():
            local_copy(part).wait()

        @pl.when(n != 0)
        def _():
            block_arrival(part, n).wait_recv()

        for m in (1, 2, 3):
            slot = n + m * quarter
            if m * quarter != 2 * half:
                block_arrival(part, slot).wait_recv()
                continue

            @pl.when(n < 2)
            def _():
                for way in range(2):
                    hop2_arrival(part, way, n).wait_recv()

            @pl.when(n >= 2)
            def _():
                block_arrival(part, slot).wait_recv()

    def work(part):
        start, size, at, piece = parts[part]

        def group(n, carry):
            arrived(part, n)
            kept, _ = leaf(n, start, size)
            given, limit = leaf(n + 2 * quarter, start, size)
            first_sum = kept + clipped(given, limit[0:1])
            kept, limit_1 = leaf(n + quarter, start, size)
            given, limit = leaf(n + 3 * quarter, start, size)
            second_sum = kept + clipped(given, limit[0:1])
            sums[n, pl.ds(0, size), :] = first_sum + clipped(second_sum, limit_1[1:2])
            return carry

        lax.fori_loop(0, quarter, group, 0)
        level = 2
        width_now = quarter
        while width_now > 1:
            width_now //= 2
            for n in range(width_now):
                source = xor(i_at, n + width_now, ibits)
                limit = wide(limits[source])
                value = sums[n, pl.ds(0, size), :] + clipped(
                    sums[n + width_now, pl.ds(0, size), :], limit[level : level + 1]
                )
                if width_now == 1:
                    total[pl.ds(0, size), :] = value
                else:
                    sums[n, pl.ds(0, size), :] = value
            level += 1
        for owner in range(no):
            out_box[owner, pl.ds(at, 16), :] = total[pl.ds(owner * piece, 16), :].astype(
                jnp.bfloat16
            )
        for step in range(1, no):
            out_copy(part, lax.rem(o_at + step, no)).start()

    def finish(part):
        _, _, at, piece = parts[part]
        for step in range(1, no):
            out_arrival(part, lax.rem(o_at + step, no)).wait_recv()
        leaves = [out_box[o_at, pl.ds(at, 16), :].astype(jnp.float32)]
        caps = [None]
        for slot in range(1, no):
            source = xor(o_at, slot, obits)
            leaves.append(in_box[source, pl.ds(at, 16), :].astype(jnp.float32))
            caps.append(wide(limits_in[source]))
        many = no
        for hop in range(obits):
            many //= 2
            level = ibits + hop
            leaves = [
                leaves[n] + clipped(leaves[n + many], caps[n + many][level : level + 1])
                for n in range(many)
            ]
        out_ref[pl.ds(at, piece), :] = leaves[0][0:piece]

    def pieces_sent(part):
        for step in range(1, no):
            out_copy(part, lax.rem(o_at + step, no)).wait_send()

    def relays_sent(part):
        for way in range(2):
            for k in range(2):
                hop2(part, way, k).wait_send()

    for part in range(count):
        if part + 2 < count:
            next_steps(part + 2, far, nz, part, 0)
            forward(part + 2)
        if part + 3 < count:
            next_steps(part + 3, 0, far, part, nz - far)
        if part == 0:
            for offset in range(nz):
                wait_arrived(twin(offset, 1 - core))
            for step in range(1, no):
                limit_arrival(lax.rem(o_at + step, no)).wait_recv()
        if part + 1 == count:
            for way in range(2):
                for step in range(1, half + 1):
                    wait_sent(ring(way, step))
            for offset in range(nz):
                wait_sent(twin(offset, core))
            for step in range(1, no):
                limit_copy(lax.rem(o_at + step, no)).wait_send()
            if part > 1:
                wait_steps(part - 2, nz - far, nz)
            if part > 0:
                wait_steps(part - 1, 0, nz)
            for early in range(part):
                relays_sent(early)
                pieces_sent(early)
            if part > 0:
                finish(part - 1)
        work(part)
        if 0 < part < count - 1:
            finish(part - 1)
    wait_steps(count - 1, 0, nz)
    relays_sent(count - 1)
    finish(count - 1)
    pieces_sent(count - 1)


def cut_parts(rows, no):
    return tuple(
        (no * at, no * min(16, rows - at), at, min(16, rows - at)) for at in range(0, rows, 16)
    )


def body(acts, key_grad, shifts):
    ni = lax.axis_size("inner")
    no = lax.axis_size("outer")
    tokens, width = acts.shape
    keys = key_grad.shape[1]
    block = width // ni
    rows = block // no
    nz = ni // 2
    half = nz // 2
    parts = cut_parts(rows, no)
    count = len(parts)
    widest = parts[0][1]
    span = max(
        round_up(block * (n + 1), 128) - block * n // 128 * 128 for n in range(ni)
    )
    padded = round_up(rows, 16)
    dma = pltpu.SemaphoreType.DMA
    return pl.pallas_call(
        functools.partial(kernel, ni, no, parts, span),
        out_shape=pltpu.VMEM((rows, keys), jnp.float32),
        in_specs=[
            pl.BlockSpec(memory_space=pl.ANY),
            pl.BlockSpec(memory_space=pl.ANY),
            pl.BlockSpec(memory_space=pl.ANY),
        ],
        out_specs=pl.BlockSpec(memory_space=pltpu.VMEM),
        scratch_shapes=[
            pltpu.VMEM((tokens, width), jnp.bfloat16),
            pltpu.VMEM((width, tokens), jnp.bfloat16),
            pltpu.VMEM((ni, block, tokens), jnp.bfloat16),
            pltpu.VMEM((2, block, tokens), jnp.bfloat16),
            pltpu.VMEM((ni, tokens, keys), jnp.bfloat16),
            pltpu.VMEM((ni, BOUND_ROWS, 128), jnp.bfloat16),
            pltpu.VMEM((ni // 4, widest, keys), jnp.float32),
            pltpu.VMEM((widest, keys), jnp.float32),
            pltpu.VMEM((widest, span), jnp.int32),
            pltpu.VMEM((parts[-1][1], span), jnp.int32),
            pltpu.VMEM((no, padded, keys), jnp.bfloat16),
            pltpu.VMEM((no, padded, keys), jnp.bfloat16),
            pltpu.VMEM((BOUND_ROWS, 128), jnp.bfloat16),
            pltpu.VMEM((no, BOUND_ROWS, 128), jnp.bfloat16),
            pltpu.SMEM(shifts.shape, jnp.int32),
            dma,
            dma((4,)),
            dma,
            dma((2, half, 2)),
            dma((2, half, 2)),
            dma((2, half)),
            dma((2, half)),
            dma((nz,)),
            dma((nz,)),
            dma((nz,)),
            dma((nz,)),
            dma((count, ni)),
            dma((count, ni)),
            dma((count, 2, 2)),
            dma((count, 2, 2)),
            dma((count, 2, 2)),
            dma((count, 2, 2)),
            dma((count,)),
            dma((count, no)),
            dma((count, no)),
            dma((no,)),
            dma((no,)),
        ],
        compiler_params=pltpu.CompilerParams(
            collective_id=0, has_side_effects=True, vmem_limit_bytes=56 * 1024 * 1024
        ),
        cost_estimate=pl.CostEstimate(
            flops=2 * tokens * width * keys, bytes_accessed=2 * tokens * width, transcendentals=0
        ),
    )(acts, key_grad, shifts)


def solution(mesh):
    return jax.shard_map(
        body,
        mesh=mesh,
        in_specs=(
            P(("inner", "outer"), None),
            P(("inner", "outer"), None),
            P(("inner", "outer"), None),
        ),
        out_specs=P(("inner", "outer"), None),
        check_vma=False,
    )
```

```python
import functools

import jax
import jax.numpy as jnp
from jax import lax
from jax.experimental import pallas as pl
from jax.experimental.pallas import tpu as pltpu
from jax.sharding import PartitionSpec as P

MESH = pl.DeviceIdType.MESH
BOUND_ROWS = 16


def xor(a, b, bits):
    total = 0
    for bit in range(bits):
        step = 1 << bit
        total = total + step * lax.rem(lax.div(a, step) + lax.div(b, step), 2)
    return total


def clipped(values, bound):
    return jnp.clip(values, -bound, bound).astype(jnp.bfloat16).astype(jnp.float32)


def aligned(index):
    return pl.multiple_of(index, 16)


def round_up(value, unit):
    return -(-value // unit) * unit


def kernel(
    ni,
    no,
    parts,
    span,
    acts_hbm,
    grad_hbm,
    shifts_hbm,
    out_ref,
    raw,
    acts_t,
    recv,
    relay,
    grads,
    limits,
    sums,
    total,
    place,
    place_last,
    out_box,
    in_box,
    limit_box,
    limits_in,
    shifts_smem,
    shift_sem,
    fetch_sem,
    grad_sem,
    ring_send,
    ring_recv,
    tile_send,
    tile_recv,
    twin_send,
    twin_recv,
    twin_tile_send,
    twin_tile_recv,
    block_send,
    block_recv,
    hop1_send,
    hop1_recv,
    hop2_send,
    hop2_recv,
    local_sem,
    out_send,
    out_recv,
    limit_send,
    limit_recv,
):
    tokens, width = raw.shape
    keys = grads.shape[2]
    block = width // ni
    rows = block // no
    nz = ni // 2
    half = nz // 2
    first = half // 2
    ibits = ni.bit_length() - 1
    obits = no.bit_length() - 1
    quarters = 4
    strip = width // quarters
    count = len(parts)

    i_at = lax.axis_index("inner")
    o_at = lax.axis_index("outer")
    z_at = lax.div(i_at, 2)
    core = lax.rem(i_at, 2)

    def z_off(step):
        return lax.rem(z_at + step + nz, nz)

    def at_inner(z, k):
        return (2 * z + k, o_at)

    def fetch(q):
        cols = pl.ds(q * strip, strip)
        return pltpu.make_async_copy(acts_hbm.at[:, cols], raw.at[:, cols], fetch_sem.at[q])

    shift_copy = pltpu.make_async_copy(shifts_hbm, shifts_smem, shift_sem)
    shift_copy.start()
    grad_copy = pltpu.make_async_copy(grad_hbm, grads.at[i_at, pl.ds(0, tokens)], grad_sem)
    grad_copy.start()
    for q in range(quarters):
        fetch(q).start()

    barrier = pltpu.get_barrier_semaphore()
    for step in range(1, ni):
        pl.semaphore_signal(
            barrier, inc=1, device_id=(lax.rem(i_at + step, ni), o_at), device_id_type=MESH
        )
    for step in range(1, no):
        pl.semaphore_signal(
            barrier, inc=1, device_id=(i_at, lax.rem(o_at + step, no)), device_id_type=MESH
        )

    row_at = lax.broadcasted_iota(jnp.int32, (BOUND_ROWS, 128), 0)
    left_shift = jnp.zeros((BOUND_ROWS, 128), jnp.int32)
    shift_copy.wait()
    for hop in range(ibits + obits):
        left_shift = jnp.where(row_at == hop, 12 - shifts_smem[0, hop], left_shift)
    own_limits = jnp.left_shift(jnp.ones_like(left_shift), left_shift).astype(jnp.float32) * 0.109375
    own_limits = own_limits.astype(jnp.bfloat16)
    limits[i_at, :, :] = own_limits
    limit_box[...] = own_limits

    def fill_place(ref, piece):
        size = ref.shape[0]
        row = lax.broadcasted_iota(jnp.int32, (size, 128), 0)
        lane = lax.broadcasted_iota(jnp.int32, (size, 128), 1)
        owner = lax.div(row, piece)
        offset = lane - (owner * rows + row - owner * piece)
        for n in range(span // 128):
            ref[:, pl.ds(n * 128, 128)] = offset + n * 128

    fill_place(place, parts[0][3])
    if place_last is not None:
        fill_place(place_last, parts[-1][3])

    grad_copy.wait()
    pl.semaphore_wait(barrier, ni + no - 2)

    cut = tokens // 2

    def ring(way, step):
        sign = 1 if way == 0 else -1
        source = 2 * z_off(sign * (1 - step)) + core
        target = at_inner(z_off(sign), core)
        pieces = (0, 1) if step < half else (way,)
        copies = []
        for n in pieces:
            piece = grads.at[source, pl.ds(n * cut, cut)]
            copies.append(
                pltpu.make_async_remote_copy(
                    src_ref=piece,
                    dst_ref=piece,
                    send_sem=ring_send.at[way, step - 1, n],
                    recv_sem=ring_recv.at[way, step - 1, n],
                    device_id=target,
                    device_id_type=MESH,
                )
            )
        if step < half or way == 0:
            copies.append(
                pltpu.make_async_remote_copy(
                    src_ref=limits.at[source],
                    dst_ref=limits.at[source],
                    send_sem=tile_send.at[way, step - 1],
                    recv_sem=tile_recv.at[way, step - 1],
                    device_id=target,
                    device_id_type=MESH,
                )
            )
        return copies

    def twin(offset, side):
        source = 2 * z_off(offset) + side
        return [
            pltpu.make_async_remote_copy(
                src_ref=ref.at[source],
                dst_ref=ref.at[source],
                send_sem=send.at[offset % nz],
                recv_sem=recv_at.at[offset % nz],
                device_id=at_inner(z_at, 1 - core),
                device_id_type=MESH,
            )
            for ref, send, recv_at in (
                (grads, twin_send, twin_recv),
                (limits, twin_tile_send, twin_tile_recv),
            )
        ]

    def start_all(copies):
        for copy in copies:
            copy.start()

    def wait_sent(copies):
        for copy in copies:
            copy.wait_send()

    def wait_arrived(copies):
        for copy in copies:
            copy.wait_recv()

    def ring_arrived(step):
        wait_arrived(ring(0, step))
        wait_arrived(ring(1, step))
        if step < half:
            start_all(ring(0, step + 1))
            start_all(ring(1, step + 1))
            start_all(twin(-step, core))
            start_all(twin(step, core))
        else:
            start_all(twin(half, core))

    def limit_copy(target):
        return pltpu.make_async_remote_copy(
            src_ref=limit_box,
            dst_ref=limits_in.at[o_at],
            send_sem=limit_send.at[target],
            recv_sem=limit_recv.at[o_at],
            device_id=(i_at, target),
            device_id_type=MESH,
        )

    def limit_arrival(source):
        return pltpu.make_async_remote_copy(
            src_ref=limit_box,
            dst_ref=limits_in.at[source],
            send_sem=limit_send.at[source],
            recv_sem=limit_recv.at[source],
            device_id=(i_at, source),
            device_id_type=MESH,
        )

    def turn(part, target):
        start, size, at, piece = parts[part]
        column = target * block
        tile = lax.div(column, 128)
        source = place if piece == parts[0][3] else place_last
        pick = (source[...] == column - tile * 128 + at).astype(jnp.bfloat16)
        window = raw[:, pl.ds(pl.multiple_of(tile * 128, 128), span)]
        acts_t[pl.ds(aligned(column + start), size), :] = lax.dot_general(
            pick, window, (((1,), (1,)), ((), ())), preferred_element_type=jnp.float32
        ).astype(jnp.bfloat16)

    def block_copy(part, target):
        start, size = parts[part][:2]
        slot = xor(i_at, target, ibits)
        return pltpu.make_async_remote_copy(
            src_ref=acts_t.at[pl.ds(aligned(target * block + start), size)],
            dst_ref=recv.at[slot, pl.ds(start, size)],
            send_sem=block_send.at[part, slot],
            recv_sem=block_recv.at[part, slot],
            device_id=(target, o_at),
            device_id_type=MESH,
        )

    def halves(part):
        start, size = parts[part][:2]
        low = round_up(size // 2, 16)
        return ((start, low), (start + low, size - low))

    def hop1(part, way, k):
        start, size = halves(part)[way]
        sign = 1 if way == 0 else -1
        target = 2 * z_off(half) + k
        return pltpu.make_async_remote_copy(
            src_ref=acts_t.at[pl.ds(aligned(target * block + start), size)],
            dst_ref=relay.at[k, pl.ds(start, size)],
            send_sem=hop1_send.at[part, way, k],
            recv_sem=hop1_recv.at[part, way, k],
            device_id=at_inner(z_off(sign * first), core),
            device_id_type=MESH,
        )

    def hop2(part, way, k):
        start, size = halves(part)[way]
        sign = 1 if way == 0 else -1
        differ = lax.rem(core + k, 2)
        return pltpu.make_async_remote_copy(
            src_ref=relay.at[k, pl.ds(start, size)],
            dst_ref=recv.at[2 * half + differ, pl.ds(start, size)],
            send_sem=hop2_send.at[part, way, differ],
            recv_sem=hop2_recv.at[part, way, differ],
            device_id=at_inner(z_off(sign * (half - first)), k),
            device_id_type=MESH,
        )

    def hop2_arrival(part, way, differ):
        start, size = halves(part)[way]
        piece = recv.at[2 * half + differ, pl.ds(start, size)]
        return pltpu.make_async_remote_copy(
            src_ref=piece,
            dst_ref=piece,
            send_sem=hop2_send.at[part, way, differ],
            recv_sem=hop2_recv.at[part, way, differ],
            device_id=at_inner(z_off(half), core),
            device_id_type=MESH,
        )

    def block_arrival(part, slot):
        start, size = parts[part][:2]
        piece = recv.at[slot, pl.ds(start, size)]
        return pltpu.make_async_remote_copy(
            src_ref=piece,
            dst_ref=piece,
            send_sem=block_send.at[part, slot],
            recv_sem=block_recv.at[part, slot],
            device_id=at_inner(z_at, 1 - core),
            device_id_type=MESH,
        )

    def local_copy(part):
        start, size = parts[part][:2]
        return pltpu.make_async_copy(
            acts_t.at[pl.ds(aligned(i_at * block + start), size)],
            recv.at[0, pl.ds(start, size)],
            local_sem.at[part],
        )

    def z_of_step(step):
        odd = lax.rem(step, 2)
        return z_off((2 * odd - 1) * (1 - 2 * core) * (half - lax.div(step + odd, 2)))

    def by_step(part, step, act):
        z = z_of_step(step)

        @pl.when(step == 0)
        def _():
            for way in range(2):
                for k in range(2):
                    act(hop1(part, way, k))

        @pl.when(jnp.logical_and(step > 0, step < nz - 1))
        def _():
            for k in range(2):
                act(block_copy(part, 2 * z + k))

        @pl.when(step == nz - 1)
        def _():
            act(block_copy(part, 2 * z_at + 1 - core))

    def start(copy):
        copy.start()

    def leave(copy):
        copy.wait_send()

    def turn_steps(part, low, high):
        def one(step, carry):
            z = z_of_step(step)
            for k in range(2):
                turn(part, 2 * z + k)
            return carry

        lax.fori_loop(low, high, one, 0)
        if high == nz:
            local_copy(part).start()

    def first_steps(part, low, high):
        def one(step, carry):
            z = z_of_step(step)
            for k in range(2):
                turn(part, 2 * z + k)
            by_step(part, step, start)
            return carry

        lax.fori_loop(low, high, one, 0)
        if high == nz:
            local_copy(part).start()

    def wait_steps(part, low, high):
        def one(step, carry):
            by_step(part, step, leave)
            return carry

        lax.fori_loop(low, high, one, 0)

    def next_steps(part, low, high, part_before, low_before):
        def one(step, carry):
            by_step(part_before, step - low + low_before, leave)
            by_step(part, step, start)
            return carry

        lax.fori_loop(low, high, one, 0)

    def forward(part):
        for way in range(2):
            for k in range(2):
                hop1(part, way, k).wait_recv()
                hop2(part, way, k).start()

    start_all(ring(0, 1))
    start_all(ring(1, 1))
    start_all(twin(0, core))
    for step in range(1, no):
        limit_copy(lax.rem(o_at + step, no)).start()
    for q in range(quarters):
        fetch(q).wait()
    far = min(3, nz)
    first_steps(0, 0, nz)
    ring_arrived(1)
    forward(0)
    if count > 1:
        first_steps(1, 0, far)
    if half > 1:
        ring_arrived(2)
    if count > 1:
        first_steps(1, far, nz)
    if half > 2:
        ring_arrived(3)
    if count > 1:
        forward(1)
    if count > 2:
        first_steps(2, 0, far)
    for step in range(4, half + 1):
        ring_arrived(step)
    if count > 2:
        turn_steps(2, far, nz)
    for part in range(3, count):
        turn_steps(part, 0, nz)

    def wide(tile):
        return jnp.tile(tile.astype(jnp.float32), (1, keys // 128))

    def leaf(slot, start, size):
        source = xor(i_at, slot, ibits)
        value = jnp.dot(
            recv[slot, pl.ds(start, size), :],
            grads[source],
            preferred_element_type=jnp.float32,
        )
        return value, wide(limits[source])

    def out_copy(part, target):
        piece_at = pl.ds(parts[part][2], 16)
        return pltpu.make_async_remote_copy(
            src_ref=out_box.at[target, piece_at],
            dst_ref=in_box.at[o_at, piece_at],
            send_sem=out_send.at[part, target],
            recv_sem=out_recv.at[part, o_at],
            device_id=(i_at, target),
            device_id_type=MESH,
        )

    def out_arrival(part, source):
        piece_at = pl.ds(parts[part][2], 16)
        return pltpu.make_async_remote_copy(
            src_ref=in_box.at[source, piece_at],
            dst_ref=in_box.at[source, piece_at],
            send_sem=out_send.at[part, source],
            recv_sem=out_recv.at[part, source],
            device_id=(i_at, source),
            device_id_type=MESH,
        )

    quarter = ni // 4

    def arrived(part, n):
        @pl.when(n == 0)
        def _():
            local_copy(part).wait()

        @pl.when(n != 0)
        def _():
            block_arrival(part, n).wait_recv()

        for m in (1, 2, 3):
            slot = n + m * quarter
            if m * quarter != 2 * half:
                block_arrival(part, slot).wait_recv()
                continue

            @pl.when(n < 2)
            def _():
                for way in range(2):
                    hop2_arrival(part, way, n).wait_recv()

            @pl.when(n >= 2)
            def _():
                block_arrival(part, slot).wait_recv()

    def work(part):
        start, size, at, piece = parts[part]

        def group(index, carry):
            n = quarter - 1 - index
            arrived(part, n)
            kept, _ = leaf(n, start, size)
            given, limit = leaf(n + 2 * quarter, start, size)
            first_sum = kept + clipped(given, limit[0:1])
            kept, limit_1 = leaf(n + quarter, start, size)
            given, limit = leaf(n + 3 * quarter, start, size)
            second_sum = kept + clipped(given, limit[0:1])
            sums[n, pl.ds(0, size), :] = first_sum + clipped(second_sum, limit_1[1:2])
            return carry

        lax.fori_loop(0, quarter, group, 0)
        level = 2
        width_now = quarter
        while width_now > 1:
            width_now //= 2
            for n in range(width_now):
                source = xor(i_at, n + width_now, ibits)
                limit = wide(limits[source])
                value = sums[n, pl.ds(0, size), :] + clipped(
                    sums[n + width_now, pl.ds(0, size), :], limit[level : level + 1]
                )
                if width_now == 1:
                    total[pl.ds(0, size), :] = value
                else:
                    sums[n, pl.ds(0, size), :] = value
            level += 1
        for owner in range(no):
            out_box[owner, pl.ds(at, 16), :] = total[pl.ds(owner * piece, 16), :].astype(
                jnp.bfloat16
            )
        for step in range(1, no):
            out_copy(part, lax.rem(o_at + step, no)).start()

    def finish(part):
        _, _, at, piece = parts[part]
        for step in range(1, no):
            out_arrival(part, lax.rem(o_at + step, no)).wait_recv()
        leaves = [out_box[o_at, pl.ds(at, 16), :].astype(jnp.float32)]
        caps = [None]
        for slot in range(1, no):
            source = xor(o_at, slot, obits)
            leaves.append(in_box[source, pl.ds(at, 16), :].astype(jnp.float32))
            caps.append(wide(limits_in[source]))
        many = no
        for hop in range(obits):
            many //= 2
            level = ibits + hop
            leaves = [
                leaves[n] + clipped(leaves[n + many], caps[n + many][level : level + 1])
                for n in range(many)
            ]
        out_ref[pl.ds(at, piece), :] = leaves[0][0:piece]

    def pieces_sent(part):
        for step in range(1, no):
            out_copy(part, lax.rem(o_at + step, no)).wait_send()

    def relays_sent(part):
        for way in range(2):
            for k in range(2):
                hop2(part, way, k).wait_send()

    for part in range(count):
        if part + 2 < count:
            forward(part + 2)
            next_steps(part + 2, far, nz, part, 0)
        if part + 3 < count:
            next_steps(part + 3, 0, far, part, nz - far)
        if part == 0:
            for offset in range(nz):
                wait_arrived(twin(offset, 1 - core))
            for step in range(1, no):
                limit_arrival(lax.rem(o_at + step, no)).wait_recv()
        if part + 1 == count:
            for way in range(2):
                for step in range(1, half + 1):
                    wait_sent(ring(way, step))
            for offset in range(nz):
                wait_sent(twin(offset, core))
            for step in range(1, no):
                limit_copy(lax.rem(o_at + step, no)).wait_send()
            if part > 1:
                wait_steps(part - 2, nz - far, nz)
            if part > 0:
                wait_steps(part - 1, 0, nz)
            for early in range(part):
                relays_sent(early)
                pieces_sent(early)
            if part > 0:
                finish(part - 1)
        work(part)
        if 0 < part < count - 1:
            finish(part - 1)
    wait_steps(count - 1, 0, nz)
    relays_sent(count - 1)
    finish(count - 1)
    pieces_sent(count - 1)


def cut_parts(rows, no):
    return tuple(
        (no * at, no * min(16, rows - at), at, min(16, rows - at)) for at in range(0, rows, 16)
    )


def body(acts, key_grad, shifts):
    ni = lax.axis_size("inner")
    no = lax.axis_size("outer")
    tokens, width = acts.shape
    keys = key_grad.shape[1]
    block = width // ni
    rows = block // no
    nz = ni // 2
    half = nz // 2
    parts = cut_parts(rows, no)
    count = len(parts)
    widest = parts[0][1]
    span = max(
        round_up(block * (n + 1), 128) - block * n // 128 * 128 for n in range(ni)
    )
    padded = round_up(rows, 16)
    dma = pltpu.SemaphoreType.DMA
    return pl.pallas_call(
        functools.partial(kernel, ni, no, parts, span),
        out_shape=pltpu.VMEM((rows, keys), jnp.float32),
        in_specs=[
            pl.BlockSpec(memory_space=pl.ANY),
            pl.BlockSpec(memory_space=pl.ANY),
            pl.BlockSpec(memory_space=pl.ANY),
        ],
        out_specs=pl.BlockSpec(memory_space=pltpu.VMEM),
        scratch_shapes=[
            pltpu.VMEM((tokens, width), jnp.bfloat16),
            pltpu.VMEM((width, tokens), jnp.bfloat16),
            pltpu.VMEM((ni, block, tokens), jnp.bfloat16),
            pltpu.VMEM((2, block, tokens), jnp.bfloat16),
            pltpu.VMEM((ni, tokens, keys), jnp.bfloat16),
            pltpu.VMEM((ni, BOUND_ROWS, 128), jnp.bfloat16),
            pltpu.VMEM((ni // 4, widest, keys), jnp.float32),
            pltpu.VMEM((widest, keys), jnp.float32),
            pltpu.VMEM((widest, span), jnp.int32),
            pltpu.VMEM((parts[-1][1], span), jnp.int32),
            pltpu.VMEM((no, padded, keys), jnp.bfloat16),
            pltpu.VMEM((no, padded, keys), jnp.bfloat16),
            pltpu.VMEM((BOUND_ROWS, 128), jnp.bfloat16),
            pltpu.VMEM((no, BOUND_ROWS, 128), jnp.bfloat16),
            pltpu.SMEM(shifts.shape, jnp.int32),
            dma,
            dma((4,)),
            dma,
            dma((2, half, 2)),
            dma((2, half, 2)),
            dma((2, half)),
            dma((2, half)),
            dma((nz,)),
            dma((nz,)),
            dma((nz,)),
            dma((nz,)),
            dma((count, ni)),
            dma((count, ni)),
            dma((count, 2, 2)),
            dma((count, 2, 2)),
            dma((count, 2, 2)),
            dma((count, 2, 2)),
            dma((count,)),
            dma((count, no)),
            dma((count, no)),
            dma((no,)),
            dma((no,)),
        ],
        compiler_params=pltpu.CompilerParams(
            collective_id=0, has_side_effects=True, vmem_limit_bytes=56 * 1024 * 1024
        ),
        cost_estimate=pl.CostEstimate(
            flops=2 * tokens * width * keys, bytes_accessed=2 * tokens * width, transcendentals=0
        ),
    )(acts, key_grad, shifts)


def solution(mesh):
    return jax.shard_map(
        body,
        mesh=mesh,
        in_specs=(
            P(("inner", "outer"), None),
            P(("inner", "outer"), None),
            P(("inner", "outer"), None),
        ),
        out_specs=P(("inner", "outer"), None),
        check_vma=False,
    )
```

```python
import functools

import jax
import jax.numpy as jnp
from jax import lax
from jax.experimental import pallas as pl
from jax.experimental.pallas import tpu as pltpu
from jax.sharding import PartitionSpec as P

MESH = pl.DeviceIdType.MESH
BOUND_ROWS = 16


def xor(a, b, bits):
    total = 0
    for bit in range(bits):
        step = 1 << bit
        total = total + step * lax.rem(lax.div(a, step) + lax.div(b, step), 2)
    return total


def clipped(values, bound):
    return jnp.clip(values, -bound, bound).astype(jnp.bfloat16).astype(jnp.float32)


def aligned(index):
    return pl.multiple_of(index, 16)


def round_up(value, unit):
    return -(-value // unit) * unit


def kernel(
    ni,
    no,
    parts,
    span,
    acts_hbm,
    grad_hbm,
    shifts_hbm,
    out_ref,
    raw,
    acts_t,
    recv,
    relay,
    grads,
    limits,
    sums,
    total,
    places,
    out_box,
    in_box,
    limit_box,
    limits_in,
    shifts_smem,
    shift_sem,
    fetch_sem,
    grad_sem,
    ring_send,
    ring_recv,
    tile_send,
    tile_recv,
    twin_send,
    twin_recv,
    twin_tile_send,
    twin_tile_recv,
    block_send,
    block_recv,
    hop1_send,
    hop1_recv,
    hop2_send,
    hop2_recv,
    local_sem,
    out_send,
    out_recv,
    limit_send,
    limit_recv,
):
    tokens, width = raw.shape
    keys = grads.shape[2]
    block = width // ni
    rows = block // no
    nz = ni // 2
    half = nz // 2
    first = half // 2
    ibits = ni.bit_length() - 1
    obits = no.bit_length() - 1
    quarters = 4
    strip = width // quarters
    count = len(parts)

    i_at = lax.axis_index("inner")
    o_at = lax.axis_index("outer")
    z_at = lax.div(i_at, 2)
    core = lax.rem(i_at, 2)

    def z_off(step):
        return lax.rem(z_at + step + nz, nz)

    def at_inner(z, k):
        return (2 * z + k, o_at)

    def fetch(q):
        cols = pl.ds(q * strip, strip)
        return pltpu.make_async_copy(acts_hbm.at[:, cols], raw.at[:, cols], fetch_sem.at[q])

    shift_copy = pltpu.make_async_copy(shifts_hbm, shifts_smem, shift_sem)
    shift_copy.start()
    grad_copy = pltpu.make_async_copy(grad_hbm, grads.at[i_at, pl.ds(0, tokens)], grad_sem)
    grad_copy.start()
    for q in range(quarters):
        fetch(q).start()

    barrier = pltpu.get_barrier_semaphore()
    for step in range(1, ni):
        pl.semaphore_signal(
            barrier, inc=1, device_id=(lax.rem(i_at + step, ni), o_at), device_id_type=MESH
        )
    for step in range(1, no):
        pl.semaphore_signal(
            barrier, inc=1, device_id=(i_at, lax.rem(o_at + step, no)), device_id_type=MESH
        )

    row_at = lax.broadcasted_iota(jnp.int32, (BOUND_ROWS, 128), 0)
    left_shift = jnp.zeros((BOUND_ROWS, 128), jnp.int32)
    shift_copy.wait()
    for hop in range(ibits + obits):
        left_shift = jnp.where(row_at == hop, 12 - shifts_smem[0, hop], left_shift)
    own_limits = jnp.left_shift(jnp.ones_like(left_shift), left_shift).astype(jnp.float32) * 0.109375
    own_limits = own_limits.astype(jnp.bfloat16)
    limits[i_at, :, :] = own_limits
    limit_box[...] = own_limits

    def fill_place(ref, piece):
        size = ref.shape[0]
        row = lax.broadcasted_iota(jnp.int32, (size, 128), 0)
        lane = lax.broadcasted_iota(jnp.int32, (size, 128), 1)
        owner = lax.div(row, piece)
        offset = lane - (owner * rows + row - owner * piece)
        for n in range(span // 128):
            ref[:, pl.ds(n * 128, 128)] = offset + n * 128

    kinds = sorted(set(piece for _, _, _, piece in parts))
    for kind, ref in zip(kinds, places):
        fill_place(ref, kind)

    grad_copy.wait()
    pl.semaphore_wait(barrier, ni + no - 2)

    cut = tokens // 2

    def ring(way, step):
        sign = 1 if way == 0 else -1
        source = 2 * z_off(sign * (1 - step)) + core
        target = at_inner(z_off(sign), core)
        pieces = (0, 1) if step < half else (way,)
        copies = []
        for n in pieces:
            piece = grads.at[source, pl.ds(n * cut, cut)]
            copies.append(
                pltpu.make_async_remote_copy(
                    src_ref=piece,
                    dst_ref=piece,
                    send_sem=ring_send.at[way, step - 1, n],
                    recv_sem=ring_recv.at[way, step - 1, n],
                    device_id=target,
                    device_id_type=MESH,
                )
            )
        if step < half or way == 0:
            copies.append(
                pltpu.make_async_remote_copy(
                    src_ref=limits.at[source],
                    dst_ref=limits.at[source],
                    send_sem=tile_send.at[way, step - 1],
                    recv_sem=tile_recv.at[way, step - 1],
                    device_id=target,
                    device_id_type=MESH,
                )
            )
        return copies

    def twin(offset, side):
        source = 2 * z_off(offset) + side
        return [
            pltpu.make_async_remote_copy(
                src_ref=ref.at[source],
                dst_ref=ref.at[source],
                send_sem=send.at[offset % nz],
                recv_sem=recv_at.at[offset % nz],
                device_id=at_inner(z_at, 1 - core),
                device_id_type=MESH,
            )
            for ref, send, recv_at in (
                (grads, twin_send, twin_recv),
                (limits, twin_tile_send, twin_tile_recv),
            )
        ]

    def start_all(copies):
        for copy in copies:
            copy.start()

    def wait_sent(copies):
        for copy in copies:
            copy.wait_send()

    def wait_arrived(copies):
        for copy in copies:
            copy.wait_recv()

    def ring_arrived(step):
        wait_arrived(ring(0, step))
        wait_arrived(ring(1, step))
        if step < half:
            start_all(ring(0, step + 1))
            start_all(ring(1, step + 1))
            start_all(twin(-step, core))
            start_all(twin(step, core))
        else:
            start_all(twin(half, core))

    def limit_copy(target):
        return pltpu.make_async_remote_copy(
            src_ref=limit_box,
            dst_ref=limits_in.at[o_at],
            send_sem=limit_send.at[target],
            recv_sem=limit_recv.at[o_at],
            device_id=(i_at, target),
            device_id_type=MESH,
        )

    def limit_arrival(source):
        return pltpu.make_async_remote_copy(
            src_ref=limit_box,
            dst_ref=limits_in.at[source],
            send_sem=limit_send.at[source],
            recv_sem=limit_recv.at[source],
            device_id=(i_at, source),
            device_id_type=MESH,
        )

    def turn(part, target):
        start, size, at, piece = parts[part]
        column = target * block
        tile = lax.div(column, 128)
        source = places[kinds.index(piece)]
        pick = (source[...] == column - tile * 128 + at).astype(jnp.bfloat16)
        window = raw[:, pl.ds(pl.multiple_of(tile * 128, 128), span)]
        acts_t[pl.ds(aligned(column + start), size), :] = lax.dot_general(
            pick, window, (((1,), (1,)), ((), ())), preferred_element_type=jnp.float32
        ).astype(jnp.bfloat16)

    def block_copy(part, target):
        start, size = parts[part][:2]
        slot = xor(i_at, target, ibits)
        return pltpu.make_async_remote_copy(
            src_ref=acts_t.at[pl.ds(aligned(target * block + start), size)],
            dst_ref=recv.at[slot, pl.ds(start, size)],
            send_sem=block_send.at[part, slot],
            recv_sem=block_recv.at[part, slot],
            device_id=(target, o_at),
            device_id_type=MESH,
        )

    def halves(part):
        start, size = parts[part][:2]
        low = round_up(size // 2, 16)
        return ((start, low), (start + low, size - low))

    def hop1(part, way, k):
        start, size = halves(part)[way]
        sign = 1 if way == 0 else -1
        target = 2 * z_off(half) + k
        return pltpu.make_async_remote_copy(
            src_ref=acts_t.at[pl.ds(aligned(target * block + start), size)],
            dst_ref=relay.at[k, pl.ds(start, size)],
            send_sem=hop1_send.at[part, way, k],
            recv_sem=hop1_recv.at[part, way, k],
            device_id=at_inner(z_off(sign * first), core),
            device_id_type=MESH,
        )

    def hop2(part, way, k):
        start, size = halves(part)[way]
        sign = 1 if way == 0 else -1
        differ = lax.rem(core + k, 2)
        return pltpu.make_async_remote_copy(
            src_ref=relay.at[k, pl.ds(start, size)],
            dst_ref=recv.at[2 * half + differ, pl.ds(start, size)],
            send_sem=hop2_send.at[part, way, differ],
            recv_sem=hop2_recv.at[part, way, differ],
            device_id=at_inner(z_off(sign * (half - first)), k),
            device_id_type=MESH,
        )

    def hop2_arrival(part, way, differ):
        start, size = halves(part)[way]
        piece = recv.at[2 * half + differ, pl.ds(start, size)]
        return pltpu.make_async_remote_copy(
            src_ref=piece,
            dst_ref=piece,
            send_sem=hop2_send.at[part, way, differ],
            recv_sem=hop2_recv.at[part, way, differ],
            device_id=at_inner(z_off(half), core),
            device_id_type=MESH,
        )

    def block_arrival(part, slot):
        start, size = parts[part][:2]
        piece = recv.at[slot, pl.ds(start, size)]
        return pltpu.make_async_remote_copy(
            src_ref=piece,
            dst_ref=piece,
            send_sem=block_send.at[part, slot],
            recv_sem=block_recv.at[part, slot],
            device_id=at_inner(z_at, 1 - core),
            device_id_type=MESH,
        )

    def local_copy(part):
        start, size = parts[part][:2]
        return pltpu.make_async_copy(
            acts_t.at[pl.ds(aligned(i_at * block + start), size)],
            recv.at[0, pl.ds(start, size)],
            local_sem.at[part],
        )

    def z_of_step(step):
        odd = lax.rem(step, 2)
        return z_off((2 * odd - 1) * (1 - 2 * core) * (half - lax.div(step + odd, 2)))

    def by_step(part, step, act):
        z = z_of_step(step)

        @pl.when(step == 0)
        def _():
            for way in range(2):
                for k in range(2):
                    act(hop1(part, way, k))

        @pl.when(jnp.logical_and(step > 0, step < nz - 1))
        def _():
            for k in range(2):
                act(block_copy(part, 2 * z + k))

        @pl.when(step == nz - 1)
        def _():
            act(block_copy(part, 2 * z_at + 1 - core))

    def start(copy):
        copy.start()

    def leave(copy):
        copy.wait_send()

    def turn_steps(part, low, high):
        def one(step, carry):
            z = z_of_step(step)
            for k in range(2):
                turn(part, 2 * z + k)
            return carry

        lax.fori_loop(low, high, one, 0)
        if high == nz:
            local_copy(part).start()

    def first_steps(part, low, high):
        def one(step, carry):
            z = z_of_step(step)
            for k in range(2):
                turn(part, 2 * z + k)
            by_step(part, step, start)
            return carry

        lax.fori_loop(low, high, one, 0)
        if high == nz:
            local_copy(part).start()

    def wait_steps(part, low, high):
        def one(step, carry):
            by_step(part, step, leave)
            return carry

        lax.fori_loop(low, high, one, 0)

    def next_steps(part, low, high, part_before, low_before):
        def one(step, carry):
            by_step(part_before, step - low + low_before, leave)
            by_step(part, step, start)
            return carry

        lax.fori_loop(low, high, one, 0)

    def forward(part):
        for way in range(2):
            for k in range(2):
                hop1(part, way, k).wait_recv()
                hop2(part, way, k).start()

    start_all(ring(0, 1))
    start_all(ring(1, 1))
    start_all(twin(0, core))
    for step in range(1, no):
        limit_copy(lax.rem(o_at + step, no)).start()
    for q in range(quarters):
        fetch(q).wait()
    far = min(3, nz)
    first_steps(0, 0, nz)
    ring_arrived(1)
    forward(0)
    if count > 1:
        first_steps(1, 0, far)
    if half > 1:
        ring_arrived(2)
    if count > 1:
        first_steps(1, far, nz)
    if half > 2:
        ring_arrived(3)
    if count > 1:
        forward(1)
    if count > 2:
        first_steps(2, 0, far)
    for step in range(4, half + 1):
        ring_arrived(step)
    if count > 2:
        turn_steps(2, far, nz)
    for part in range(3, count):
        turn_steps(part, 0, nz)

    def wide(tile):
        return jnp.tile(tile.astype(jnp.float32), (1, keys // 128))

    def leaf(slot, start, size):
        source = xor(i_at, slot, ibits)
        value = jnp.dot(
            recv[slot, pl.ds(start, size), :],
            grads[source],
            preferred_element_type=jnp.float32,
        )
        return value, wide(limits[source])

    def out_copy(part, target):
        piece_at = pl.ds(parts[part][2], round_up(parts[part][3], 16))
        return pltpu.make_async_remote_copy(
            src_ref=out_box.at[target, piece_at],
            dst_ref=in_box.at[o_at, piece_at],
            send_sem=out_send.at[part, target],
            recv_sem=out_recv.at[part, o_at],
            device_id=(i_at, target),
            device_id_type=MESH,
        )

    def out_arrival(part, source):
        piece_at = pl.ds(parts[part][2], round_up(parts[part][3], 16))
        return pltpu.make_async_remote_copy(
            src_ref=in_box.at[source, piece_at],
            dst_ref=in_box.at[source, piece_at],
            send_sem=out_send.at[part, source],
            recv_sem=out_recv.at[part, source],
            device_id=(i_at, source),
            device_id_type=MESH,
        )

    quarter = ni // 4

    def arrived(part, n):
        @pl.when(n == 0)
        def _():
            local_copy(part).wait()

        @pl.when(n != 0)
        def _():
            block_arrival(part, n).wait_recv()

        for m in (1, 2, 3):
            slot = n + m * quarter
            if m * quarter != 2 * half:
                block_arrival(part, slot).wait_recv()
                continue

            @pl.when(n < 2)
            def _():
                for way in range(2):
                    hop2_arrival(part, way, n).wait_recv()

            @pl.when(n >= 2)
            def _():
                block_arrival(part, slot).wait_recv()

    def work(part):
        start, size, at, piece = parts[part]
        high = round_up(piece, 16)

        def group(index, carry):
            n = quarter - 1 - index
            arrived(part, n)
            kept, _ = leaf(n, start, size)
            given, limit = leaf(n + 2 * quarter, start, size)
            first_sum = kept + clipped(given, limit[0:1])
            kept, limit_1 = leaf(n + quarter, start, size)
            given, limit = leaf(n + 3 * quarter, start, size)
            second_sum = kept + clipped(given, limit[0:1])
            sums[n, pl.ds(0, size), :] = first_sum + clipped(second_sum, limit_1[1:2])
            return carry

        lax.fori_loop(0, quarter, group, 0)
        level = 2
        width_now = quarter
        while width_now > 1:
            width_now //= 2
            for n in range(width_now):
                source = xor(i_at, n + width_now, ibits)
                limit = wide(limits[source])
                value = sums[n, pl.ds(0, size), :] + clipped(
                    sums[n + width_now, pl.ds(0, size), :], limit[level : level + 1]
                )
                if width_now == 1:
                    total[pl.ds(0, size), :] = value
                else:
                    sums[n, pl.ds(0, size), :] = value
            level += 1
        for owner in range(no):
            out_box[owner, pl.ds(at, high), :] = total[pl.ds(owner * piece, high), :].astype(
                jnp.bfloat16
            )
        for step in range(1, no):
            out_copy(part, lax.rem(o_at + step, no)).start()

    def finish(part):
        _, _, at, piece = parts[part]
        high = round_up(piece, 16)
        for step in range(1, no):
            out_arrival(part, lax.rem(o_at + step, no)).wait_recv()
        leaves = [out_box[o_at, pl.ds(at, high), :].astype(jnp.float32)]
        caps = [None]
        for slot in range(1, no):
            source = xor(o_at, slot, obits)
            leaves.append(in_box[source, pl.ds(at, high), :].astype(jnp.float32))
            caps.append(wide(limits_in[source]))
        many = no
        for hop in range(obits):
            many //= 2
            level = ibits + hop
            leaves = [
                leaves[n] + clipped(leaves[n + many], caps[n + many][level : level + 1])
                for n in range(many)
            ]
        out_ref[pl.ds(at, piece), :] = leaves[0][0:piece]

    def pieces_sent(part):
        for step in range(1, no):
            out_copy(part, lax.rem(o_at + step, no)).wait_send()

    def relays_sent(part):
        for way in range(2):
            for k in range(2):
                hop2(part, way, k).wait_send()

    for part in range(count):
        if part + 2 < count:
            forward(part + 2)
            next_steps(part + 2, far, nz, part, 0)
        if part + 3 < count:
            next_steps(part + 3, 0, far, part, nz - far)
        if part == 0:
            for offset in range(nz):
                wait_arrived(twin(offset, 1 - core))
            for step in range(1, no):
                limit_arrival(lax.rem(o_at + step, no)).wait_recv()
        if part + 1 == count:
            for way in range(2):
                for step in range(1, half + 1):
                    wait_sent(ring(way, step))
            for offset in range(nz):
                wait_sent(twin(offset, core))
            for step in range(1, no):
                limit_copy(lax.rem(o_at + step, no)).wait_send()
            if part > 1:
                wait_steps(part - 2, nz - far, nz)
            if part > 0:
                wait_steps(part - 1, 0, nz)
            for early in range(part):
                relays_sent(early)
                pieces_sent(early)
            if part > 0:
                finish(part - 1)
        work(part)
        if 0 < part < count - 1:
            finish(part - 1)
    wait_steps(count - 1, 0, nz)
    relays_sent(count - 1)
    finish(count - 1)
    pieces_sent(count - 1)


def cut_parts(rows, no):
    parts, at = [], 0
    for piece in (16, 32, 16, 16):
        piece = min(piece, rows - at)
        if piece > 0:
            parts.append((no * at, no * piece, at, piece))
        at += piece
    return tuple(parts)


def body(acts, key_grad, shifts):
    ni = lax.axis_size("inner")
    no = lax.axis_size("outer")
    tokens, width = acts.shape
    keys = key_grad.shape[1]
    block = width // ni
    rows = block // no
    nz = ni // 2
    half = nz // 2
    parts = cut_parts(rows, no)
    count = len(parts)
    widest = max(size for _, size, _, _ in parts)
    kinds = sorted(set((piece, size) for _, size, _, piece in parts))
    span = max(
        round_up(block * (n + 1), 128) - block * n // 128 * 128 for n in range(ni)
    )
    padded = round_up(rows, 16)
    dma = pltpu.SemaphoreType.DMA
    return pl.pallas_call(
        functools.partial(kernel, ni, no, parts, span),
        out_shape=pltpu.VMEM((rows, keys), jnp.float32),
        in_specs=[
            pl.BlockSpec(memory_space=pl.ANY),
            pl.BlockSpec(memory_space=pl.ANY),
            pl.BlockSpec(memory_space=pl.ANY),
        ],
        out_specs=pl.BlockSpec(memory_space=pltpu.VMEM),
        scratch_shapes=[
            pltpu.VMEM((tokens, width), jnp.bfloat16),
            pltpu.VMEM((width, tokens), jnp.bfloat16),
            pltpu.VMEM((ni, block, tokens), jnp.bfloat16),
            pltpu.VMEM((2, block, tokens), jnp.bfloat16),
            pltpu.VMEM((ni, tokens, keys), jnp.bfloat16),
            pltpu.VMEM((ni, BOUND_ROWS, 128), jnp.bfloat16),
            pltpu.VMEM((ni // 4, widest, keys), jnp.float32),
            pltpu.VMEM((round_up(widest + 16, 16), keys), jnp.float32),
            [pltpu.VMEM((size, span), jnp.int32) for _, size in kinds],
            pltpu.VMEM((no, padded, keys), jnp.bfloat16),
            pltpu.VMEM((no, padded, keys), jnp.bfloat16),
            pltpu.VMEM((BOUND_ROWS, 128), jnp.bfloat16),
            pltpu.VMEM((no, BOUND_ROWS, 128), jnp.bfloat16),
            pltpu.SMEM(shifts.shape, jnp.int32),
            dma,
            dma((4,)),
            dma,
            dma((2, half, 2)),
            dma((2, half, 2)),
            dma((2, half)),
            dma((2, half)),
            dma((nz,)),
            dma((nz,)),
            dma((nz,)),
            dma((nz,)),
            dma((count, ni)),
            dma((count, ni)),
            dma((count, 2, 2)),
            dma((count, 2, 2)),
            dma((count, 2, 2)),
            dma((count, 2, 2)),
            dma((count,)),
            dma((count, no)),
            dma((count, no)),
            dma((no,)),
            dma((no,)),
        ],
        compiler_params=pltpu.CompilerParams(
            collective_id=0, has_side_effects=True, vmem_limit_bytes=56 * 1024 * 1024
        ),
        cost_estimate=pl.CostEstimate(
            flops=2 * tokens * width * keys, bytes_accessed=2 * tokens * width, transcendentals=0
        ),
    )(acts, key_grad, shifts)


def solution(mesh):
    return jax.shard_map(
        body,
        mesh=mesh,
        in_specs=(
            P(("inner", "outer"), None),
            P(("inner", "outer"), None),
            P(("inner", "outer"), None),
        ),
        out_specs=P(("inner", "outer"), None),
        check_vma=False,
    )
```

```python
import functools

import jax
import jax.numpy as jnp
from jax import lax
from jax.experimental import pallas as pl
from jax.experimental.pallas import tpu as pltpu
from jax.sharding import PartitionSpec as P

MESH = pl.DeviceIdType.MESH
BOUND_ROWS = 16


def xor(a, b, bits):
    total = 0
    for bit in range(bits):
        step = 1 << bit
        total = total + step * lax.rem(lax.div(a, step) + lax.div(b, step), 2)
    return total


def clipped(values, bound):
    return jnp.clip(values, -bound, bound).astype(jnp.bfloat16).astype(jnp.float32)


def aligned(index):
    return pl.multiple_of(index, 16)


def round_up(value, unit):
    return -(-value // unit) * unit


def kernel(
    ni,
    no,
    parts,
    span,
    acts_hbm,
    grad_hbm,
    shifts_hbm,
    out_ref,
    raw,
    acts_t,
    recv,
    relay,
    grads,
    limits,
    sums,
    total,
    places,
    out_box,
    in_box,
    limit_box,
    limits_in,
    shifts_smem,
    shift_sem,
    fetch_sem,
    grad_sem,
    ring_send,
    ring_recv,
    tile_send,
    tile_recv,
    twin_send,
    twin_recv,
    twin_tile_send,
    twin_tile_recv,
    block_send,
    block_recv,
    hop1_send,
    hop1_recv,
    hop2_send,
    hop2_recv,
    local_sem,
    out_send,
    out_recv,
    limit_send,
    limit_recv,
):
    tokens, width = raw.shape
    keys = grads.shape[2]
    block = width // ni
    rows = block // no
    nz = ni // 2
    half = nz // 2
    first = half // 2
    ibits = ni.bit_length() - 1
    obits = no.bit_length() - 1
    quarters = 4
    strip = width // quarters
    count = len(parts)

    i_at = lax.axis_index("inner")
    o_at = lax.axis_index("outer")
    z_at = lax.div(i_at, 2)
    core = lax.rem(i_at, 2)

    def z_off(step):
        return lax.rem(z_at + step + nz, nz)

    def at_inner(z, k):
        return (2 * z + k, o_at)

    def fetch(q):
        cols = pl.ds(q * strip, strip)
        return pltpu.make_async_copy(acts_hbm.at[:, cols], raw.at[:, cols], fetch_sem.at[q])

    shift_copy = pltpu.make_async_copy(shifts_hbm, shifts_smem, shift_sem)
    shift_copy.start()
    grad_copy = pltpu.make_async_copy(grad_hbm, grads.at[i_at, pl.ds(0, tokens)], grad_sem)
    grad_copy.start()
    barrier = pltpu.get_barrier_semaphore()
    for step in range(1, ni):
        pl.semaphore_signal(
            barrier, inc=1, device_id=(lax.rem(i_at + step, ni), o_at), device_id_type=MESH
        )
    for step in range(1, no):
        pl.semaphore_signal(
            barrier, inc=1, device_id=(i_at, lax.rem(o_at + step, no)), device_id_type=MESH
        )

    for q in range(quarters):
        fetch(q).start()

    row_at = lax.broadcasted_iota(jnp.int32, (BOUND_ROWS, 128), 0)
    left_shift = jnp.zeros((BOUND_ROWS, 128), jnp.int32)
    shift_copy.wait()
    for hop in range(ibits + obits):
        left_shift = jnp.where(row_at == hop, 12 - shifts_smem[0, hop], left_shift)
    own_limits = jnp.left_shift(jnp.ones_like(left_shift), left_shift).astype(jnp.float32) * 0.109375
    own_limits = own_limits.astype(jnp.bfloat16)
    limits[i_at, :, :] = own_limits
    limit_box[...] = own_limits

    def fill_place(ref, piece):
        size = ref.shape[0]
        row = lax.broadcasted_iota(jnp.int32, (size, 128), 0)
        lane = lax.broadcasted_iota(jnp.int32, (size, 128), 1)
        owner = lax.div(row, piece)
        offset = lane - (owner * rows + row - owner * piece)
        for n in range(span // 128):
            ref[:, pl.ds(n * 128, 128)] = offset + n * 128

    kinds = sorted(set(piece for _, _, _, piece in parts))

    grad_copy.wait()
    pl.semaphore_wait(barrier, ni + no - 2)

    cut = tokens // 2

    def ring(way, step):
        sign = 1 if way == 0 else -1
        source = 2 * z_off(sign * (1 - step)) + core
        target = at_inner(z_off(sign), core)
        pieces = (0, 1) if step < half else (way,)
        copies = []
        for n in pieces:
            piece = grads.at[source, pl.ds(n * cut, cut)]
            copies.append(
                pltpu.make_async_remote_copy(
                    src_ref=piece,
                    dst_ref=piece,
                    send_sem=ring_send.at[way, step - 1, n],
                    recv_sem=ring_recv.at[way, step - 1, n],
                    device_id=target,
                    device_id_type=MESH,
                )
            )
        if step < half or way == 0:
            copies.append(
                pltpu.make_async_remote_copy(
                    src_ref=limits.at[source],
                    dst_ref=limits.at[source],
                    send_sem=tile_send.at[way, step - 1],
                    recv_sem=tile_recv.at[way, step - 1],
                    device_id=target,
                    device_id_type=MESH,
                )
            )
        return copies

    def twin(offset, side):
        source = 2 * z_off(offset) + side
        return [
            pltpu.make_async_remote_copy(
                src_ref=ref.at[source],
                dst_ref=ref.at[source],
                send_sem=send.at[offset % nz],
                recv_sem=recv_at.at[offset % nz],
                device_id=at_inner(z_at, 1 - core),
                device_id_type=MESH,
            )
            for ref, send, recv_at in (
                (grads, twin_send, twin_recv),
                (limits, twin_tile_send, twin_tile_recv),
            )
        ]

    def start_all(copies):
        for copy in copies:
            copy.start()

    def wait_sent(copies):
        for copy in copies:
            copy.wait_send()

    def wait_arrived(copies):
        for copy in copies:
            copy.wait_recv()

    def ring_arrived(step):
        wait_arrived(ring(0, step))
        wait_arrived(ring(1, step))
        if step < half:
            start_all(ring(0, step + 1))
            start_all(ring(1, step + 1))
            start_all(twin(-step, core))
            start_all(twin(step, core))
        else:
            start_all(twin(half, core))

    def limit_copy(target):
        return pltpu.make_async_remote_copy(
            src_ref=limit_box,
            dst_ref=limits_in.at[o_at],
            send_sem=limit_send.at[target],
            recv_sem=limit_recv.at[o_at],
            device_id=(i_at, target),
            device_id_type=MESH,
        )

    def limit_arrival(source):
        return pltpu.make_async_remote_copy(
            src_ref=limit_box,
            dst_ref=limits_in.at[source],
            send_sem=limit_send.at[source],
            recv_sem=limit_recv.at[source],
            device_id=(i_at, source),
            device_id_type=MESH,
        )

    def turn(part, target):
        start, size, at, piece = parts[part]
        column = target * block
        tile = lax.div(column, 128)
        source = places[kinds.index(piece)]
        pick = (source[...] == column - tile * 128 + at).astype(jnp.bfloat16)
        window = raw[:, pl.ds(pl.multiple_of(tile * 128, 128), span)]
        acts_t[pl.ds(aligned(column + start), size), :] = lax.dot_general(
            pick, window, (((1,), (1,)), ((), ())), preferred_element_type=jnp.float32
        ).astype(jnp.bfloat16)

    def block_copy(part, target):
        start, size = parts[part][:2]
        slot = xor(i_at, target, ibits)
        return pltpu.make_async_remote_copy(
            src_ref=acts_t.at[pl.ds(aligned(target * block + start), size)],
            dst_ref=recv.at[slot, pl.ds(start, size)],
            send_sem=block_send.at[part, slot],
            recv_sem=block_recv.at[part, slot],
            device_id=(target, o_at),
            device_id_type=MESH,
        )

    def halves(part):
        start, size = parts[part][:2]
        low = round_up(size // 2, 16)
        return ((start, low), (start + low, size - low))

    def hop1(part, way, k):
        start, size = halves(part)[way]
        sign = 1 if way == 0 else -1
        target = 2 * z_off(half) + k
        return pltpu.make_async_remote_copy(
            src_ref=acts_t.at[pl.ds(aligned(target * block + start), size)],
            dst_ref=relay.at[k, pl.ds(start, size)],
            send_sem=hop1_send.at[part, way, k],
            recv_sem=hop1_recv.at[part, way, k],
            device_id=at_inner(z_off(sign * first), core),
            device_id_type=MESH,
        )

    def hop2(part, way, k):
        start, size = halves(part)[way]
        sign = 1 if way == 0 else -1
        differ = lax.rem(core + k, 2)
        return pltpu.make_async_remote_copy(
            src_ref=relay.at[k, pl.ds(start, size)],
            dst_ref=recv.at[2 * half + differ, pl.ds(start, size)],
            send_sem=hop2_send.at[part, way, differ],
            recv_sem=hop2_recv.at[part, way, differ],
            device_id=at_inner(z_off(sign * (half - first)), k),
            device_id_type=MESH,
        )

    def hop2_arrival(part, way, differ):
        start, size = halves(part)[way]
        piece = recv.at[2 * half + differ, pl.ds(start, size)]
        return pltpu.make_async_remote_copy(
            src_ref=piece,
            dst_ref=piece,
            send_sem=hop2_send.at[part, way, differ],
            recv_sem=hop2_recv.at[part, way, differ],
            device_id=at_inner(z_off(half), core),
            device_id_type=MESH,
        )

    def block_arrival(part, slot):
        start, size = parts[part][:2]
        piece = recv.at[slot, pl.ds(start, size)]
        return pltpu.make_async_remote_copy(
            src_ref=piece,
            dst_ref=piece,
            send_sem=block_send.at[part, slot],
            recv_sem=block_recv.at[part, slot],
            device_id=at_inner(z_at, 1 - core),
            device_id_type=MESH,
        )

    def local_copy(part):
        start, size = parts[part][:2]
        return pltpu.make_async_copy(
            acts_t.at[pl.ds(aligned(i_at * block + start), size)],
            recv.at[0, pl.ds(start, size)],
            local_sem.at[part],
        )

    def z_of_step(step):
        odd = lax.rem(step, 2)
        return z_off((2 * odd - 1) * (1 - 2 * core) * (half - lax.div(step + odd, 2)))

    def by_step(part, step, act):
        z = z_of_step(step)

        @pl.when(step == 0)
        def _():
            for way in range(2):
                for k in range(2):
                    act(hop1(part, way, k))

        @pl.when(jnp.logical_and(step > 0, step < nz - 1))
        def _():
            for k in range(2):
                act(block_copy(part, 2 * z + k))

        @pl.when(step == nz - 1)
        def _():
            act(block_copy(part, 2 * z_at + 1 - core))

    def start(copy):
        copy.start()

    def leave(copy):
        copy.wait_send()

    def turn_steps(part, low, high):
        def one(step, carry):
            z = z_of_step(step)
            for k in range(2):
                turn(part, 2 * z + k)
            return carry

        lax.fori_loop(low, high, one, 0)
        if high == nz:
            local_copy(part).start()

    def first_steps(part, low, high):
        def one(step, carry):
            z = z_of_step(step)
            for k in range(2):
                turn(part, 2 * z + k)
            by_step(part, step, start)
            return carry

        lax.fori_loop(low, high, one, 0)
        if high == nz:
            local_copy(part).start()

    def wait_steps(part, low, high):
        def one(step, carry):
            by_step(part, step, leave)
            return carry

        lax.fori_loop(low, high, one, 0)

    def next_steps(part, low, high, part_before, low_before):
        def one(step, carry):
            by_step(part_before, step - low + low_before, leave)
            by_step(part, step, start)
            return carry

        lax.fori_loop(low, high, one, 0)

    def forward(part):
        for way in range(2):
            for k in range(2):
                hop1(part, way, k).wait_recv()
                hop2(part, way, k).start()

    start_all(ring(0, 1))
    start_all(ring(1, 1))
    start_all(twin(0, core))
    first_kind = kinds.index(parts[0][3])
    fill_place(places[first_kind], kinds[first_kind])
    for step in range(1, no):
        limit_copy(lax.rem(o_at + step, no)).start()
    for q in range(quarters):
        fetch(q).wait()
    far = min(3, nz)
    first_steps(0, 0, nz)
    for n, kind in enumerate(kinds):
        if n != first_kind:
            fill_place(places[n], kind)
    ring_arrived(1)
    forward(0)
    if count > 1:
        first_steps(1, 0, far)
    if half > 1:
        ring_arrived(2)
    if count > 1:
        first_steps(1, far, nz)
    if half > 2:
        ring_arrived(3)
    if count > 1:
        forward(1)
    if count > 2:
        first_steps(2, 0, far)
    for step in range(4, half + 1):
        ring_arrived(step)
    if count > 2:
        turn_steps(2, far, nz)
    for part in range(3, count):
        turn_steps(part, 0, nz)

    def wide(tile):
        return jnp.tile(tile.astype(jnp.float32), (1, keys // 128))

    def leaf(slot, start, size):
        source = xor(i_at, slot, ibits)
        value = jnp.dot(
            recv[slot, pl.ds(start, size), :],
            grads[source],
            preferred_element_type=jnp.float32,
        )
        return value, wide(limits[source])

    def out_copy(part, target):
        piece_at = pl.ds(parts[part][2], round_up(parts[part][3], 16))
        return pltpu.make_async_remote_copy(
            src_ref=out_box.at[target, piece_at],
            dst_ref=in_box.at[o_at, piece_at],
            send_sem=out_send.at[part, target],
            recv_sem=out_recv.at[part, o_at],
            device_id=(i_at, target),
            device_id_type=MESH,
        )

    def out_arrival(part, source):
        piece_at = pl.ds(parts[part][2], round_up(parts[part][3], 16))
        return pltpu.make_async_remote_copy(
            src_ref=in_box.at[source, piece_at],
            dst_ref=in_box.at[source, piece_at],
            send_sem=out_send.at[part, source],
            recv_sem=out_recv.at[part, source],
            device_id=(i_at, source),
            device_id_type=MESH,
        )

    quarter = ni // 4

    def arrived(part, n):
        @pl.when(n == 0)
        def _():
            local_copy(part).wait()

        @pl.when(n != 0)
        def _():
            block_arrival(part, n).wait_recv()

        for m in (1, 2, 3):
            slot = n + m * quarter
            if m * quarter != 2 * half:
                block_arrival(part, slot).wait_recv()
                continue

            @pl.when(n < 2)
            def _():
                for way in range(2):
                    hop2_arrival(part, way, n).wait_recv()

            @pl.when(n >= 2)
            def _():
                block_arrival(part, slot).wait_recv()

    def work(part):
        start, size, at, piece = parts[part]
        high = round_up(piece, 16)

        def group(index, carry):
            n = quarter - 1 - index
            arrived(part, n)
            kept, _ = leaf(n, start, size)
            given, limit = leaf(n + 2 * quarter, start, size)
            first_sum = kept + clipped(given, limit[0:1])
            kept, limit_1 = leaf(n + quarter, start, size)
            given, limit = leaf(n + 3 * quarter, start, size)
            second_sum = kept + clipped(given, limit[0:1])
            sums[n, pl.ds(0, size), :] = first_sum + clipped(second_sum, limit_1[1:2])
            return carry

        lax.fori_loop(0, quarter, group, 0)
        level = 2
        width_now = quarter
        while width_now > 1:
            width_now //= 2
            for n in range(width_now):
                source = xor(i_at, n + width_now, ibits)
                limit = wide(limits[source])
                value = sums[n, pl.ds(0, size), :] + clipped(
                    sums[n + width_now, pl.ds(0, size), :], limit[level : level + 1]
                )
                if width_now == 1:
                    total[pl.ds(0, size), :] = value
                else:
                    sums[n, pl.ds(0, size), :] = value
            level += 1
        for owner in range(no):
            out_box[owner, pl.ds(at, high), :] = total[pl.ds(owner * piece, high), :].astype(
                jnp.bfloat16
            )
        for step in range(1, no):
            out_copy(part, lax.rem(o_at + step, no)).start()

    def finish(part):
        _, _, at, piece = parts[part]
        high = round_up(piece, 16)
        for step in range(1, no):
            out_arrival(part, lax.rem(o_at + step, no)).wait_recv()
        leaves = [out_box[o_at, pl.ds(at, high), :].astype(jnp.float32)]
        caps = [None]
        for slot in range(1, no):
            source = xor(o_at, slot, obits)
            leaves.append(in_box[source, pl.ds(at, high), :].astype(jnp.float32))
            caps.append(wide(limits_in[source]))
        many = no
        for hop in range(obits):
            many //= 2
            level = ibits + hop
            leaves = [
                leaves[n] + clipped(leaves[n + many], caps[n + many][level : level + 1])
                for n in range(many)
            ]
        out_ref[pl.ds(at, piece), :] = leaves[0][0:piece]

    def pieces_sent(part):
        for step in range(1, no):
            out_copy(part, lax.rem(o_at + step, no)).wait_send()

    def relays_sent(part):
        for way in range(2):
            for k in range(2):
                hop2(part, way, k).wait_send()

    for part in range(count):
        if part + 2 < count:
            forward(part + 2)
            next_steps(part + 2, far, nz, part, 0)
        if part + 3 < count:
            next_steps(part + 3, 0, far, part, nz - far)
        if part == 0:
            for offset in range(nz):
                wait_arrived(twin(offset, 1 - core))
            for step in range(1, no):
                limit_arrival(lax.rem(o_at + step, no)).wait_recv()
        if part + 1 == count:
            for way in range(2):
                for step in range(1, half + 1):
                    wait_sent(ring(way, step))
            for offset in range(nz):
                wait_sent(twin(offset, core))
            for step in range(1, no):
                limit_copy(lax.rem(o_at + step, no)).wait_send()
            if part > 1:
                wait_steps(part - 2, nz - far, nz)
            if part > 0:
                wait_steps(part - 1, 0, nz)
            for early in range(part):
                relays_sent(early)
                pieces_sent(early)
            if part > 0:
                finish(part - 1)
        work(part)
        if 0 < part < count - 1:
            finish(part - 1)
    wait_steps(count - 1, 0, nz)
    relays_sent(count - 1)
    finish(count - 1)
    pieces_sent(count - 1)


def cut_parts(rows, no):
    parts, at = [], 0
    for piece in (16, 32, 16, 16):
        piece = min(piece, rows - at)
        if piece > 0:
            parts.append((no * at, no * piece, at, piece))
        at += piece
    return tuple(parts)


def body(acts, key_grad, shifts):
    ni = lax.axis_size("inner")
    no = lax.axis_size("outer")
    tokens, width = acts.shape
    keys = key_grad.shape[1]
    block = width // ni
    rows = block // no
    nz = ni // 2
    half = nz // 2
    parts = cut_parts(rows, no)
    count = len(parts)
    widest = max(size for _, size, _, _ in parts)
    kinds = sorted(set((piece, size) for _, size, _, piece in parts))
    span = max(
        round_up(block * (n + 1), 128) - block * n // 128 * 128 for n in range(ni)
    )
    padded = round_up(rows, 16)
    dma = pltpu.SemaphoreType.DMA
    return pl.pallas_call(
        functools.partial(kernel, ni, no, parts, span),
        out_shape=pltpu.VMEM((rows, keys), jnp.float32),
        in_specs=[
            pl.BlockSpec(memory_space=pl.ANY),
            pl.BlockSpec(memory_space=pl.ANY),
            pl.BlockSpec(memory_space=pl.ANY),
        ],
        out_specs=pl.BlockSpec(memory_space=pltpu.VMEM),
        scratch_shapes=[
            pltpu.VMEM((tokens, width), jnp.bfloat16),
            pltpu.VMEM((width, tokens), jnp.bfloat16),
            pltpu.VMEM((ni, block, tokens), jnp.bfloat16),
            pltpu.VMEM((2, block, tokens), jnp.bfloat16),
            pltpu.VMEM((ni, tokens, keys), jnp.bfloat16),
            pltpu.VMEM((ni, BOUND_ROWS, 128), jnp.bfloat16),
            pltpu.VMEM((ni // 4, widest, keys), jnp.float32),
            pltpu.VMEM((round_up(widest + 16, 16), keys), jnp.float32),
            [pltpu.VMEM((size, span), jnp.int32) for _, size in kinds],
            pltpu.VMEM((no, padded, keys), jnp.bfloat16),
            pltpu.VMEM((no, padded, keys), jnp.bfloat16),
            pltpu.VMEM((BOUND_ROWS, 128), jnp.bfloat16),
            pltpu.VMEM((no, BOUND_ROWS, 128), jnp.bfloat16),
            pltpu.SMEM(shifts.shape, jnp.int32),
            dma,
            dma((4,)),
            dma,
            dma((2, half, 2)),
            dma((2, half, 2)),
            dma((2, half)),
            dma((2, half)),
            dma((nz,)),
            dma((nz,)),
            dma((nz,)),
            dma((nz,)),
            dma((count, ni)),
            dma((count, ni)),
            dma((count, 2, 2)),
            dma((count, 2, 2)),
            dma((count, 2, 2)),
            dma((count, 2, 2)),
            dma((count,)),
            dma((count, no)),
            dma((count, no)),
            dma((no,)),
            dma((no,)),
        ],
        compiler_params=pltpu.CompilerParams(
            collective_id=0, has_side_effects=True, vmem_limit_bytes=56 * 1024 * 1024
        ),
        cost_estimate=pl.CostEstimate(
            flops=2 * tokens * width * keys, bytes_accessed=2 * tokens * width, transcendentals=0
        ),
    )(acts, key_grad, shifts)


def solution(mesh):
    return jax.shard_map(
        body,
        mesh=mesh,
        in_specs=(
            P(("inner", "outer"), None),
            P(("inner", "outer"), None),
            P(("inner", "outer"), None),
        ),
        out_specs=P(("inner", "outer"), None),
        check_vma=False,
    )
```
